512 devices in a mesh: region: 64 (over x, z, core), lane: 8 (over y).
Axes of the slice: x: 4, y: 8, z: 8, core: 2. Of those that a mesh axis runs over, the one named last changes fastest.
Arguments:
- init_disp: float32 [3, 524288], P(None, 'region'), may hold values from -0.9 to 1.2
- init_vel: float32 [3, 524288], P(None, 'region'), may hold values from -3 to 3
- mass: float32 [524288], P('region'), may hold values from 0.5 to 2
- contact: float32 [524288], P('region'), may hold values from 0.1 to 16, as said below
- modulus: float32 [32768, 16], P(('region', 'lane')), may hold values from 0.5 to 3
- stiffness: float32 [24, 24], replicated, may hold values from -0.5 to 1.5, as said below
- levels: int32 [32768], P(('region', 'lane')), may hold values from 1 to 8, as said below
- windows: int32 [32768], P(('region', 'lane')), may hold values from 0 to 64
- conn: int32 [32768, 128], P(('region', 'lane')), may hold values from 0 to 255
Outputs:
- displacement: float32 [3, 524288], P(None, 'region')
- velocity: float32 [3, 524288], P(None, 'region')
- reaction: float32 [8], replicated
The draws below stay inside these ranges and needn't reach their ends.
Inputs may be any that keep to these rules, and one draw needn't show every extreme that they name: `levels`: each entry is 1, 2, 4 or 8. The number of 1s among the 64 blocks of one device differs between devices and equals 64 on some device. `contact`: positive weights. `stiffness`: Symmetric.
All inputs are finite; a program needn't handle non-finite values.
Results may differ from the reference program's by a relative error of at most 0.0003.
Values sent between devices are 32-bit elements; how exact they have to be, the bound alone decides.
A program may use at most 64 MiB of HBM per device.

```python
import math
import jax
import jax.numpy as jnp
from jax import lax

NB = 128
EB = 16
SLOTS = 128
BLK_DEV = 64
SUBSTEPS = 8
NBR = 64
NODE_REG = 8192
NODES = 524288
BLOCKS = 32768
N_REGION = 64


def draw_init_disp(key, part):
    key = jax.random.fold_in(key, 5)
    noise_key, shift_key = jax.random.split(key)
    region_index = jnp.arange(NODES, dtype=jnp.int32) // NODE_REG
    noise = jnp.clip(jax.random.normal(noise_key, (3, NODES), jnp.float32), -3.0, 3.0) * 0.3
    shift = jax.random.uniform(shift_key, (NODES // NODE_REG,), jnp.float32, 0.05, 0.25)
    offset = shift[region_index]
    return jnp.stack([noise[0] + offset, noise[1], noise[2]])


def draw_contact(key, part):
    key = jax.random.fold_in(key, 11)
    base_key, region_key = jax.random.split(key)
    position = jnp.arange(NODES, dtype=jnp.float32) / NODES
    region_index = jnp.arange(NODES, dtype=jnp.int32) // NODE_REG
    factor = jnp.exp(jax.random.uniform(region_key, (NODES // NODE_REG,), jnp.float32, jnp.log(0.5), jnp.log(2.0)))
    region_factor = factor[region_index]
    base = jax.random.uniform(base_key, (NODES,), jnp.float32, 0.5, 1.5)
    return base * (1.0 + 2.0 * position) * region_factor


def draw_stiffness(key, part):
    key = jax.random.fold_in(key, 23)
    noise = jnp.clip(jax.random.normal(key, (24, 24), jnp.float32), -3.0, 3.0) * 0.12
    return jnp.eye(24, dtype=jnp.float32) + 0.5 * (noise + noise.T)


def draw_levels(key, part):
    key = jax.random.fold_in(key, 37)
    first, second, third, fourth = jax.random.split(key, 4)
    devices_all = BLOCKS // BLK_DEV
    fine_count = jax.random.randint(first, (devices_all,), 0, BLK_DEV + 1)
    chosen = jax.random.randint(second, (), 0, devices_all)
    fine_count = jnp.where(jnp.arange(devices_all) == chosen, BLK_DEV, fine_count)
    ranking = jax.vmap(lambda sub_key: jax.random.permutation(sub_key, BLK_DEV))(jax.random.split(third, devices_all))
    table = jnp.array([2, 4, 8, 8], jnp.int32)
    coarse = table[jax.random.randint(fourth, (devices_all, BLK_DEV), 0, 4)]
    level = jnp.where(ranking < fine_count[:, None], 1, coarse)
    return level.reshape(-1).astype(jnp.int32)


def place_ends(values, own_key, least, top_value):
    longest = values.shape.index(max(values.shape))
    spots = []
    for shift in (0, 1):
        where = [jax.random.randint(jax.random.fold_in(own_key, axis), (), 0, length) for axis, length in enumerate(values.shape)]
        where[longest] = (where[longest] + shift) % values.shape[longest]
        spots.append(tuple(where))
    return values.at[spots[0]].set(least).at[spots[1]].set(top_value)


def block_scale(own_key, extent, cuts, low, high):
    def one(axis_at, shards_of):
        heights = jax.random.uniform(jax.random.fold_in(jax.random.fold_in(own_key, 6), axis_at), (shards_of,), jnp.float32, low / len(cuts), high / len(cuts))
        return jnp.repeat(jnp.exp(heights), extent[axis_at] // shards_of).reshape((-1,) + (1,) * (len(extent) - axis_at - 1))

    loudness = one(*cuts[0])
    for cut in cuts[1:]:
        loudness = loudness * one(*cut)
    return loudness


def bell_draw(key, shape, width, bound, cuts=(), held_as=jnp.bfloat16):
    entries = width * jax.random.normal(key, shape, jnp.float32)
    if cuts:
        entries = entries * block_scale(key, shape, cuts, -0.22, 0.18)
    return jnp.clip(entries, -bound, bound).astype(held_as)


def setup_inputs(seed: int = 0) -> dict:
    seeds = jax.random.split(jax.random.key(seed), 10)
    return {
        "init_disp": draw_init_disp(jax.random.fold_in(seeds[9], 71), 0),
        "init_vel": bell_draw(seeds[1], (3, NODES), 0.5, 3.0, ((1, 64),), jnp.float32),
        "mass": jnp.clip(jnp.exp(math.log(2.0) - 1.3862944 * jax.random.uniform(seeds[2], (NODES,), jnp.float32) ** block_scale(seeds[2], (NODES,), ((0, 64),), -0.2, 0.2)), 0.5, 2.0),
        "contact": draw_contact(jax.random.fold_in(seeds[9], 71), 0),
        "modulus": jnp.clip(jnp.exp(math.log(3.0) - 1.7917595 * jax.random.uniform(seeds[4], (BLOCKS, EB), jnp.float32) ** block_scale(seeds[4], (BLOCKS, EB), ((0, 512),), -0.2, 0.2)), 0.5, 3.0),
        "stiffness": draw_stiffness(jax.random.fold_in(seeds[9], 71), 0),
        "levels": draw_levels(jax.random.fold_in(seeds[9], 71), 0),
        "windows": place_ends(jax.random.randint(seeds[7], (BLOCKS,), 0, NBR + 1), jax.random.fold_in(seeds[7], 1), 0, NBR).astype(jnp.int32),
        "conn": place_ends(jax.random.randint(seeds[8], (BLOCKS, SLOTS), 0, 2 * NB), jax.random.fold_in(seeds[8], 1), 0, (2 * NB) - 1).astype(jnp.int32),
    }


time_step = 0.05
contact_stiffness = 1.0
hardening = 2.0
impactor_ratio = 0.05
start_gap = 1.0
start_speed = 1.0


def element_forces(slot_disp, block_modulus, stiffness):
    count = slot_disp.shape[0]
    elements = block_modulus.shape[1]
    vectors = slot_disp.reshape(count, 3, elements, 8).transpose(0, 2, 1, 3).reshape(count, elements, 24)
    strain = jnp.einsum("bek,jk->bej", vectors, stiffness, precision=lax.Precision.HIGHEST)
    result = block_modulus[:, :, None] * (strain + hardening * strain * strain * strain)
    return result.reshape(count, elements, 3, 8).transpose(0, 2, 1, 3).reshape(count, 3, elements * 8)


def reference(init_disp, init_vel, mass, contact, modulus, stiffness, levels, windows, conn):
    node_total = init_disp.shape[1]
    block_total = levels.shape[0]
    per_region = block_total // N_REGION
    node_region = node_total // N_REGION
    region_of = (jnp.arange(block_total, dtype=jnp.int32) // per_region).astype(jnp.int32)
    index = (region_of[:, None] * node_region + (windows[:, None] - 1) * NB + conn) % node_total
    index = index.astype(jnp.int32)
    flat_index = index.reshape(-1)
    held = jnp.zeros((block_total, 3, conn.shape[1]), jnp.float32)
    disp, vel = init_disp, init_vel
    gap_now = jnp.float32(start_gap)
    speed = jnp.float32(start_speed)
    impactor_mass = impactor_ratio * node_total
    history = []
    for substep in range(SUBSTEPS):
        slot_disp = disp[:, index].transpose(1, 0, 2)
        fresh = element_forces(slot_disp, modulus, stiffness)
        active = (substep % levels) == 0
        held = jnp.where(active[:, None, None], fresh, held)
        force = jnp.zeros((3, node_total), jnp.float32).at[:, flat_index].add(
            held.transpose(1, 0, 2).reshape(3, -1))
        gap = gap_now - disp[0]
        total = jnp.sum(contact * gap)
        history.append(total / node_total)
        push = jnp.zeros((3, node_total), jnp.float32).at[0].set(contact_stiffness * contact * gap)
        accel = (push - force) / mass[None, :]
        vel = vel + time_step * accel
        disp = disp + time_step * vel
        speed = speed - time_step * contact_stiffness * total / impactor_mass
        gap_now = gap_now + time_step * speed
    return disp, vel, jnp.stack(history)
```

```python
import functools

import jax
import jax.numpy as jnp
from jax import lax
from jax.experimental import pallas as pl
from jax.experimental.pallas import tpu as pltpu
from jax.sharding import PartitionSpec as P

NB = 128
SUBSTEPS = 8
LANES = 8
OWN = 8
EXT = 3 * OWN
ROWS = 256
EDGE = 24
AUX = 24

time_step = 0.05
contact_stiffness = 1.0
hardening = 2.0
impactor_ratio = 0.05
start_gap = 1.0
start_speed = 1.0
group_size = 8

f32, bf16, i32 = jnp.float32, jnp.bfloat16, jnp.int32


def iota(shape, dim):
    return lax.broadcasted_iota(i32, shape, dim)


def dot(a, b):
    return jnp.dot(a, b, preferred_element_type=f32)


def dot_t(a, b):
    return lax.dot_general(a, b, (((1,), (1,)), ((), ())), preferred_element_type=f32)


def split2(value):
    high = value.astype(bf16)
    return high, (value - high.astype(f32)).astype(bf16)


def split3(value):
    high = value.astype(bf16)
    rest = value - high.astype(f32)
    middle = rest.astype(bf16)
    return high, middle, (rest - middle.astype(f32)).astype(bf16)


def take(value, index):
    return jnp.take_along_axis(value, index, axis=1, mode="promise_in_bounds")


def onehot(mask):
    return jnp.where(mask, 1.0, 0.0).astype(bf16)


def cycle_kernel(
    regions,
    disp_in, vel_in, mass_in, contact_in, modulus_in, stiff_in, level_in, window_in, conn_in,
    vel_out, disp_out, react_out,
    conn_all, aux_all, aux_own, edge_out, edge_in, rim_out, rim_in,
    first_pay, first_a, first_b, pay, buf_a, pay_b, buf_b,
    disp, vel, mass, contact, table, slot_cols, kron, tri,
    wa, wb, back, conn_idx, half, perm, end1, end2, modulus, level, held, state,
    send_sem, recv_sem, pay_send, first_recv, a_recv, b_recv,
):
    r = lax.axis_index("region")
    lane = lax.axis_index("lane")
    core = lax.rem(r, 2)
    chip = r // 2
    chips = regions // 2
    up = lax.rem(r + 1, regions)
    down = lax.rem(r + regions - 1, regions)
    size_a = 2 * LANES
    spot_a = lane * 2 + core
    dt = time_step
    node_total = regions * LANES * OWN * NB
    impactor_mass = impactor_ratio * node_total

    def peer_a(k):
        return (chip * 2 + lax.rem(k, 2), k // 2)

    def peer_b(k):
        return (k * 2 + core, lane)

    def signal(device):
        pl.semaphore_signal(
            pltpu.get_barrier_semaphore(), inc=1, device_id=device,
            device_id_type=pl.DeviceIdType.MESH,
        )

    def shifted(spot, step, size):
        return lax.rem(spot + step, size)

    @pl.loop(1, size_a)
    def _(k):
        signal(peer_a(shifted(spot_a, k, size_a)))

    @pl.loop(1, chips)
    def _(k):
        signal(peer_b(shifted(chip, k, chips)))

    @pl.when(lane == 0)
    def _():
        @pl.loop(0, LANES)
        def _(j):
            signal((down, j))

    @pl.when(lane == LANES - 1)
    def _():
        @pl.loop(0, LANES)
        def _(j):
            signal((up, j))

    def copy(src, dst, send, recv, device):
        return pltpu.make_async_remote_copy(
            src_ref=src, dst_ref=dst, send_sem=send, recv_sem=recv,
            device_id=device, device_id_type=pl.DeviceIdType.MESH,
        )

    def wait_bytes(ref, sem):
        pltpu.make_async_copy(ref, ref, sem).wait()

    def load_nodes(place, source_lane):
        start = pl.multiple_of(source_lane * (OWN * NB), OWN * NB)
        for j in range(OWN):
            part = pl.ds(start + j * NB, NB)
            for c in range(3):
                disp[c, place + j : place + j + 1, :] = disp_in[c : c + 1, part]
                vel[c, place + j : place + j + 1, :] = vel_in[c : c + 1, part]
        rows = pl.ds(pl.multiple_of(source_lane * OWN, OWN), OWN)
        mass[place : place + OWN, :] = mass_in[rows, :]
        contact[place : place + OWN, :] = contact_in[rows, :]

    load_nodes(0, jnp.maximum(lane - 1, 0))
    load_nodes(OWN, lane)
    load_nodes(2 * OWN, jnp.minimum(lane + 1, LANES - 1))

    rim_lane = jnp.where(lane == 0, LANES - 1, 0)
    start = pl.multiple_of(rim_lane * (OWN * NB), OWN * NB)
    for j in range(OWN):
        part = pl.ds(start + j * NB, NB)
        for c in range(3):
            rim_out[8 * c + j : 8 * c + j + 1, :] = disp_in[c : c + 1, part]
            rim_out[24 + 8 * c + j : 25 + 8 * c + j, :] = vel_in[c : c + 1, part]
    rows = pl.ds(pl.multiple_of(rim_lane * OWN, OWN), OWN)
    rim_out[48:56, :] = mass_in[rows, :]
    rim_out[56:64, :] = contact_in[rows, :]

    own = pl.ds(OWN, OWN)
    own_contact = contact[own, :]
    own_mass = mass[own, :]
    push_rate = (dt * dt * contact_stiffness) * own_contact / own_mass
    sums = [
        jnp.sum(own_contact * (start_gap - disp[0, own, :]), axis=0, keepdims=True),
        jnp.sum(own_contact, axis=0, keepdims=True),
        jnp.sum(own_contact * push_rate, axis=0, keepdims=True),
    ]
    first_pay[...] = jnp.concatenate(sums + [jnp.zeros((5, NB), f32)], axis=0)

    shift = 64 * lax.rem(lane, 2)
    place = onehot(iota((64, NB), 1) == iota((64, NB), 0) + shift)
    level_row = level_in[...].astype(f32)
    window_row = window_in[...].astype(f32)
    mod_parts = split3(modulus_in[...])
    mod_rows = sum(
        lax.dot_general(part, place, (((0,), (0,)), ((), ())), preferred_element_type=f32)
        for part in mod_parts
    )
    pair = jnp.concatenate([level_row, window_row, jnp.zeros((6, 64), f32)], axis=0).astype(bf16)
    pair_rows = dot(pair, place)
    aux_own[...] = jnp.concatenate([mod_rows, pair_rows], axis=0)

    before = onehot(iota((64, 64), 0) < iota((64, 64), 1))
    conn_b = conn_in[...].astype(f32).astype(bf16)
    low = (window_row <= 7.0).astype(f32)
    high = (window_row >= 57.0).astype(f32)
    ends = jnp.concatenate([high, low, jnp.zeros((6, 64), f32)], axis=0)
    end_rank = dot(ends.astype(bf16), before)
    end_full = jnp.sum(ends, axis=1, keepdims=True)
    overflow = jnp.max(jnp.where(end_full > EDGE, 1.0, 0.0), axis=0, keepdims=True)
    rank_key = jnp.where(ends > 0.0, end_rank, -1.0)
    mod_wide = [
        dot(part, onehot(iota((16, NB), 0) == iota((16, NB), 1))).astype(bf16) for part in mod_parts
    ]
    for side, offset in ((0, -57.0), (1, 15.0)):
        pick = onehot(iota((EDGE, 64), 0).astype(f32) == rank_key[side : side + 1, :])
        edge_out[side, :, :NB] = dot(pick, conn_b)
        moduli = sum(dot(pick, part) for part in mod_wide)
        extra = jnp.concatenate(
            [level_row, window_row + offset, jnp.zeros((6, 64), f32)], axis=0
        ).astype(bf16)
        extra_cols = dot_t(pick, extra)
        spread = onehot(iota((8, NB), 1) == iota((8, NB), 0) + 16)
        edge_out[side, :, NB:] = moduli + dot(extra_cols.astype(bf16), spread)

    pl.semaphore_wait(pltpu.get_barrier_semaphore(), size_a - 1 + chips - 1 + 2)

    edge_up = copy(edge_out.at[0], edge_in.at[lane], send_sem.at[0], recv_sem.at[0], (up, 0))
    edge_down = copy(
        edge_out.at[1], edge_in.at[lane], send_sem.at[1], recv_sem.at[0], (down, LANES - 1)
    )
    edge_up.start()
    edge_down.start()
    rim_up = copy(rim_out, rim_in, send_sem.at[2], recv_sem.at[1], (up, 0))
    rim_down = copy(rim_out, rim_in, send_sem.at[2], recv_sem.at[1], (down, LANES - 1))

    @pl.when(lane == 0)
    def _():
        rim_up.start()

    @pl.when(lane == LANES - 1)
    def _():
        rim_down.start()

    @pl.loop(1, size_a)
    def _(k):
        copy(
            first_pay, first_a.at[spot_a], pay_send.at[0], first_recv.at[0],
            peer_a(shifted(spot_a, k, size_a)),
        ).start()

    @pl.loop(1, LANES)
    def _(k):
        there = (r, shifted(lane, k, LANES))
        copy(conn_in, conn_all.at[lane], send_sem.at[3], recv_sem.at[2], there).start()
        copy(aux_own, aux_all.at[lane], send_sem.at[4], recv_sem.at[3], there).start()

    conn_all[lane] = conn_in[...]
    aux_all[lane] = aux_own[...]
    first_a[spot_a] = first_pay[...]

    stiff = split2(stiff_in[...])
    at = iota((3 * NB, 24), 0)
    names = onehot((at // NB) * 8 + lax.rem(at, 8) == iota((3 * NB, 24), 1))
    row_of = lax.rem(iota((3 * NB, 3 * NB), 0), NB) // 8
    col_of = lax.rem(iota((3 * NB, 3 * NB), 1), NB) // 8
    same = row_of == col_of
    for part, places in ((stiff[0], (0, 1)), (stiff[1], (2,))):
        grown = dot_t(dot_t(names, part).astype(bf16), names)
        grown = jnp.where(same, grown, 0.0).astype(bf16)
        for at_place in places:
            kron[at_place * 3 * NB : (at_place + 1) * 3 * NB, :] = grown
    running = onehot(iota((NB, NB), 0) <= iota((NB, NB), 1))
    tri[0:NB, :] = running
    tri[NB:, :] = running

    @pl.when((lane != 0) & (lane != LANES - 1))
    def _():
        edge_in[...] = jnp.zeros_like(edge_in)

    wait_bytes(first_a.at[pl.ds(0, size_a - 1)], first_recv.at[0])
    total = first_a[0]
    for k in range(1, size_a):
        total = total + first_a[k]
    first_b[chip] = total
    first_pay2 = first_b.at[chip]

    @pl.loop(1, chips)
    def _(k):
        copy(
            first_pay2, first_b.at[chip], pay_send.at[1], first_recv.at[1],
            peer_b(shifted(chip, k, chips)),
        ).start()

    @pl.when((lane == 0) | (lane == LANES - 1))
    def _():
        wait_bytes(edge_in, recv_sem.at[0])
        wait_bytes(rim_in, recv_sem.at[1])

    def unpack_rim(place):
        for c in range(3):
            disp[c, place : place + OWN, :] = rim_in[8 * c : 8 * c + 8, :]
            vel[c, place : place + OWN, :] = rim_in[24 + 8 * c : 32 + 8 * c, :]
        mass[place : place + OWN, :] = rim_in[48:56, :]
        contact[place : place + OWN, :] = rim_in[56:64, :]

    @pl.when(lane == 0)
    def _():
        unpack_rim(0)

    @pl.when(lane == LANES - 1)
    def _():
        unpack_rim(2 * OWN)

    wait_bytes(conn_all.at[pl.ds(0, LANES - 1)], recv_sem.at[2])
    wait_bytes(aux_all.at[pl.ds(0, LANES - 1)], recv_sem.at[3])

    window_shift = (OWN - 1 - OWN * lane).astype(f32)
    last_anchor = 2 * OWN + OWN - 2.0
    columns = []
    anchors = []
    for k in range(LANES // 2):
        aux_pair = aux_all[2 * k] + aux_all[2 * k + 1]
        anchor = aux_pair[17:18, :] + window_shift
        padded = jnp.concatenate(
            [aux_pair[:17, :], anchor, jnp.zeros((NB - 18, NB), f32)], axis=0
        )
        columns.append(padded.T)
        anchors.append(anchor)
    edge_rows = edge_in[...].reshape(LANES * EDGE, 2 * NB)
    edge_aux = edge_rows[:, NB:]
    looked = onehot(iota((8, NB), 1) == iota((8, NB), 0) + 16)
    edge_look = dot_t(looked, edge_aux.astype(bf16))
    wanted = [jnp.where((a >= 0.0) & (a <= last_anchor), 1.0, 0.0) for a in anchors]
    edge_wanted = jnp.where(edge_look[0:1, :] > 0.0, 1.0, 0.0)
    flags = jnp.concatenate(wanted + [jnp.zeros((4, NB), f32)], axis=0)
    strict = onehot(iota((NB, NB), 0) < iota((NB, NB), 1))
    ranks = dot(flags.astype(bf16), strict)
    edge_count = LANES * EDGE
    strict_edge = onehot(iota((edge_count, edge_count), 0) < iota((edge_count, edge_count), 1))
    edge_flags = jnp.concatenate([edge_wanted, jnp.zeros((7, edge_count), f32)], axis=0)
    edge_ranks = dot(edge_flags.astype(bf16), strict_edge)
    counts = jnp.sum(flags, axis=1, keepdims=True)
    picks = []
    taken = jnp.zeros((1, 1), f32)
    row_number = iota((ROWS, NB), 0).astype(f32)
    for k in range(LANES // 2):
        key = jnp.where(wanted[k] > 0.0, ranks[k : k + 1, :] + taken, -1.0)
        picks.append(onehot(row_number == key))
        taken = taken + counts[k : k + 1, :]
    key = jnp.where(edge_wanted > 0.0, edge_ranks[0:1, :] + taken, -1.0)
    picks.append(onehot(iota((ROWS, edge_count), 0).astype(f32) == key))
    taken = taken + jnp.sum(edge_wanted, axis=1, keepdims=True)
    overflow = jnp.maximum(overflow, jnp.where(taken > float(ROWS), 1.0, 0.0))
    pick = jnp.concatenate(picks, axis=1)
    conn_rows = jnp.concatenate(
        [conn_all[...].astype(f32).reshape(LANES * 64, NB), edge_rows[:, :NB]], axis=0
    ).astype(bf16)
    aux_rows = jnp.concatenate(columns + [edge_aux], axis=0)
    aux_parts = split3(aux_rows)
    conn = dot(pick, conn_rows)
    aux = dot(pick, aux_parts[0]) + dot(pick, aux_parts[1]) + dot(pick, aux_parts[2])

    lane_no = iota((ROWS, NB), 1)
    modulus[...] = take(aux, lane_no // 8)
    level[...] = take(aux, jnp.full((ROWS, NB), 16, i32)).astype(i32) - 1
    anchor = take(aux, jnp.full((ROWS, NB), 17, i32)).astype(i32)
    wa[...] = onehot((lane_no & 31) == anchor)
    wb[...] = onehot((lane_no & 31) == anchor + 1)
    anchor_row = aux.T[17:18, :].astype(i32)
    ext_row = iota((32, ROWS), 0)
    back_a = onehot(ext_row == anchor_row)
    back_b = onehot(ext_row == anchor_row + 1)
    back[...] = jnp.concatenate([back_a, back_b, back_a, back_b], axis=1)
    conn_i = conn.astype(i32)
    conn_idx[...] = conn_i & (NB - 1)
    half[...] = conn_i >> 7

    keys = conn * float(NB) + lane_no.astype(f32)
    span = 2
    while span <= NB:
        step = span // 2
        while step >= 1:
            other = take(keys, lane_no ^ step)
            keep_low = ((lane_no & step) == 0) == ((lane_no & span) == 0)
            keys = jnp.where(keep_low, jnp.minimum(keys, other), jnp.maximum(keys, other))
            step //= 2
        span *= 2
    keys_i = keys.astype(i32)
    perm[...] = keys_i & (NB - 1)
    nodes = keys_i >> 7
    for ref, base in ((end1, 0), (end2, NB)):
        target = lane_no + base
        found = jnp.zeros((ROWS, NB), i32)
        for step in (64, 32, 16, 8, 4, 2, 1, 0):
            probe = take(nodes, found + (step - 1 if step else 0))
            found = jnp.where(probe <= target, found + max(step, 1), found)
        ref[...] = found - 1

    held[...] = jnp.zeros_like(held)
    table[...] = jnp.zeros_like(table)

    wait_bytes(first_b.at[pl.ds(0, chips - 1)], first_recv.at[1])
    total = first_b[0]
    for k in range(1, chips):
        total = total + first_b[k]
    first = jnp.sum(total, axis=1, keepdims=True)
    reaction0, contact_sum, push_sum = first[0:1, :], first[1:2, :], first[2:3, :]
    zero_row = jnp.zeros((1, NB), f32)
    gap1 = jnp.full((1, NB), start_gap, f32)
    w1 = start_speed - dt * contact_stiffness * (reaction0 + zero_row) / impactor_mass
    state[0:1, :] = gap1
    state[1:2, :] = gap1 + dt * w1
    state[2:3, :] = w1
    state[3:4, :] = contact_sum + zero_row
    state[4:5, :] = push_sum + zero_row
    react_out[0:1, :] = (reaction0 + zero_row) / node_total
    poison = jnp.where(overflow > 0.0, jnp.inf, 0.0) + zero_row
    state[5:6, :] = poison

    first_lane = iota((ROWS, NB), 1) == 0

    def forces(s):
        parts = [split3(disp[c]) for c in range(3)]
        for k in range(3):
            table[32 * k : 32 * k + EXT, :] = jnp.concatenate([parts[c][k] for c in range(3)], axis=1)
        source = table[...]
        near = dot(wa[...], source)
        far = dot(wb[...], source)
        index = conn_idx[...]
        second = half[...] > 0
        slots = []
        for c in range(3):
            cols = slice(c * NB, (c + 1) * NB)
            slots.append(jnp.where(second, take(far[:, cols], index), take(near[:, cols], index)))
        spread = jnp.concatenate(slots, axis=1)
        top, rest = split2(spread)
        strain = dot(jnp.concatenate([top, rest, top], axis=1), kron[...])
        active = (level[...] & s) == 0
        order = perm[...]
        mod = modulus[...]
        e1 = end1[...]
        e2 = end2[...]
        for c in range(3):
            g = strain[:, c * NB : (c + 1) * NB]
            fresh = mod * (g + hardening * g * g * g)
            now = jnp.where(active, fresh, held[c])
            held[c] = now
            sorted_force = take(now, order)
            sums = dot(jnp.concatenate(split2(sorted_force), axis=1), tri[...])
            upto1 = jnp.where(e1 >= 0, take(sums, e1 & (NB - 1)), 0.0)
            upto2 = jnp.where(e2 >= 0, take(sums, e2 & (NB - 1)), 0.0)
            prev1 = pltpu.roll(upto1, 1, 1)
            prev2 = pltpu.roll(upto2, 1, 1)
            f1 = split2(upto1 - jnp.where(first_lane, 0.0, prev1))
            f2 = split2(upto2 - jnp.where(first_lane, prev1, prev2))
            cols = slice(c * NB, (c + 1) * NB)
            slot_cols[0:ROWS, cols] = f1[0]
            slot_cols[ROWS : 2 * ROWS, cols] = f2[0]
            slot_cols[2 * ROWS : 3 * ROWS, cols] = f1[1]
            slot_cols[3 * ROWS :, cols] = f2[1]
        return dot(back[...], slot_cols[...])

    def relay(s):
        wait_bytes(buf_a.at[s, pl.ds(0, size_a - 1)], a_recv.at[s])
        value = buf_a[s, 0]
        for k in range(1, size_a):
            value = value + buf_a[s, k]
        buf_b[s, chip] = value

        @pl.loop(1, chips)
        def _(k):
            copy(
                buf_b.at[s, chip], buf_b.at[s, chip], pay_send.at[3], b_recv.at[s],
                peer_b(shifted(chip, k, chips)),
            ).start()

    def collect(s):
        wait_bytes(buf_b.at[s, pl.ds(0, chips - 1)], b_recv.at[s])
        value = buf_b[s, 0]
        for k in range(1, chips):
            value = value + buf_b[s, k]
        total = jnp.sum(value, axis=1, keepdims=True) + zero_row
        before_z = state[0:1, :]
        now_z = state[1:2, :]
        reaction = total + (now_z - start_gap) * state[3:4, :] - before_z * state[4:5, :]
        react_out[pl.ds(s + 1, 1), :] = reaction / node_total
        speed = state[2:3, :] - dt * contact_stiffness * reaction / impactor_mass
        state[0:1, :] = now_z
        state[1:2, :] = now_z + dt * speed
        state[2:3, :] = speed

    def substep(s, z_row_of):
        force = forces(s)
        ext_no = iota((EXT, NB), 0)
        valid = (ext_no >= 1 + s) & (ext_no <= EXT - 2 - s)
        weight = contact[...]
        inverse = 1.0 / mass[...]
        based = []
        for c in range(3):
            pull = -force[:EXT, c * NB : (c + 1) * NB]
            if c == 0:
                pull = pull - contact_stiffness * weight * disp[0]
            based.append(vel[c] + dt * (pull * inverse))
        free = disp[0, own, :] + dt * based[0][OWN : 2 * OWN]
        part = jnp.sum(contact[own, :] * (start_gap - free), axis=0, keepdims=True)
        pay[s] = part + state[5:6, :]
        buf_a[s, spot_a] = pay[s]

        @pl.when(s < SUBSTEPS - 1)
        def _():
            @pl.loop(1, size_a)
            def _(k):
                copy(
                    pay.at[s], buf_a.at[s, spot_a], pay_send.at[2], a_recv.at[s],
                    peer_a(shifted(spot_a, k, size_a)),
                ).start()

        @pl.when((s == 2) | (s == 5))
        def _():
            @pl.loop(0, 3)
            def _(k):
                relay(s - 2 + k)

        @pl.when(s >= 2)
        def _():
            collect(s - 2)

        z_now = z_row_of(s)
        based[0] = based[0] + (dt * contact_stiffness) * z_now * (weight * inverse)
        for c in range(3):
            vel[c] = jnp.where(valid, based[c], vel[c])
            disp[c] = jnp.where(valid, disp[c] + dt * based[c], disp[c])

    def z_row_of(s):
        return jnp.where(s == 0, start_gap, state[1:2, :])

    def gather_out(ref, slot):
        @pl.loop(1, LANES)
        def _(k):
            there = (r, shifted(lane, k, LANES))
            copy(
                ref.at[lane], ref.at[lane], send_sem.at[5 + slot], recv_sem.at[4 + slot], there
            ).start()

    @pl.loop(0, SUBSTEPS)
    def _(s):
        substep(s, z_row_of)

        @pl.when(s == SUBSTEPS - 2)
        def _():
            for c in range(3):
                disp_out[lane, c] = disp[c, own, :]
            gather_out(disp_out, 0)

    for c in range(3):
        vel_out[lane, c] = vel[c, own, :]
    gather_out(vel_out, 1)
    relay(SUBSTEPS - 2)
    collect(SUBSTEPS - 2)
    wait_bytes(disp_out.at[pl.ds(0, LANES - 1)], recv_sem.at[4])
    wait_bytes(vel_out.at[pl.ds(0, LANES - 1)], recv_sem.at[5])

    edge_up.wait_send()
    edge_down.wait_send()

    @pl.when((lane == 0) | (lane == LANES - 1))
    def _():
        rim_up.wait_send()

    wait_bytes(conn_all.at[pl.ds(0, LANES - 1)], send_sem.at[3])
    wait_bytes(aux_all.at[pl.ds(0, LANES - 1)], send_sem.at[4])
    wait_bytes(disp_out.at[pl.ds(0, LANES - 1)], send_sem.at[5])
    wait_bytes(vel_out.at[pl.ds(0, LANES - 1)], send_sem.at[6])
    wait_bytes(first_a.at[pl.ds(0, size_a - 1)], pay_send.at[0])
    wait_bytes(first_b.at[pl.ds(0, chips - 1)], pay_send.at[1])
    wait_bytes(buf_a.at[pl.ds(0, SUBSTEPS - 1), pl.ds(0, size_a - 1)], pay_send.at[2])
    wait_bytes(buf_b.at[pl.ds(0, SUBSTEPS - 1), pl.ds(0, chips - 1)], pay_send.at[3])


def run_cycle(regions, init_disp, init_vel, mass, contact, modulus, stiffness, levels, windows, conn):
    chips = regions // 2
    vmem = pl.BlockSpec(memory_space=pltpu.VMEM)
    V = pltpu.VMEM
    vel, disp, react = pl.pallas_call(
        functools.partial(cycle_kernel, regions),
        out_shape=(
            jax.ShapeDtypeStruct((LANES, 3, OWN, NB), f32),
            jax.ShapeDtypeStruct((LANES, 3, OWN, NB), f32),
            jax.ShapeDtypeStruct((SUBSTEPS, NB), f32),
        ),
        in_specs=[vmem] * 9,
        out_specs=[vmem] * 3,
        scratch_shapes=[
            V((LANES, 64, NB), i32), V((LANES, AUX, NB), f32), V((AUX, NB), f32),
            V((2, EDGE, 2 * NB), f32), V((LANES, EDGE, 2 * NB), f32),
            V((64, NB), f32), V((64, NB), f32),
            V((8, NB), f32), V((2 * LANES, 8, NB), f32), V((chips, 8, NB), f32),
            V((SUBSTEPS, 1, NB), f32), V((SUBSTEPS, 2 * LANES, 1, NB), f32),
            V((SUBSTEPS, 1, NB), f32), V((SUBSTEPS, chips, 1, NB), f32),
            V((3, EXT, NB), f32), V((3, EXT, NB), f32), V((EXT, NB), f32), V((EXT, NB), f32),
            V((NB, 3 * NB), bf16), V((4 * ROWS, 3 * NB), bf16),
            V((9 * NB, 3 * NB), bf16), V((2 * NB, NB), bf16),
            V((ROWS, NB), bf16), V((ROWS, NB), bf16), V((32, 4 * ROWS), bf16),
            V((ROWS, NB), i32), V((ROWS, NB), i32), V((ROWS, NB), i32),
            V((ROWS, NB), i32), V((ROWS, NB), i32),
            V((ROWS, NB), f32), V((ROWS, NB), i32), V((3, ROWS, NB), f32), V((8, NB), f32),
            pltpu.SemaphoreType.DMA((7,)), pltpu.SemaphoreType.DMA((6,)),
            pltpu.SemaphoreType.DMA((4,)), pltpu.SemaphoreType.DMA((2,)),
            pltpu.SemaphoreType.DMA((SUBSTEPS,)), pltpu.SemaphoreType.DMA((SUBSTEPS,)),
        ],
        compiler_params=pltpu.CompilerParams(
            collective_id=0, has_side_effects=True, vmem_limit_bytes=48 * 1024 * 1024
        ),
        name="crush_cycle",
    )(
        init_disp, init_vel, mass.reshape(-1, NB), contact.reshape(-1, NB), modulus, stiffness,
        levels.reshape(1, -1), windows.reshape(1, -1), conn,
    )
    velocity = vel.transpose(1, 0, 2, 3).reshape(3, -1)
    displacement = disp.transpose(1, 0, 2, 3).reshape(3, -1) + time_step * velocity
    return displacement, velocity, react[:, 0]


def with_halo(array, sides, width):
    for axis, dim in sides:
        count, length = (lax.axis_size(axis), array.shape[dim])
        up = [(i, (i + 1) % count) for i in range(count)]
        down = [(j, i) for i, j in up]
        last = lax.slice_in_dim(array, length - width, length, axis=dim)
        initial = lax.slice_in_dim(array, 0, width, axis=dim)
        before = lax.ppermute(last, axis, up)
        after = lax.ppermute(initial, axis, down)
        array = jnp.concatenate([before, array, after], axis=dim)
    return array


def element_forces(slot_disp, block_modulus, stiffness):
    count = slot_disp.shape[0]
    elements = block_modulus.shape[1]
    vectors = (
        slot_disp.reshape(count, 3, elements, 8).transpose(0, 2, 1, 3).reshape(count, elements, 24)
    )
    strain = jnp.einsum("bek,jk->bej", vectors, stiffness, precision=lax.Precision.HIGHEST)
    result = block_modulus[:, :, None] * (strain + hardening * strain * strain * strain)
    return (
        result.reshape(count, elements, 3, 8).transpose(0, 2, 1, 3).reshape(count, 3, elements * 8)
    )


def plain_cycle(init_disp, init_vel, mass, contact, modulus, stiffness, levels, windows, conn):
    region_count = lax.axis_size("region")
    node_region = init_disp.shape[1]
    slot_count = conn.shape[1]
    block_rows = NB
    node_total = node_region * region_count
    impactor_mass = impactor_ratio * node_total
    extended_blocks = node_region // block_rows + 2
    block_order = jnp.argsort(levels, stable=True)
    conn = conn[block_order]
    windows = windows[block_order]
    levels = levels[block_order]
    modulus = modulus[block_order]
    level_slot = (
        (levels >= 2).astype(jnp.int32)
        + (levels >= 4).astype(jnp.int32)
        + (levels >= 8).astype(jnp.int32)
    )
    level_force = jnp.zeros((4, 3, extended_blocks, block_rows), jnp.float32)
    disp_full = init_disp
    disp_state = init_disp
    vel_state = init_vel
    gap_now = jnp.float32(start_gap)
    speed = jnp.float32(start_speed)
    history = []
    slot_iota = lax.broadcasted_iota(jnp.int32, (group_size, 2 * block_rows, slot_count), 1)
    for substep in range(SUBSTEPS):
        top_level = SUBSTEPS if substep == 0 else min(substep & -substep, SUBSTEPS)
        top_index = top_level.bit_length() - 1
        active_count = jnp.sum((levels <= top_level).astype(jnp.int32))
        level_force = level_force.at[: top_index + 1].set(0.0)
        disp_ext = with_halo(disp_full, (("region", 1),), block_rows)

        def one_group(group_index, totals):
            offset = group_index * group_size
            conn_group = lax.dynamic_slice_in_dim(conn, offset, group_size, 0)
            window_group = lax.dynamic_slice_in_dim(windows, offset, group_size, 0)
            level_group = lax.dynamic_slice_in_dim(level_slot, offset, group_size, 0)
            modulus_group = lax.dynamic_slice_in_dim(modulus, offset, group_size, 0)
            valid = offset + jnp.arange(group_size, dtype=jnp.int32) < active_count
            window_disp = jax.vmap(
                lambda first_block: lax.dynamic_slice_in_dim(
                    disp_ext, first_block * block_rows, 2 * block_rows, 1
                )
            )(window_group)
            onehot = (slot_iota == conn_group[:, None, :]).astype(jnp.float32)
            slot_disp = jnp.einsum(
                "gcw,gws->gcs", window_disp, onehot, precision=lax.Precision.HIGHEST
            )
            slot_force = element_forces(slot_disp, modulus_group, stiffness)
            slot_force = jnp.where(valid[:, None, None], slot_force, 0.0)
            window_force = jnp.einsum(
                "gcs,gws->gcw", slot_force, onehot, precision=lax.Precision.HIGHEST
            )
            window_force = window_force.reshape(group_size, 3, 2, block_rows)
            totals = totals.at[level_group, :, window_group].add(window_force[:, :, 0])
            totals = totals.at[level_group, :, window_group + 1].add(window_force[:, :, 1])
            return totals

        group_total = (active_count + group_size - 1) // group_size
        level_force = lax.fori_loop(0, group_total, one_group, level_force)
        force_ext = jnp.sum(level_force, axis=0).reshape(3, extended_blocks * block_rows)
        outer_rims = jnp.concatenate(
            (force_ext[:, :block_rows], force_ext[:, -block_rows:]), axis=1
        )
        rim_terms = with_halo(outer_rims, (("region", 1),), block_rows)
        partial_force = force_ext[:, block_rows:-block_rows]
        partial_force = partial_force.at[:, :block_rows].add(rim_terms[:, :block_rows])
        partial_force = partial_force.at[:, -block_rows:].add(rim_terms[:, -block_rows:])
        force = lax.psum(partial_force, "lane")
        disp_state = disp_full
        gap = gap_now - disp_state[0]
        total = lax.psum(jnp.sum(contact * gap), "region")
        history.append(total / node_total)
        push = jnp.zeros_like(force).at[0].set(contact_stiffness * contact * gap)
        accel = (push - force) / mass[None, :]
        vel_state = vel_state + time_step * accel
        disp_state = disp_state + time_step * vel_state
        speed = speed - time_step * contact_stiffness * total / impactor_mass
        gap_now = gap_now + time_step * speed
        disp_full = disp_state
    return (disp_full, vel_state, jnp.stack(history))


def on_device(*arguments):
    regions = lax.axis_size("region")
    fast = run_cycle(regions, *arguments)
    fits = jnp.all(jnp.isfinite(fast[2]))
    return lax.cond(fits, lambda: fast, lambda: plain_cycle(*arguments))


def solution(mesh):
    in_specs = (
        P(None, "region"),
        P(None, "region"),
        P("region"),
        P("region"),
        P(("region", "lane"), None),
        P(),
        P(("region", "lane")),
        P(("region", "lane")),
        P(("region", "lane"), None),
    )
    out_specs = (P(None, "region"), P(None, "region"), P())
    return jax.shard_map(
        on_device, mesh=mesh, in_specs=in_specs, out_specs=out_specs, check_vma=False
    )
```

```python
import functools

import jax
import jax.numpy as jnp
from jax import lax
from jax.experimental import pallas as pl
from jax.experimental.pallas import tpu as pltpu
from jax.sharding import PartitionSpec as P

NB = 128
SUBSTEPS = 8
LANES = 8
OWN = 8
EXT = 3 * OWN
ROWS = 256
EDGE = 24
AUX = 24

time_step = 0.05
contact_stiffness = 1.0
hardening = 2.0
impactor_ratio = 0.05
start_gap = 1.0
start_speed = 1.0
group_size = 8

f32, bf16, i32 = jnp.float32, jnp.bfloat16, jnp.int32


def iota(shape, dim):
    return lax.broadcasted_iota(i32, shape, dim)


def dot(a, b):
    return jnp.dot(a, b, preferred_element_type=f32)


def dot_t(a, b):
    return lax.dot_general(a, b, (((1,), (1,)), ((), ())), preferred_element_type=f32)


def split2(value):
    high = value.astype(bf16)
    return high, (value - high.astype(f32)).astype(bf16)


def split3(value):
    high = value.astype(bf16)
    rest = value - high.astype(f32)
    middle = rest.astype(bf16)
    return high, middle, (rest - middle.astype(f32)).astype(bf16)


def take(value, index):
    return jnp.take_along_axis(value, index, axis=1, mode="promise_in_bounds")


def onehot(mask):
    return jnp.where(mask, 1.0, 0.0).astype(bf16)


def cycle_kernel(
    regions,
    disp_far, vel_far, mass_far, contact_far, modulus_far, stiff_far, level_far, window_far, conn_far,
    vel_out, disp_out, react_out, flag_out,
    disp_in, vel_in, mass_in, contact_in, modulus_in, stiff_in, level_in, window_in, conn_in,
    conn_all, aux_all, aux_own, edge_out, edge_in, rim_out, rim_in,
    first_pay, first_a, first_b, pay, buf_a, pay_b, buf_b,
    disp, vel, mass, contact, table, slot_cols, kron, tri,
    wa, wb, back, conn_idx, half, perm, end1, end2, modulus, level, held, state,
    send_sem, recv_sem, pay_send, first_recv, a_recv, b_recv, load_sem,
):
    r = lax.axis_index("region")
    lane = lax.axis_index("lane")
    core = lax.rem(r, 2)
    chip = r // 2
    chips = regions // 2
    up = lax.rem(r + 1, regions)
    down = lax.rem(r + regions - 1, regions)
    size_a = 2 * LANES
    spot_a = lane * 2 + core
    dt = time_step
    node_total = regions * LANES * OWN * NB
    impactor_mass = impactor_ratio * node_total

    def peer_a(k):
        return (chip * 2 + lax.rem(k, 2), k // 2)

    def peer_b(k):
        return (k * 2 + core, lane)

    def signal(device):
        pl.semaphore_signal(
            pltpu.get_barrier_semaphore(), inc=1, device_id=device,
            device_id_type=pl.DeviceIdType.MESH,
        )

    def shifted(spot, step, size):
        return lax.rem(spot + step, size)

    @pl.loop(1, size_a)
    def _(k):
        signal(peer_a(shifted(spot_a, k, size_a)))

    @pl.loop(1, chips)
    def _(k):
        signal(peer_b(shifted(chip, k, chips)))

    @pl.when(lane == 0)
    def _():
        @pl.loop(0, LANES)
        def _(j):
            signal((down, j))

    @pl.when(lane == LANES - 1)
    def _():
        @pl.loop(0, LANES)
        def _(j):
            signal((up, j))

    def copy(src, dst, send, recv, device):
        return pltpu.make_async_remote_copy(
            src_ref=src, dst_ref=dst, send_sem=send, recv_sem=recv,
            device_id=device, device_id_type=pl.DeviceIdType.MESH,
        )

    def wait_bytes(ref, sem):
        pltpu.make_async_copy(ref, ref, sem).wait()

    loads = []
    for k, (far, here) in enumerate((
        (level_far, level_in), (window_far, window_in), (modulus_far, modulus_in),
        (conn_far, conn_in), (contact_far, contact_in), (mass_far, mass_in),
        (disp_far, disp_in), (vel_far, vel_in), (stiff_far, stiff_in),
    )):
        loads.append(pltpu.make_async_copy(far, here, load_sem.at[k]))
        loads[-1].start()
    for load in loads:
        load.wait()

    def load_nodes(place, source_lane):
        start = pl.multiple_of(source_lane * (OWN * NB), OWN * NB)
        for j in range(OWN):
            part = pl.ds(start + j * NB, NB)
            for c in range(3):
                disp[c, place + j : place + j + 1, :] = disp_in[c : c + 1, part]
                vel[c, place + j : place + j + 1, :] = vel_in[c : c + 1, part]
        rows = pl.ds(pl.multiple_of(source_lane * OWN, OWN), OWN)
        mass[place : place + OWN, :] = mass_in[rows, :]
        contact[place : place + OWN, :] = contact_in[rows, :]

    load_nodes(0, jnp.maximum(lane - 1, 0))
    load_nodes(OWN, lane)
    load_nodes(2 * OWN, jnp.minimum(lane + 1, LANES - 1))

    rim_lane = jnp.where(lane == 0, LANES - 1, 0)
    start = pl.multiple_of(rim_lane * (OWN * NB), OWN * NB)
    for j in range(OWN):
        part = pl.ds(start + j * NB, NB)
        for c in range(3):
            rim_out[8 * c + j : 8 * c + j + 1, :] = disp_in[c : c + 1, part]
            rim_out[24 + 8 * c + j : 25 + 8 * c + j, :] = vel_in[c : c + 1, part]
    rows = pl.ds(pl.multiple_of(rim_lane * OWN, OWN), OWN)
    rim_out[48:56, :] = mass_in[rows, :]
    rim_out[56:64, :] = contact_in[rows, :]

    own = pl.ds(OWN, OWN)
    own_contact = contact[own, :]
    own_mass = mass[own, :]
    push_rate = (dt * dt * contact_stiffness) * own_contact / own_mass
    sums = [
        jnp.sum(own_contact * (start_gap - disp[0, own, :]), axis=0, keepdims=True),
        jnp.sum(own_contact, axis=0, keepdims=True),
        jnp.sum(own_contact * push_rate, axis=0, keepdims=True),
    ]
    first_pay[...] = jnp.concatenate(sums + [jnp.zeros((5, NB), f32)], axis=0)

    shift = 64 * lax.rem(lane, 2)
    place = onehot(iota((64, NB), 1) == iota((64, NB), 0) + shift)
    level_row = level_in[...].astype(f32)
    window_row = window_in[...].astype(f32)
    mod_parts = split3(modulus_in[...])
    mod_rows = sum(
        dot(part, place) for part in mod_parts
    )
    pair = jnp.concatenate([level_row, window_row, jnp.zeros((6, 64), f32)], axis=0).astype(bf16)
    pair_rows = dot(pair, place)
    aux_own[...] = jnp.concatenate([mod_rows, pair_rows], axis=0)

    before = onehot(iota((64, 64), 0) < iota((64, 64), 1))
    conn_b = conn_in[...].astype(f32).astype(bf16)
    low = (window_row <= 7.0).astype(f32)
    high = (window_row >= 57.0).astype(f32)
    ends = jnp.concatenate([high, low, jnp.zeros((6, 64), f32)], axis=0)
    end_rank = dot(ends.astype(bf16), before)
    end_full = jnp.sum(ends, axis=1, keepdims=True)
    overflow = jnp.max(jnp.where(end_full > EDGE, 1.0, 0.0), axis=0, keepdims=True)
    rank_key = jnp.where(ends > 0.0, end_rank, -1.0)
    for side, offset in ((0, -57.0), (1, 15.0)):
        pick = onehot(iota((EDGE, 64), 0).astype(f32) == rank_key[side : side + 1, :])
        edge_out[side, :, :NB] = dot(pick, conn_b)
        moduli = sum(
            dot(dot_t(pick, part).astype(bf16), onehot(iota((16, NB), 0) == iota((16, NB), 1)))
            for part in mod_parts
        )
        extra = jnp.concatenate(
            [level_row, window_row + offset, jnp.zeros((6, 64), f32)], axis=0
        ).astype(bf16)
        extra_cols = dot_t(pick, extra)
        spread = onehot(iota((8, NB), 1) == iota((8, NB), 0) + 16)
        edge_out[side, :, NB:] = moduli + dot(extra_cols.astype(bf16), spread)

    pl.semaphore_wait(pltpu.get_barrier_semaphore(), size_a - 1 + chips - 1 + 2)

    edge_up = copy(edge_out.at[0], edge_in.at[lane], send_sem.at[0], recv_sem.at[0], (up, 0))
    edge_down = copy(
        edge_out.at[1], edge_in.at[lane], send_sem.at[1], recv_sem.at[0], (down, LANES - 1)
    )
    edge_up.start()
    edge_down.start()
    rim_up = copy(rim_out, rim_in, send_sem.at[2], recv_sem.at[1], (up, 0))
    rim_down = copy(rim_out, rim_in, send_sem.at[2], recv_sem.at[1], (down, LANES - 1))

    @pl.when(lane == 0)
    def _():
        rim_up.start()

    @pl.when(lane == LANES - 1)
    def _():
        rim_down.start()

    @pl.loop(1, size_a)
    def _(k):
        copy(
            first_pay, first_a.at[spot_a], pay_send.at[0], first_recv.at[0],
            peer_a(shifted(spot_a, k, size_a)),
        ).start()

    @pl.loop(1, LANES)
    def _(k):
        there = (r, shifted(lane, k, LANES))
        copy(conn_in, conn_all.at[lane], send_sem.at[3], recv_sem.at[2], there).start()
        copy(aux_own, aux_all.at[lane], send_sem.at[4], recv_sem.at[3], there).start()

    conn_all[lane] = conn_in[...]
    aux_all[lane] = aux_own[...]
    first_a[spot_a] = first_pay[...]

    stiff = split2(stiff_in[...])
    at = iota((3 * NB, 24), 0)
    names = onehot((at // NB) * 8 + lax.rem(at, 8) == iota((3 * NB, 24), 1))
    row_of = lax.rem(iota((3 * NB, 3 * NB), 0), NB) // 8
    col_of = lax.rem(iota((3 * NB, 3 * NB), 1), NB) // 8
    same = row_of == col_of
    for part, places in ((stiff[0], (0, 1)), (stiff[1], (2,))):
        grown = dot_t(dot_t(names, part).astype(bf16), names)
        grown = jnp.where(same, grown, 0.0).astype(bf16)
        for at_place in places:
            kron[at_place * 3 * NB : (at_place + 1) * 3 * NB, :] = grown
    running = onehot(iota((NB, NB), 0) <= iota((NB, NB), 1))
    tri[0:NB, :] = running
    tri[NB:, :] = running

    @pl.when((lane != 0) & (lane != LANES - 1))
    def _():
        edge_in[...] = jnp.zeros_like(edge_in)

    wait_bytes(first_a.at[pl.ds(0, size_a - 1)], first_recv.at[0])
    total = first_a[0]
    for k in range(1, size_a):
        total = total + first_a[k]
    first_b[chip] = total
    first_pay2 = first_b.at[chip]

    @pl.loop(1, chips)
    def _(k):
        copy(
            first_pay2, first_b.at[chip], pay_send.at[1], first_recv.at[1],
            peer_b(shifted(chip, k, chips)),
        ).start()

    @pl.when((lane == 0) | (lane == LANES - 1))
    def _():
        wait_bytes(edge_in, recv_sem.at[0])
        wait_bytes(rim_in, recv_sem.at[1])

    def unpack_rim(place):
        for c in range(3):
            disp[c, place : place + OWN, :] = rim_in[8 * c : 8 * c + 8, :]
            vel[c, place : place + OWN, :] = rim_in[24 + 8 * c : 32 + 8 * c, :]
        mass[place : place + OWN, :] = rim_in[48:56, :]
        contact[place : place + OWN, :] = rim_in[56:64, :]

    @pl.when(lane == 0)
    def _():
        unpack_rim(0)

    @pl.when(lane == LANES - 1)
    def _():
        unpack_rim(2 * OWN)

    wait_bytes(conn_all.at[pl.ds(0, LANES - 1)], recv_sem.at[2])
    wait_bytes(aux_all.at[pl.ds(0, LANES - 1)], recv_sem.at[3])

    window_shift = (OWN - 1 - OWN * lane).astype(f32)
    last_anchor = 2 * OWN + OWN - 2.0
    columns = []
    anchors = []
    for k in range(LANES // 2):
        aux_pair = aux_all[2 * k] + aux_all[2 * k + 1]
        anchor = aux_pair[17:18, :] + window_shift
        padded = jnp.concatenate(
            [aux_pair[:17, :], anchor, jnp.zeros((NB - 18, NB), f32)], axis=0
        )
        columns.append(padded.T)
        anchors.append(anchor)
    edge_rows = edge_in[...].reshape(LANES * EDGE, 2 * NB)
    edge_aux = edge_rows[:, NB:]
    looked = onehot(iota((8, NB), 1) == iota((8, NB), 0) + 16)
    edge_look = dot_t(looked, edge_aux.astype(bf16))
    wanted = [jnp.where((a >= 0.0) & (a <= last_anchor), 1.0, 0.0) for a in anchors]
    edge_wanted = jnp.where(edge_look[0:1, :] > 0.0, 1.0, 0.0)
    flags = jnp.concatenate(wanted + [jnp.zeros((4, NB), f32)], axis=0)
    strict = onehot(iota((NB, NB), 0) < iota((NB, NB), 1))
    ranks = dot(flags.astype(bf16), strict)
    edge_count = LANES * EDGE
    strict_edge = onehot(iota((edge_count, edge_count), 0) < iota((edge_count, edge_count), 1))
    edge_flags = jnp.concatenate([edge_wanted, jnp.zeros((7, edge_count), f32)], axis=0)
    edge_ranks = dot(edge_flags.astype(bf16), strict_edge)
    counts = jnp.sum(flags, axis=1, keepdims=True)
    picks = []
    taken = jnp.zeros((1, 1), f32)
    row_number = iota((ROWS, NB), 0).astype(f32)
    for k in range(LANES // 2):
        key = jnp.where(wanted[k] > 0.0, ranks[k : k + 1, :] + taken, -1.0)
        picks.append(onehot(row_number == key))
        taken = taken + counts[k : k + 1, :]
    key = jnp.where(edge_wanted > 0.0, edge_ranks[0:1, :] + taken, -1.0)
    picks.append(onehot(iota((ROWS, edge_count), 0).astype(f32) == key))
    taken = taken + jnp.sum(edge_wanted, axis=1, keepdims=True)
    overflow = jnp.maximum(overflow, jnp.where(taken > float(ROWS), 1.0, 0.0))
    pick = jnp.concatenate(picks, axis=1)
    conn_rows = jnp.concatenate(
        [conn_all[...].astype(f32).reshape(LANES * 64, NB), edge_rows[:, :NB]], axis=0
    ).astype(bf16)
    aux_rows = jnp.concatenate(columns + [edge_aux], axis=0)
    aux_parts = split3(aux_rows)
    conn = dot(pick, conn_rows)
    aux = dot(pick, aux_parts[0]) + dot(pick, aux_parts[1]) + dot(pick, aux_parts[2])

    lane_no = iota((ROWS, NB), 1)
    modulus[...] = take(aux, lane_no // 8)
    level[...] = take(aux, jnp.full((ROWS, NB), 16, i32)).astype(i32) - 1
    anchor = take(aux, jnp.full((ROWS, NB), 17, i32)).astype(i32)
    wa[...] = onehot((lane_no & 31) == anchor)
    wb[...] = onehot((lane_no & 31) == anchor + 1)
    anchor_row = aux.T[17:18, :].astype(i32)
    ext_row = iota((32, ROWS), 0)
    back_a = onehot(ext_row == anchor_row)
    back_b = onehot(ext_row == anchor_row + 1)
    back[...] = jnp.concatenate([back_a, back_b, back_a, back_b], axis=1)
    conn_i = conn.astype(i32)
    conn_idx[...] = conn_i & (NB - 1)
    half[...] = conn_i >> 7

    keys = conn * float(NB) + lane_no.astype(f32)
    span = 2
    while span <= NB:
        step = span // 2
        while step >= 1:
            other = take(keys, lane_no ^ step)
            keep_low = ((lane_no & step) == 0) == ((lane_no & span) == 0)
            keys = jnp.where(keep_low, jnp.minimum(keys, other), jnp.maximum(keys, other))
            step //= 2
        span *= 2
    keys_i = keys.astype(i32)
    perm[...] = keys_i & (NB - 1)
    nodes = keys_i >> 7
    for ref, base in ((end1, 0), (end2, NB)):
        target = lane_no + base
        found = jnp.zeros((ROWS, NB), i32)
        for step in (64, 32, 16, 8, 4, 2, 1, 0):
            probe = take(nodes, found + (step - 1 if step else 0))
            found = jnp.where(probe <= target, found + max(step, 1), found)
        ref[...] = found - 1

    held[...] = jnp.zeros_like(held)
    table[...] = jnp.zeros_like(table)

    wait_bytes(first_b.at[pl.ds(0, chips - 1)], first_recv.at[1])
    total = first_b[0]
    for k in range(1, chips):
        total = total + first_b[k]
    first = jnp.sum(total, axis=1, keepdims=True)
    reaction0, contact_sum, push_sum = first[0:1, :], first[1:2, :], first[2:3, :]
    zero_row = jnp.zeros((1, NB), f32)
    gap1 = jnp.full((1, NB), start_gap, f32)
    w1 = start_speed - dt * contact_stiffness * (reaction0 + zero_row) / impactor_mass
    state[0:1, :] = gap1
    state[1:2, :] = gap1 + dt * w1
    state[2:3, :] = w1
    state[3:4, :] = contact_sum + zero_row
    state[4:5, :] = push_sum + zero_row
    react_out[0:1, :] = (reaction0 + zero_row) / node_total
    poison = jnp.where(overflow > 0.0, jnp.inf, 0.0) + zero_row
    state[5:6, :] = poison

    first_lane = iota((ROWS, NB), 1) == 0

    def forces(s):
        parts = [split3(disp[c]) for c in range(3)]
        for k in range(3):
            table[32 * k : 32 * k + EXT, :] = jnp.concatenate([parts[c][k] for c in range(3)], axis=1)
        source = table[...]
        near = dot(wa[...], source)
        far = dot(wb[...], source)
        index = conn_idx[...]
        second = half[...] > 0
        slots = []
        for c in range(3):
            cols = slice(c * NB, (c + 1) * NB)
            slots.append(jnp.where(second, take(far[:, cols], index), take(near[:, cols], index)))
        spread = jnp.concatenate(slots, axis=1)
        top, rest = split2(spread)
        strain = dot(jnp.concatenate([top, rest, top], axis=1), kron[...])
        active = (level[...] & s) == 0
        order = perm[...]
        mod = modulus[...]
        e1 = end1[...]
        e2 = end2[...]
        for c in range(3):
            g = strain[:, c * NB : (c + 1) * NB]
            fresh = mod * (g + hardening * g * g * g)
            now = jnp.where(active, fresh, held[c])
            held[c] = now
            sorted_force = take(now, order)
            sums = dot(jnp.concatenate(split2(sorted_force), axis=1), tri[...])
            upto1 = jnp.where(e1 >= 0, take(sums, e1 & (NB - 1)), 0.0)
            upto2 = jnp.where(e2 >= 0, take(sums, e2 & (NB - 1)), 0.0)
            prev1 = pltpu.roll(upto1, 1, 1)
            prev2 = pltpu.roll(upto2, 1, 1)
            f1 = split2(upto1 - jnp.where(first_lane, 0.0, prev1))
            f2 = split2(upto2 - jnp.where(first_lane, prev1, prev2))
            cols = slice(c * NB, (c + 1) * NB)
            slot_cols[0:ROWS, cols] = f1[0]
            slot_cols[ROWS : 2 * ROWS, cols] = f2[0]
            slot_cols[2 * ROWS : 3 * ROWS, cols] = f1[1]
            slot_cols[3 * ROWS :, cols] = f2[1]
        return dot(back[...], slot_cols[...])

    def relay(s):
        wait_bytes(buf_a.at[s, pl.ds(0, size_a - 1)], a_recv.at[s])
        value = buf_a[s, 0]
        for k in range(1, size_a):
            value = value + buf_a[s, k]
        buf_b[s, chip] = value

        @pl.loop(1, chips)
        def _(k):
            copy(
                buf_b.at[s, chip], buf_b.at[s, chip], pay_send.at[3], b_recv.at[s],
                peer_b(shifted(chip, k, chips)),
            ).start()

    def collect(s):
        wait_bytes(buf_b.at[s, pl.ds(0, chips - 1)], b_recv.at[s])
        value = buf_b[s, 0]
        for k in range(1, chips):
            value = value + buf_b[s, k]
        total = jnp.sum(value, axis=1, keepdims=True) + zero_row
        before_z = state[0:1, :]
        now_z = state[1:2, :]
        reaction = total + (now_z - start_gap) * state[3:4, :] - before_z * state[4:5, :]
        react_out[pl.ds(s + 1, 1), :] = reaction / node_total
        speed = state[2:3, :] - dt * contact_stiffness * reaction / impactor_mass
        state[0:1, :] = now_z
        state[1:2, :] = now_z + dt * speed
        state[2:3, :] = speed

    def substep(s, z_row_of):
        force = forces(s)
        ext_no = iota((EXT, NB), 0)
        valid = (ext_no >= 1 + s) & (ext_no <= EXT - 2 - s)
        weight = contact[...]
        inverse = 1.0 / mass[...]
        based = []
        for c in range(3):
            pull = -force[:EXT, c * NB : (c + 1) * NB]
            if c == 0:
                pull = pull - contact_stiffness * weight * disp[0]
            based.append(vel[c] + dt * (pull * inverse))
        free = disp[0, own, :] + dt * based[0][OWN : 2 * OWN]
        part = jnp.sum(contact[own, :] * (start_gap - free), axis=0, keepdims=True)
        pay[s] = part + state[5:6, :]
        buf_a[s, spot_a] = pay[s]

        @pl.when(s < SUBSTEPS - 1)
        def _():
            @pl.loop(1, size_a)
            def _(k):
                copy(
                    pay.at[s], buf_a.at[s, spot_a], pay_send.at[2], a_recv.at[s],
                    peer_a(shifted(spot_a, k, size_a)),
                ).start()

        @pl.when((s == 2) | (s == 5))
        def _():
            @pl.loop(0, 3)
            def _(k):
                relay(s - 2 + k)

        @pl.when(s >= 2)
        def _():
            collect(s - 2)

        z_now = z_row_of(s)
        based[0] = based[0] + (dt * contact_stiffness) * z_now * (weight * inverse)
        for c in range(3):
            vel[c] = jnp.where(valid, based[c], vel[c])
            disp[c] = jnp.where(valid, disp[c] + dt * based[c], disp[c])

    def z_row_of(s):
        return jnp.where(s == 0, start_gap, state[1:2, :])

    def gather_out(ref, slot):
        @pl.loop(1, LANES)
        def _(k):
            there = (r, shifted(lane, k, LANES))
            copy(
                ref.at[lane], ref.at[lane], send_sem.at[5 + slot], recv_sem.at[4 + slot], there
            ).start()

    @pl.loop(0, SUBSTEPS)
    def _(s):
        substep(s, z_row_of)

        @pl.when(s == SUBSTEPS - 2)
        def _():
            for c in range(3):
                disp_out[lane, c] = disp[c, own, :]
            gather_out(disp_out, 0)

    for c in range(3):
        vel_out[lane, c] = vel[c, own, :]
    gather_out(vel_out, 1)
    relay(SUBSTEPS - 2)
    collect(SUBSTEPS - 2)
    wait_bytes(disp_out.at[pl.ds(0, LANES - 1)], recv_sem.at[4])
    wait_bytes(vel_out.at[pl.ds(0, LANES - 1)], recv_sem.at[5])

    whole = jnp.where(jnp.abs(react_out[...]) < jnp.inf, 0, 1)
    flag_out[0] = jnp.max(whole)

    edge_up.wait_send()
    edge_down.wait_send()

    @pl.when((lane == 0) | (lane == LANES - 1))
    def _():
        rim_up.wait_send()

    wait_bytes(conn_all.at[pl.ds(0, LANES - 1)], send_sem.at[3])
    wait_bytes(aux_all.at[pl.ds(0, LANES - 1)], send_sem.at[4])
    wait_bytes(disp_out.at[pl.ds(0, LANES - 1)], send_sem.at[5])
    wait_bytes(vel_out.at[pl.ds(0, LANES - 1)], send_sem.at[6])
    wait_bytes(first_a.at[pl.ds(0, size_a - 1)], pay_send.at[0])
    wait_bytes(first_b.at[pl.ds(0, chips - 1)], pay_send.at[1])
    wait_bytes(buf_a.at[pl.ds(0, SUBSTEPS - 1), pl.ds(0, size_a - 1)], pay_send.at[2])
    wait_bytes(buf_b.at[pl.ds(0, SUBSTEPS - 1), pl.ds(0, chips - 1)], pay_send.at[3])


def run_cycle(regions, init_disp, init_vel, mass, contact, modulus, stiffness, levels, windows, conn):
    chips = regions // 2
    vmem = pl.BlockSpec(memory_space=pltpu.VMEM)
    V = pltpu.VMEM
    vel, disp, react, flag = pl.pallas_call(
        functools.partial(cycle_kernel, regions),
        out_shape=(
            jax.ShapeDtypeStruct((LANES, 3, OWN, NB), f32),
            jax.ShapeDtypeStruct((LANES, 3, OWN, NB), f32),
            jax.ShapeDtypeStruct((SUBSTEPS, NB), f32),
            jax.ShapeDtypeStruct((1,), i32),
        ),
        in_specs=[pl.BlockSpec(memory_space=pl.ANY)] * 9,
        out_specs=[vmem] * 3 + [pl.BlockSpec(memory_space=pltpu.SMEM)],
        scratch_shapes=[
            V(init_disp.shape, f32), V(init_vel.shape, f32), V((LANES * OWN, NB), f32),
            V((LANES * OWN, NB), f32), V((16, 64), f32), V((24, 24), f32),
            V((1, 64), i32), V((1, 64), i32), V((64, NB), i32),
            V((LANES, 64, NB), i32), V((LANES, AUX, NB), f32), V((AUX, NB), f32),
            V((2, EDGE, 2 * NB), f32), V((LANES, EDGE, 2 * NB), f32),
            V((64, NB), f32), V((64, NB), f32),
            V((8, NB), f32), V((2 * LANES, 8, NB), f32), V((chips, 8, NB), f32),
            V((SUBSTEPS, 1, NB), f32), V((SUBSTEPS, 2 * LANES, 1, NB), f32),
            V((SUBSTEPS, 1, NB), f32), V((SUBSTEPS, chips, 1, NB), f32),
            V((3, EXT, NB), f32), V((3, EXT, NB), f32), V((EXT, NB), f32), V((EXT, NB), f32),
            V((NB, 3 * NB), bf16), V((4 * ROWS, 3 * NB), bf16),
            V((9 * NB, 3 * NB), bf16), V((2 * NB, NB), bf16),
            V((ROWS, NB), bf16), V((ROWS, NB), bf16), V((32, 4 * ROWS), bf16),
            V((ROWS, NB), i32), V((ROWS, NB), i32), V((ROWS, NB), i32),
            V((ROWS, NB), i32), V((ROWS, NB), i32),
            V((ROWS, NB), f32), V((ROWS, NB), i32), V((3, ROWS, NB), f32), V((8, NB), f32),
            pltpu.SemaphoreType.DMA((7,)), pltpu.SemaphoreType.DMA((6,)),
            pltpu.SemaphoreType.DMA((4,)), pltpu.SemaphoreType.DMA((2,)),
            pltpu.SemaphoreType.DMA((SUBSTEPS,)), pltpu.SemaphoreType.DMA((SUBSTEPS,)),
            pltpu.SemaphoreType.DMA((9,)),
        ],
        compiler_params=pltpu.CompilerParams(
            collective_id=0, has_side_effects=True, vmem_limit_bytes=48 * 1024 * 1024
        ),
        name="crush_cycle",
    )(
        init_disp, init_vel, mass.reshape(-1, NB), contact.reshape(-1, NB), modulus.T, stiffness,
        levels.reshape(1, -1), windows.reshape(1, -1), conn,
    )
    velocity = vel.transpose(1, 0, 2, 3).reshape(3, -1)
    displacement = disp.transpose(1, 0, 2, 3).reshape(3, -1) + time_step * velocity
    return (displacement, velocity, react[:, 0]), flag[0]


def sum_over(value, axis):
    count = lax.axis_size(axis)
    step = 1
    while step < count:
        value = value + lax.ppermute(value, axis, [(i, i ^ step) for i in range(count)])
        step *= 2
    return value


def with_halo(array, sides, width):
    for axis, dim in sides:
        count, length = (lax.axis_size(axis), array.shape[dim])
        up = [(i, (i + 1) % count) for i in range(count)]
        down = [(j, i) for i, j in up]
        last = lax.slice_in_dim(array, length - width, length, axis=dim)
        initial = lax.slice_in_dim(array, 0, width, axis=dim)
        before = lax.ppermute(last, axis, up)
        after = lax.ppermute(initial, axis, down)
        array = jnp.concatenate([before, array, after], axis=dim)
    return array


def element_forces(slot_disp, block_modulus, stiffness):
    count = slot_disp.shape[0]
    elements = block_modulus.shape[1]
    vectors = (
        slot_disp.reshape(count, 3, elements, 8).transpose(0, 2, 1, 3).reshape(count, elements, 24)
    )
    strain = jnp.einsum("bek,jk->bej", vectors, stiffness, precision=lax.Precision.HIGHEST)
    result = block_modulus[:, :, None] * (strain + hardening * strain * strain * strain)
    return (
        result.reshape(count, elements, 3, 8).transpose(0, 2, 1, 3).reshape(count, 3, elements * 8)
    )


def plain_cycle(init_disp, init_vel, mass, contact, modulus, stiffness, levels, windows, conn):
    region_count = lax.axis_size("region")
    node_region = init_disp.shape[1]
    slot_count = conn.shape[1]
    block_rows = NB
    node_total = node_region * region_count
    impactor_mass = impactor_ratio * node_total
    extended_blocks = node_region // block_rows + 2
    block_order = jnp.argsort(levels, stable=True)
    conn = conn[block_order]
    windows = windows[block_order]
    levels = levels[block_order]
    modulus = modulus[block_order]
    level_slot = (
        (levels >= 2).astype(jnp.int32)
        + (levels >= 4).astype(jnp.int32)
        + (levels >= 8).astype(jnp.int32)
    )
    level_force = jnp.zeros((4, 3, extended_blocks, block_rows), jnp.float32)
    disp_full = init_disp
    disp_state = init_disp
    vel_state = init_vel
    gap_now = jnp.float32(start_gap)
    speed = jnp.float32(start_speed)
    history = []
    slot_iota = lax.broadcasted_iota(jnp.int32, (group_size, 2 * block_rows, slot_count), 1)
    for substep in range(SUBSTEPS):
        top_level = SUBSTEPS if substep == 0 else min(substep & -substep, SUBSTEPS)
        top_index = top_level.bit_length() - 1
        active_count = jnp.sum((levels <= top_level).astype(jnp.int32))
        level_force = level_force.at[: top_index + 1].set(0.0)
        disp_ext = with_halo(disp_full, (("region", 1),), block_rows)

        def one_group(group_index, totals):
            offset = group_index * group_size
            conn_group = lax.dynamic_slice_in_dim(conn, offset, group_size, 0)
            window_group = lax.dynamic_slice_in_dim(windows, offset, group_size, 0)
            level_group = lax.dynamic_slice_in_dim(level_slot, offset, group_size, 0)
            modulus_group = lax.dynamic_slice_in_dim(modulus, offset, group_size, 0)
            valid = offset + jnp.arange(group_size, dtype=jnp.int32) < active_count
            window_disp = jax.vmap(
                lambda first_block: lax.dynamic_slice_in_dim(
                    disp_ext, first_block * block_rows, 2 * block_rows, 1
                )
            )(window_group)
            onehot = (slot_iota == conn_group[:, None, :]).astype(jnp.float32)
            slot_disp = jnp.einsum(
                "gcw,gws->gcs", window_disp, onehot, precision=lax.Precision.HIGHEST
            )
            slot_force = element_forces(slot_disp, modulus_group, stiffness)
            slot_force = jnp.where(valid[:, None, None], slot_force, 0.0)
            window_force = jnp.einsum(
                "gcs,gws->gcw", slot_force, onehot, precision=lax.Precision.HIGHEST
            )
            window_force = window_force.reshape(group_size, 3, 2, block_rows)
            totals = totals.at[level_group, :, window_group].add(window_force[:, :, 0])
            totals = totals.at[level_group, :, window_group + 1].add(window_force[:, :, 1])
            return totals

        group_total = (active_count + group_size - 1) // group_size
        level_force = lax.fori_loop(0, group_total, one_group, level_force)
        force_ext = jnp.sum(level_force, axis=0).reshape(3, extended_blocks * block_rows)
        outer_rims = jnp.concatenate(
            (force_ext[:, :block_rows], force_ext[:, -block_rows:]), axis=1
        )
        rim_terms = with_halo(outer_rims, (("region", 1),), block_rows)
        partial_force = force_ext[:, block_rows:-block_rows]
        partial_force = partial_force.at[:, :block_rows].add(rim_terms[:, :block_rows])
        partial_force = partial_force.at[:, -block_rows:].add(rim_terms[:, -block_rows:])
        force = sum_over(partial_force, "lane")
        disp_state = disp_full
        gap = gap_now - disp_state[0]
        total = sum_over(jnp.sum(contact * gap), "region")
        history.append(total / node_total)
        push = jnp.zeros_like(force).at[0].set(contact_stiffness * contact * gap)
        accel = (push - force) / mass[None, :]
        vel_state = vel_state + time_step * accel
        disp_state = disp_state + time_step * vel_state
        speed = speed - time_step * contact_stiffness * total / impactor_mass
        gap_now = gap_now + time_step * speed
        disp_full = disp_state
    return (disp_full, vel_state, jnp.stack(history))


def on_device(*arguments):
    regions = lax.axis_size("region")
    fast, flag = run_cycle(regions, *arguments)
    return lax.cond(flag == 0, lambda: fast, lambda: plain_cycle(*arguments))


def solution(mesh):
    in_specs = (
        P(None, "region"),
        P(None, "region"),
        P("region"),
        P("region"),
        P(("region", "lane"), None),
        P(),
        P(("region", "lane")),
        P(("region", "lane")),
        P(("region", "lane"), None),
    )
    out_specs = (P(None, "region"), P(None, "region"), P())
    return jax.shard_map(
        on_device, mesh=mesh, in_specs=in_specs, out_specs=out_specs, check_vma=False
    )
```

```python
import functools

import jax
import jax.numpy as jnp
from jax import lax
from jax.experimental import pallas as pl
from jax.experimental.pallas import tpu as pltpu
from jax.sharding import PartitionSpec as P

NB = 128
SUBSTEPS = 8
LANES = 8
OWN = 8
DEPTH = 3
NODE_ROWS = 16
ANCHORS = OWN - 1 + 2 * DEPTH
ROWS = 160
PACK = 32
EDGE = 16

time_step = 0.05
contact_stiffness = 1.0
hardening = 2.0
impactor_ratio = 0.05
start_gap = 1.0
start_speed = 1.0
group_size = 8

f32, bf16, i32 = jnp.float32, jnp.bfloat16, jnp.int32


def iota(shape, dim):
    return lax.broadcasted_iota(i32, shape, dim)


def dot(a, b):
    return jnp.dot(a, b, preferred_element_type=f32)


def dot_t(a, b):
    return lax.dot_general(a, b, (((1,), (1,)), ((), ())), preferred_element_type=f32)


def split2(value):
    high = value.astype(bf16)
    return high, (value - high.astype(f32)).astype(bf16)


def split3(value):
    high = value.astype(bf16)
    rest = value - high.astype(f32)
    middle = rest.astype(bf16)
    return high, middle, (rest - middle.astype(f32)).astype(bf16)


def take(value, index):
    return jnp.take_along_axis(value, index, axis=1, mode="promise_in_bounds")


def row_of(ext):
    return jnp.where(ext < DEPTH, ext + OWN, jnp.where(ext < DEPTH + OWN, ext - DEPTH, ext))


def onehot(mask):
    return jnp.where(mask, 1.0, 0.0).astype(bf16)


def cycle_kernel(
    regions,
    disp_far, vel_far, mass_far, contact_far, modulus_far, stiff_far, level_far, window_far, conn_far,
    vel_out, disp_out, react_out, flag_out,
    disp_in, vel_in, mass_in, contact_in, modulus_in, stiff_in, level_in, window_in, conn_in,
    pack_out, pack_in, edge_out, edge_in, order_out, order_in, order_edge_out, order_edge_in,
    rim_out, rim_in, halo_out, halo_in,
    first_pay, first_a, first_b, pay, buf_a, buf_b, last_pay, last_a, last_b, react, disp_all,
    disp, vel, based, mass, contact, table, slot_cols, kron, tri,
    wab, back, conn_idx, half, perm, end1, end2, modulus, level, held, state,
    send_sem, recv_sem, pay_send, first_recv, a_recv, b_recv, load_sem, halo_send, halo_recv, last_recv,
):
    r = lax.axis_index("region")
    lane = lax.axis_index("lane")
    core = lax.rem(r, 2)
    chip = r // 2
    chips = regions // 2
    up = lax.rem(r + 1, regions)
    down = lax.rem(r + regions - 1, regions)
    size_a = 2 * LANES
    spot_a = lane * 2 + core
    dt = time_step
    node_total = regions * LANES * OWN * NB
    impactor_mass = impactor_ratio * node_total

    def peer_a(k):
        return (chip * 2 + lax.rem(k, 2), k // 2)

    def peer_b(k):
        return (k * 2 + core, lane)

    def signal(device):
        pl.semaphore_signal(
            pltpu.get_barrier_semaphore(), inc=1, device_id=device,
            device_id_type=pl.DeviceIdType.MESH,
        )

    def shifted(spot, step, size):
        return lax.rem(spot + step, size)

    @pl.loop(1, size_a)
    def _(k):
        signal(peer_a(shifted(spot_a, k, size_a)))

    @pl.loop(1, chips)
    def _(k):
        signal(peer_b(shifted(chip, k, chips)))

    @pl.when(lane == 0)
    def _():
        @pl.loop(0, LANES)
        def _(j):
            signal((down, j))

    @pl.when(lane == LANES - 1)
    def _():
        @pl.loop(0, LANES)
        def _(j):
            signal((up, j))

    def copy(src, dst, send, recv, device):
        return pltpu.make_async_remote_copy(
            src_ref=src, dst_ref=dst, send_sem=send, recv_sem=recv,
            device_id=device, device_id_type=pl.DeviceIdType.MESH,
        )

    def wait_bytes(ref, sem):
        pltpu.make_async_copy(ref, ref, sem).wait()

    loads = []
    for k, (far, here) in enumerate((
        (level_far, level_in), (window_far, window_in), (modulus_far, modulus_in),
        (conn_far, conn_in), (contact_far, contact_in), (mass_far, mass_in),
        (disp_far, disp_in), (vel_far, vel_in), (stiff_far, stiff_in),
    )):
        loads.append(pltpu.make_async_copy(far, here, load_sem.at[k]))
        loads[-1].start()
    for load in loads:
        load.wait()

    level_row = level_in[...].astype(f32)
    window_row = window_in[...].astype(f32)
    dest = iota((16, 64), 0)
    offsets = jnp.where(
        dest < LANES, (DEPTH - 1) - OWN * dest,
        jnp.where(dest == LANES, DEPTH - 1 - OWN * LANES, OWN + DEPTH - 1),
    ).astype(f32)
    anchor_all = window_row + offsets
    lowest = jnp.where(dest == LANES + 1, OWN + DEPTH - 1, 0).astype(f32)
    highest = jnp.where(dest == LANES, DEPTH - 1, ANCHORS - 1).astype(f32)
    wanted = jnp.where(
        (anchor_all >= lowest) & (anchor_all <= highest) & (dest < LANES + 2), 1.0, 0.0
    )
    before = onehot(iota((64, 64), 0) < iota((64, 64), 1))
    rank_key = jnp.where(wanted > 0.0, dot(wanted.astype(bf16), before), -1.0)
    count = jnp.sum(wanted, axis=1, keepdims=True)
    room = jnp.where(iota((16, 1), 0) < LANES, PACK, EDGE).astype(f32)
    overflow = jnp.max(jnp.where(count > room, 1.0, 0.0), axis=0, keepdims=True)
    picks = [
        onehot(iota((PACK, 64), 0).astype(f32) == rank_key[k : k + 1, :]) for k in range(LANES)
    ] + [
        onehot(iota((EDGE, 64), 0).astype(f32) == rank_key[k : k + 1, :])
        for k in (LANES, LANES + 1)
    ]
    pick = jnp.concatenate(picks, axis=0)
    conn_f = conn_in[...].astype(f32)
    block_data = jnp.concatenate(
        [modulus_in[...], level_row, window_row, jnp.zeros((NB - 18, 64), f32)], axis=0
    )
    chosen = sum(dot_t(pick, part) for part in split3(block_data))
    chosen_conn = dot(pick, conn_f.astype(bf16))
    for k in range(LANES):
        part = slice(k * PACK, (k + 1) * PACK)
        pack_out[k, :, :NB] = chosen_conn[part, :]
        pack_out[k, :, NB:] = chosen[part, :] + jnp.where(
            iota((PACK, NB), 1) == 17, float(DEPTH - 1 - OWN * k), 0.0
        )
    for k, offset in ((0, DEPTH - 1 - OWN * LANES), (1, OWN + DEPTH - 1)):
        part = slice(LANES * PACK + k * EDGE, LANES * PACK + (k + 1) * EDGE)
        edge_out[k, :, :NB] = chosen_conn[part, :]
        edge_out[k, :, NB:] = chosen[part, :] + jnp.where(
            iota((EDGE, NB), 1) == 17, float(offset), 0.0
        )

    def load_rim(rim_lane, first):
        for j in range(DEPTH):
            at = (rim_lane * OWN + first + j) * NB
            part = slice(at, at + NB)
            for c in range(3):
                rim_out[c, j : j + 1, :] = disp_in[c : c + 1, part]
                rim_out[3 + c, j : j + 1, :] = vel_in[c : c + 1, part]
        rows = slice(rim_lane * OWN + first, rim_lane * OWN + first + DEPTH)
        rim_out[6, :, :] = mass_in[rows, :]
        rim_out[7, :, :] = contact_in[rows, :]

    @pl.when(lane == 0)
    def _():
        load_rim(LANES - 1, OWN - DEPTH)

    @pl.when(lane == LANES - 1)
    def _():
        load_rim(0, 0)

    def load_nodes(place, source_lane, first, number):
        start = pl.multiple_of(source_lane * (OWN * NB), OWN * NB)
        for j in range(number):
            part = pl.ds(start + (first + j) * NB, NB)
            for c in range(3):
                disp[c, place + j : place + j + 1, :] = disp_in[c : c + 1, part]
                vel[c, place + j : place + j + 1, :] = vel_in[c : c + 1, part]
        rows = pl.ds(pl.multiple_of(source_lane * OWN, OWN), OWN)
        mass[place : place + number, :] = mass_in[rows, :][first : first + number, :]
        contact[place : place + number, :] = contact_in[rows, :][first : first + number, :]

    left_row, right_row = OWN, OWN + DEPTH
    disp[...] = jnp.zeros_like(disp)
    vel[...] = jnp.zeros_like(vel)
    mass[...] = jnp.ones_like(mass)
    contact[...] = jnp.zeros_like(contact)
    load_nodes(0, lane, 0, OWN)
    load_nodes(left_row, jnp.maximum(lane - 1, 0), OWN - DEPTH, DEPTH)
    load_nodes(right_row, jnp.minimum(lane + 1, LANES - 1), 0, DEPTH)

    own = pl.ds(0, OWN)
    own_contact = contact[own, :]
    own_mass = mass[own, :]
    push_rate = (dt * dt * contact_stiffness) * own_contact / own_mass
    sums = [
        jnp.sum(own_contact * (start_gap - disp[0, own, :]), axis=0, keepdims=True),
        jnp.sum(own_contact, axis=0, keepdims=True),
        jnp.sum(own_contact * push_rate, axis=0, keepdims=True),
    ]
    first_pay[...] = jnp.concatenate(sums, axis=0)
    first_a[spot_a] = first_pay[...]

    pl.semaphore_wait(pltpu.get_barrier_semaphore(), size_a - 1 + chips - 1 + 2)

    @pl.loop(1, size_a)
    def _(k):
        copy(
            first_pay, first_a.at[spot_a], pay_send.at[0], first_recv.at[0],
            peer_a(shifted(spot_a, k, size_a)),
        ).start()

    edge_up = copy(edge_out.at[0], edge_in.at[lane], send_sem.at[0], recv_sem.at[0], (up, 0))
    edge_down = copy(
        edge_out.at[1], edge_in.at[lane], send_sem.at[1], recv_sem.at[0], (down, LANES - 1)
    )
    edge_up.start()
    edge_down.start()

    @pl.loop(1, LANES)
    def _(k):
        there = shifted(lane, k, LANES)
        copy(
            pack_out.at[there], pack_in.at[lane], send_sem.at[3], recv_sem.at[2], (r, there)
        ).start()

    rim_up = copy(rim_out, rim_in, send_sem.at[2], recv_sem.at[1], (up, 0))
    rim_down = copy(rim_out, rim_in, send_sem.at[2], recv_sem.at[1], (down, LANES - 1))

    @pl.when(lane == 0)
    def _():
        rim_up.start()

    @pl.when(lane == LANES - 1)
    def _():
        rim_down.start()

    pack_in[lane] = pack_out[lane]

    lane64 = iota((64, NB), 1)
    keys = conn_f * float(NB) + lane64.astype(f32)
    span = 2
    while span <= NB:
        step = span // 2
        while step >= 1:
            other = take(keys, lane64 ^ step)
            keep_low = ((lane64 & step) == 0) == ((lane64 & span) == 0)
            keys = jnp.where(keep_low, jnp.minimum(keys, other), jnp.maximum(keys, other))
            step //= 2
        span *= 2
    order = (keys.astype(i32) & (NB - 1)).astype(f32)
    chosen_order = dot(pick, order.astype(bf16))
    for k in range(LANES):
        order_out[k] = chosen_order[k * PACK : (k + 1) * PACK, :]
    for k in range(2):
        start = LANES * PACK + k * EDGE
        order_edge_out[k] = chosen_order[start : start + EDGE, :]
    order_up = copy(
        order_edge_out.at[0], order_edge_in.at[lane], send_sem.at[7], recv_sem.at[6], (up, 0)
    )
    order_down = copy(
        order_edge_out.at[1], order_edge_in.at[lane], send_sem.at[8], recv_sem.at[6],
        (down, LANES - 1),
    )
    order_up.start()
    order_down.start()

    @pl.loop(1, LANES)
    def _(k):
        there = shifted(lane, k, LANES)
        copy(
            order_out.at[there], order_in.at[lane], send_sem.at[4], recv_sem.at[3], (r, there)
        ).start()

    order_in[lane] = order_out[lane]

    stiff = split2(stiff_in[...])
    at = iota((3 * NB, 24), 0)
    names = onehot((at // NB) * 8 + lax.rem(at, 8) == iota((3 * NB, 24), 1))
    row_element = lax.rem(iota((3 * NB, 3 * NB), 0), NB) // 8
    col_element = lax.rem(iota((3 * NB, 3 * NB), 1), NB) // 8
    same = row_element == col_element
    for part, places in ((stiff[0], (0, 1)), (stiff[1], (2,))):
        grown = dot_t(dot_t(names, part).astype(bf16), names)
        grown = jnp.where(same, grown, 0.0).astype(bf16)
        for at_place in places:
            kron[at_place * 3 * NB : (at_place + 1) * 3 * NB, :] = grown
    running = onehot(iota((NB, NB), 0) <= iota((NB, NB), 1))
    tri[0:NB, :] = running
    tri[NB:, :] = running

    @pl.when((lane != 0) & (lane != LANES - 1))
    def _():
        edge_in[...] = jnp.zeros_like(edge_in)
        order_edge_in[...] = jnp.zeros_like(order_edge_in)

    wait_bytes(first_a.at[pl.ds(0, size_a - 1)], first_recv.at[0])
    total = first_a[0]
    for k in range(1, size_a):
        total = total + first_a[k]
    first_b[chip] = total
    first_pay2 = first_b.at[chip]

    @pl.loop(1, chips)
    def _(k):
        copy(
            first_pay2, first_b.at[chip], pay_send.at[1], first_recv.at[1],
            peer_b(shifted(chip, k, chips)),
        ).start()

    @pl.when((lane == 0) | (lane == LANES - 1))
    def _():
        wait_bytes(edge_in, recv_sem.at[0])
        wait_bytes(rim_in, recv_sem.at[1])

    def unpack_rim(place):
        for c in range(3):
            disp[c, place : place + DEPTH, :] = rim_in[c]
            vel[c, place : place + DEPTH, :] = rim_in[3 + c]
        mass[place : place + DEPTH, :] = rim_in[6]
        contact[place : place + DEPTH, :] = rim_in[7]

    @pl.when(lane == 0)
    def _():
        unpack_rim(left_row)

    @pl.when(lane == LANES - 1)
    def _():
        unpack_rim(right_row)

    wait_bytes(pack_in.at[pl.ds(0, LANES - 1)], recv_sem.at[2])

    offered = LANES * (PACK + EDGE)
    rows_in = jnp.concatenate(
        [pack_in[...].reshape(LANES * PACK, 2 * NB), edge_in[...].reshape(LANES * EDGE, 2 * NB)],
        axis=0,
    )
    data_in = rows_in[:, NB:]
    data_parts = split3(data_in)
    looked = onehot(iota((8, NB), 1) == 16)
    present = jnp.where(dot_t(looked, data_parts[0]) > 0.0, 1.0, 0.0)
    strict = onehot(iota((offered, offered), 0) < iota((offered, offered), 1))
    key = jnp.where(present > 0.0, dot(present.astype(bf16), strict), -1.0)[0:1, :]
    taken = jnp.sum(present[0:1, :], axis=1, keepdims=True)
    overflow = jnp.maximum(overflow, jnp.where(taken > float(ROWS), 1.0, 0.0))
    keep = onehot(iota((ROWS, offered), 0).astype(f32) == key)
    conn = dot(keep, rows_in[:, :NB].astype(bf16))
    data = dot(keep, data_parts[0]) + dot(keep, data_parts[1]) + dot(keep, data_parts[2])

    lane_no = iota((ROWS, NB), 1)
    modulus[...] = take(data, lane_no // 8)
    level[...] = take(data, jnp.full((ROWS, NB), 16, i32)).astype(i32) - 1
    anchor = take(data, jnp.full((ROWS, NB), 17, i32)).astype(i32)
    wab[:ROWS, :] = onehot((lane_no & 31) == row_of(anchor))
    wab[ROWS:, :] = onehot((lane_no & 31) == row_of(anchor + 1))
    named = dot_t(onehot(iota((8, NB), 1) == 17), data.astype(bf16))
    anchor_row = named[0:1, :].astype(i32)
    node_row = iota((NODE_ROWS, ROWS), 0)
    back_a = onehot(node_row == row_of(anchor_row))
    back_b = onehot(node_row == row_of(anchor_row + 1))
    back[...] = jnp.concatenate([back_a, back_b, back_a, back_b], axis=1)
    conn_i = conn.astype(i32)
    conn_idx[...] = conn_i & (NB - 1)
    half[...] = conn_i >> 7

    @pl.when((lane == 0) | (lane == LANES - 1))
    def _():
        wait_bytes(order_edge_in, recv_sem.at[6])

    wait_bytes(order_in.at[pl.ds(0, LANES - 1)], recv_sem.at[3])
    order_rows = jnp.concatenate(
        [
            order_in[...].reshape(LANES * PACK, NB),
            order_edge_in[...].reshape(LANES * EDGE, NB),
        ],
        axis=0,
    )
    order = dot(keep, order_rows.astype(bf16)).astype(i32)
    perm[...] = order
    nodes = take(conn_i, order)
    for ref, base in ((end1, 0), (end2, NB)):
        target = lane_no + base
        found = jnp.zeros((ROWS, NB), i32)
        for step in (64, 32, 16, 8, 4, 2, 1, 0):
            probe = take(nodes, found + (step - 1 if step else 0))
            found = jnp.where(probe <= target, found + max(step, 1), found)
        ref[...] = found - 1

    held[...] = jnp.zeros_like(held)
    table[...] = jnp.zeros_like(table)

    zero_row = jnp.zeros((1, NB), f32)
    state[0:1, :] = zero_row + start_gap
    state[1:2, :] = zero_row + start_gap
    state[5:6, :] = jnp.where(overflow > 0.0, jnp.inf, 0.0) + zero_row

    def collect_first():
        wait_bytes(first_b.at[pl.ds(0, chips - 1)], first_recv.at[1])
        total = first_b[0]
        for k in range(1, chips):
            total = total + first_b[k]
        first = jnp.sum(total, axis=1, keepdims=True)
        reaction = first[0:1, :] + zero_row
        speed = start_speed - dt * contact_stiffness * reaction / impactor_mass
        state[1:2, :] = start_gap + dt * speed
        state[2:3, :] = speed
        state[3:4, :] = first[1:2, :] + zero_row
        state[4:5, :] = first[2:3, :] + zero_row
        react[0:1, :] = reaction / node_total

    first_lane = iota((ROWS, NB), 1) == 0

    def to_slots(fields):
        width = len(fields) * NB
        parts = [split3(field) for field in fields]
        for k in range(3):
            table[32 * k : 32 * k + NODE_ROWS, :width] = jnp.concatenate(
                [part[k] for part in parts], axis=1
            )
        both = dot(wab[...], table[:, :width])
        index = conn_idx[...]
        second = half[...] > 0
        slots = []
        for c in range(len(fields)):
            cols = slice(c * NB, (c + 1) * NB)
            slots.append(
                jnp.where(second, take(both[ROWS:, cols], index), take(both[:ROWS, cols], index))
            )
        return slots

    def forces(s):
        top, rest = split2(jnp.concatenate(to_slots([disp[c] for c in range(3)]), axis=1))
        strain = dot(jnp.concatenate([top, rest, top], axis=1), kron[...])
        active = (level[...] & s) == 0
        order = perm[...]
        mod = modulus[...]
        sorted_forces = []
        for c in range(3):
            g = strain[:, c * NB : (c + 1) * NB]
            fresh = mod * (g + hardening * g * g * g)
            now = jnp.where(active, fresh, held[c])
            held[c] = now
            sorted_forces.append(jnp.concatenate(split2(take(now, order)), axis=1))
        sums = dot(jnp.concatenate(sorted_forces, axis=0), tri[...])
        e1 = end1[...]
        e2 = end2[...]
        for c in range(3):
            part = sums[c * ROWS : (c + 1) * ROWS, :]
            upto1 = jnp.where(e1 >= 0, take(part, e1 & (NB - 1)), 0.0)
            upto2 = jnp.where(e2 >= 0, take(part, e2 & (NB - 1)), 0.0)
            prev1 = pltpu.roll(upto1, 1, 1)
            prev2 = pltpu.roll(upto2, 1, 1)
            f1 = split2(upto1 - jnp.where(first_lane, 0.0, prev1))
            f2 = split2(upto2 - jnp.where(first_lane, prev1, prev2))
            cols = slice(c * NB, (c + 1) * NB)
            slot_cols[0:ROWS, cols] = f1[0]
            slot_cols[ROWS : 2 * ROWS, cols] = f2[0]
            slot_cols[2 * ROWS : 3 * ROWS, cols] = f1[1]
            slot_cols[3 * ROWS :, cols] = f2[1]
        return dot(back[...], slot_cols[...])

    ahead = SUBSTEPS - 2

    def sum_ahead():
        centre = state[1:2, :]
        state[6:7, :] = centre
        weight = contact[...]
        inverse = 1.0 / mass[...]
        rate = (dt * contact_stiffness) * weight * inverse
        push = dt * rate
        start_vel = based[0] + centre * rate
        start_disp = [disp[0] + dt * start_vel] + [disp[c] + dt * based[c] for c in (1, 2)]
        owned = iota((NODE_ROWS, NB), 0) < OWN
        share = jnp.where(owned, dt * dt * weight * inverse, 0.0)
        slots = to_slots(start_disp + [push, share])
        top, rest = split2(jnp.concatenate(slots[:3], axis=1))
        g0 = dot(jnp.concatenate([top, rest, top], axis=1), kron[:, :NB])
        top, rest = split2(slots[3])
        first_block = jnp.concatenate(
            [kron[k * 3 * NB : k * 3 * NB + NB, :NB] for k in range(3)], axis=0
        )
        g1 = dot(jnp.concatenate([top, rest, top], axis=1), first_block)
        active = (level[...] & ahead) == 0
        scale = slots[4] * modulus[...]
        scale = jnp.where(active, scale, 0.0)
        kept = jnp.where(active, 0.0, slots[4] * held[0])
        terms = [
            kept + scale * (g0 + hardening * g0 * g0 * g0),
            scale * (g1 + 3.0 * hardening * g0 * g0 * g1),
            scale * (3.0 * hardening) * g0 * g1 * g1,
            scale * hardening * g1 * g1 * g1,
        ]
        nodal = [
            jnp.where(
                owned, weight * (start_gap - start_disp[0] - dt * start_vel + push * start_disp[0]), 0.0
            ),
            jnp.where(owned, weight * push * (push - 2.0), 0.0),
        ]
        rows = [jnp.sum(term, axis=0, keepdims=True) for term in terms]
        rows[0] = rows[0] + jnp.sum(nodal[0], axis=0, keepdims=True) + state[5:6, :]
        rows[1] = rows[1] + jnp.sum(nodal[1], axis=0, keepdims=True)
        last_pay[...] = jnp.concatenate(rows, axis=0)
        last_a[spot_a] = last_pay[...]

        @pl.loop(1, size_a)
        def _(k):
            copy(
                last_pay, last_a.at[spot_a], pay_send.at[4], last_recv.at[0],
                peer_a(shifted(spot_a, k, size_a)),
            ).start()

    def relay_last():
        wait_bytes(last_a.at[pl.ds(0, size_a - 1)], last_recv.at[0])
        value = last_a[0]
        for k in range(1, size_a):
            value = value + last_a[k]
        last_b[chip] = value

        @pl.loop(1, chips)
        def _(k):
            copy(
                last_b.at[chip], last_b.at[chip], pay_send.at[5], last_recv.at[1],
                peer_b(shifted(chip, k, chips)),
            ).start()

    def collect_last():
        wait_bytes(last_b.at[pl.ds(0, chips - 1)], last_recv.at[1])
        value = last_b[0]
        for k in range(1, chips):
            value = value + last_b[k]
        total = jnp.sum(value, axis=1, keepdims=True) + jnp.zeros((4, NB), f32)
        shift = state[7:8, :] - state[6:7, :]
        cubic = total[0:1] + shift * (total[1:2] + shift * (total[2:3] + shift * total[3:4]))
        reaction = (
            cubic + (state[1:2, :] - start_gap) * state[3:4, :] - state[0:1, :] * state[4:5, :]
        )
        react[SUBSTEPS - 1 :, :] = reaction / node_total

    def relay(s):
        wait_bytes(buf_a.at[s, pl.ds(0, size_a - 1)], a_recv.at[s])
        value = buf_a[s, 0]
        for k in range(1, size_a):
            value = value + buf_a[s, k]
        buf_b[s, chip] = value

        @pl.loop(1, chips)
        def _(k):
            copy(
                buf_b.at[s, chip], buf_b.at[s, chip], pay_send.at[3], b_recv.at[s],
                peer_b(shifted(chip, k, chips)),
            ).start()

    def collect(s):
        wait_bytes(buf_b.at[s, pl.ds(0, chips - 1)], b_recv.at[s])
        value = buf_b[s, 0]
        for k in range(1, chips):
            value = value + buf_b[s, k]
        total = jnp.sum(value, axis=1, keepdims=True) + zero_row
        before_z = state[0:1, :]
        now_z = state[1:2, :]
        reaction = total + (now_z - start_gap) * state[3:4, :] - before_z * state[4:5, :]
        react[pl.ds(s + 1, 1), :] = reaction / node_total
        speed = state[2:3, :] - dt * contact_stiffness * reaction / impactor_mass
        state[0:1, :] = now_z
        state[1:2, :] = now_z + dt * speed
        state[2:3, :] = speed

    left = (jnp.where(lane == 0, down, r), lax.rem(lane + LANES - 1, LANES))
    right = (jnp.where(lane == LANES - 1, up, r), lax.rem(lane + 1, LANES))

    def halo_copies(turn):
        return [
            copy(
                halo_out.at[turn, side], halo_in.at[turn, 1 - side],
                halo_send.at[turn, side], halo_recv.at[turn, 1 - side], there,
            )
            for side, there in ((0, left), (1, right))
        ]

    def substep(s):
        force = forces(s)
        since = lax.rem(s, DEPTH)
        row_no = iota((NODE_ROWS, NB), 0)
        ext_no = jnp.where(
            row_no < OWN, row_no + DEPTH, jnp.where(row_no < OWN + DEPTH, row_no - OWN, row_no)
        )
        margin = jnp.where(since == DEPTH - 1, 0, 1 + since)
        valid = (ext_no >= margin) & (ext_no < OWN + 2 * DEPTH - margin)
        weight = contact[...]
        inverse = 1.0 / mass[...]
        for c in range(3):
            pull = -force[:, c * NB : (c + 1) * NB]
            if c == 0:
                pull = pull - contact_stiffness * weight * disp[0]
            based[c] = vel[c] + dt * (pull * inverse)
        free = disp[0, own, :] + dt * based[0, own, :]
        part = jnp.sum(contact[own, :] * (start_gap - free), axis=0, keepdims=True)
        pay[s] = part + state[5:6, :]
        buf_a[s, spot_a] = pay[s]

        @pl.when(s < ahead)
        def _():
            @pl.loop(1, size_a)
            def _(k):
                copy(
                    pay.at[s], buf_a.at[s, spot_a], pay_send.at[2], a_recv.at[s],
                    peer_a(shifted(spot_a, k, size_a)),
                ).start()

        @pl.when((s == 2) | (s == 5))
        def _():
            turn = s // DEPTH
            for side, first in ((0, 0), (1, OWN - DEPTH)):
                for c in range(3):
                    halo_out[turn, side, c] = disp[c, first : first + DEPTH, :]
                    halo_out[turn, side, 3 + c] = based[c, first : first + DEPTH, :]
            moves = halo_copies(turn)
            for move in moves:
                move.start()

            @pl.loop(0, 3)
            def _(k):
                relay(s - 2 + k)

            for move in moves:
                move.wait_recv()
            for side, place in ((0, left_row), (1, right_row)):
                for c in range(3):
                    disp[c, place : place + DEPTH, :] = halo_in[turn, side, c]
                    based[c, place : place + DEPTH, :] = halo_in[turn, side, 3 + c]

        @pl.when(s == ahead - 1)
        def _():
            sum_ahead()

        @pl.when(s == 1)
        def _():
            collect_first()

        @pl.when(s >= 2)
        def _():
            collect(s - 2)

        @pl.when(s == ahead - 1)
        def _():
            state[7:8, :] = state[1:2, :]

        z_now = state[1:2, :]
        pushed = (dt * contact_stiffness) * z_now * (weight * inverse)
        for c in range(3):
            fresh = based[c] + pushed if c == 0 else based[c]
            vel[c] = jnp.where(valid, fresh, vel[c])
            disp[c] = jnp.where(valid, disp[c] + dt * fresh, disp[c])

    own_part = pl.ds(pl.multiple_of(lane * (OWN * NB), OWN * NB), OWN * NB)
    other_parts = pl.ds(0, (LANES - 1) * OWN * NB)

    def gather_out(source, ref, slot):
        start = pl.multiple_of(lane * (OWN * NB), OWN * NB)
        for j in range(OWN):
            for c in range(3):
                ref[c : c + 1, pl.ds(start + j * NB, NB)] = source[c, j : j + 1, :]

        @pl.loop(1, LANES)
        def _(k):
            there = (r, shifted(lane, k, LANES))
            copy(
                ref.at[:, own_part], ref.at[:, own_part], send_sem.at[5 + slot],
                recv_sem.at[4 + slot], there,
            ).start()

    @pl.loop(0, SUBSTEPS)
    def _(s):
        substep(s)

        @pl.when(s == SUBSTEPS - 2)
        def _():
            gather_out(disp, disp_all, 0)

    gather_out(vel, vel_out, 1)
    relay_last()
    wait_bytes(disp_all.at[:, other_parts], recv_sem.at[4])
    for s in range(SUBSTEPS - 1):
        react_out[s] = jnp.max(react[s : s + 1, :])
    wait_bytes(vel_out.at[:, other_parts], recv_sem.at[5])
    disp_out[...] = disp_all[...] + dt * vel_out[...]
    collect_last()
    react_out[SUBSTEPS - 1] = jnp.max(react[SUBSTEPS - 1 :, :])
    flag_out[0] = jnp.max(jnp.where(jnp.abs(react[...]) < jnp.inf, 0, 1))

    edge_up.wait_send()
    edge_down.wait_send()

    @pl.when((lane == 0) | (lane == LANES - 1))
    def _():
        rim_up.wait_send()

    order_up.wait_send()
    order_down.wait_send()
    for turn in range(2):
        for move in halo_copies(turn):
            move.wait_send()
    wait_bytes(pack_in.at[pl.ds(0, LANES - 1)], send_sem.at[3])
    wait_bytes(order_in.at[pl.ds(0, LANES - 1)], send_sem.at[4])
    wait_bytes(disp_all.at[:, other_parts], send_sem.at[5])
    wait_bytes(vel_out.at[:, other_parts], send_sem.at[6])
    wait_bytes(first_a.at[pl.ds(0, size_a - 1)], pay_send.at[0])
    wait_bytes(first_b.at[pl.ds(0, chips - 1)], pay_send.at[1])
    wait_bytes(buf_a.at[pl.ds(0, ahead), pl.ds(0, size_a - 1)], pay_send.at[2])
    wait_bytes(buf_b.at[pl.ds(0, ahead), pl.ds(0, chips - 1)], pay_send.at[3])
    wait_bytes(last_a.at[pl.ds(0, size_a - 1)], pay_send.at[4])
    wait_bytes(last_b.at[pl.ds(0, chips - 1)], pay_send.at[5])


def run_cycle(regions, init_disp, init_vel, mass, contact, modulus, stiffness, levels, windows, conn):
    chips = regions // 2
    vmem = pl.BlockSpec(memory_space=pltpu.VMEM)
    V = pltpu.VMEM
    vel, disp, react, flag = pl.pallas_call(
        functools.partial(cycle_kernel, regions),
        out_shape=(
            jax.ShapeDtypeStruct(init_vel.shape, f32),
            jax.ShapeDtypeStruct(init_disp.shape, f32),
            jax.ShapeDtypeStruct((SUBSTEPS,), f32),
            jax.ShapeDtypeStruct((1,), i32),
        ),
        in_specs=[pl.BlockSpec(memory_space=pl.ANY)] * 9,
        out_specs=[vmem] * 2 + [pl.BlockSpec(memory_space=pltpu.SMEM)] * 2,
        scratch_shapes=[
            V(init_disp.shape, f32), V(init_vel.shape, f32), V((LANES * OWN, NB), f32),
            V((LANES * OWN, NB), f32), V((16, 64), f32), V((24, 24), f32),
            V((1, 64), i32), V((1, 64), i32), V((64, NB), i32),
            V((LANES, PACK, 2 * NB), f32), V((LANES, PACK, 2 * NB), f32),
            V((2, EDGE, 2 * NB), f32), V((LANES, EDGE, 2 * NB), f32),
            V((LANES, PACK, NB), f32), V((LANES, PACK, NB), f32),
            V((2, EDGE, NB), f32), V((LANES, EDGE, NB), f32),
            V((8, DEPTH, NB), f32), V((8, DEPTH, NB), f32),
            V((2, 2, 6, DEPTH, NB), f32), V((2, 2, 6, DEPTH, NB), f32),
            V((3, NB), f32), V((2 * LANES, 3, NB), f32), V((chips, 3, NB), f32),
            V((SUBSTEPS, 1, NB), f32), V((SUBSTEPS, 2 * LANES, 1, NB), f32),
            V((SUBSTEPS, chips, 1, NB), f32),
            V((4, NB), f32), V((2 * LANES, 4, NB), f32), V((chips, 4, NB), f32),
            V((SUBSTEPS, NB), f32), V(init_disp.shape, f32),
            V((3, NODE_ROWS, NB), f32), V((3, NODE_ROWS, NB), f32), V((3, NODE_ROWS, NB), f32),
            V((NODE_ROWS, NB), f32), V((NODE_ROWS, NB), f32),
            V((NB, 5 * NB), bf16), V((4 * ROWS, 3 * NB), bf16),
            V((9 * NB, 3 * NB), bf16), V((2 * NB, NB), bf16),
            V((2 * ROWS, NB), bf16), V((NODE_ROWS, 4 * ROWS), bf16),
            V((ROWS, NB), i32), V((ROWS, NB), i32), V((ROWS, NB), i32),
            V((ROWS, NB), i32), V((ROWS, NB), i32),
            V((ROWS, NB), f32), V((ROWS, NB), i32), V((3, ROWS, NB), f32), V((8, NB), f32),
            pltpu.SemaphoreType.DMA((9,)), pltpu.SemaphoreType.DMA((7,)),
            pltpu.SemaphoreType.DMA((6,)), pltpu.SemaphoreType.DMA((2,)),
            pltpu.SemaphoreType.DMA((SUBSTEPS,)), pltpu.SemaphoreType.DMA((SUBSTEPS,)),
            pltpu.SemaphoreType.DMA((9,)),
            pltpu.SemaphoreType.DMA((2, 2)), pltpu.SemaphoreType.DMA((2, 2)),
            pltpu.SemaphoreType.DMA((2,)),
        ],
        compiler_params=pltpu.CompilerParams(
            collective_id=0, has_side_effects=True, vmem_limit_bytes=48 * 1024 * 1024
        ),
        name="crush_cycle",
    )(
        init_disp, init_vel, mass.reshape(-1, NB), contact.reshape(-1, NB), modulus.T, stiffness,
        levels.reshape(1, -1), windows.reshape(1, -1), conn,
    )
    return (disp, vel, react), flag[0]


def sum_over(value, axis):
    count = lax.axis_size(axis)
    step = 1
    while step < count:
        value = value + lax.ppermute(value, axis, [(i, i ^ step) for i in range(count)])
        step *= 2
    return value


def with_halo(array, sides, width):
    for axis, dim in sides:
        count, length = (lax.axis_size(axis), array.shape[dim])
        up = [(i, (i + 1) % count) for i in range(count)]
        down = [(j, i) for i, j in up]
        last = lax.slice_in_dim(array, length - width, length, axis=dim)
        initial = lax.slice_in_dim(array, 0, width, axis=dim)
        before = lax.ppermute(last, axis, up)
        after = lax.ppermute(initial, axis, down)
        array = jnp.concatenate([before, array, after], axis=dim)
    return array


def element_forces(slot_disp, block_modulus, stiffness):
    count = slot_disp.shape[0]
    elements = block_modulus.shape[1]
    vectors = (
        slot_disp.reshape(count, 3, elements, 8).transpose(0, 2, 1, 3).reshape(count, elements, 24)
    )
    strain = jnp.einsum("bek,jk->bej", vectors, stiffness, precision=lax.Precision.HIGHEST)
    result = block_modulus[:, :, None] * (strain + hardening * strain * strain * strain)
    return (
        result.reshape(count, elements, 3, 8).transpose(0, 2, 1, 3).reshape(count, 3, elements * 8)
    )


def plain_cycle(init_disp, init_vel, mass, contact, modulus, stiffness, levels, windows, conn):
    region_count = lax.axis_size("region")
    node_region = init_disp.shape[1]
    slot_count = conn.shape[1]
    block_rows = NB
    node_total = node_region * region_count
    impactor_mass = impactor_ratio * node_total
    extended_blocks = node_region // block_rows + 2
    block_order = jnp.argsort(levels, stable=True)
    conn = conn[block_order]
    windows = windows[block_order]
    levels = levels[block_order]
    modulus = modulus[block_order]
    level_slot = (
        (levels >= 2).astype(jnp.int32)
        + (levels >= 4).astype(jnp.int32)
        + (levels >= 8).astype(jnp.int32)
    )
    level_force = jnp.zeros((4, 3, extended_blocks, block_rows), jnp.float32)
    disp_full = init_disp
    disp_state = init_disp
    vel_state = init_vel
    gap_now = jnp.float32(start_gap)
    speed = jnp.float32(start_speed)
    history = []
    slot_iota = lax.broadcasted_iota(jnp.int32, (group_size, 2 * block_rows, slot_count), 1)
    for substep in range(SUBSTEPS):
        top_level = SUBSTEPS if substep == 0 else min(substep & -substep, SUBSTEPS)
        top_index = top_level.bit_length() - 1
        active_count = jnp.sum((levels <= top_level).astype(jnp.int32))
        level_force = level_force.at[: top_index + 1].set(0.0)
        disp_ext = with_halo(disp_full, (("region", 1),), block_rows)

        def one_group(group_index, totals):
            offset = group_index * group_size
            conn_group = lax.dynamic_slice_in_dim(conn, offset, group_size, 0)
            window_group = lax.dynamic_slice_in_dim(windows, offset, group_size, 0)
            level_group = lax.dynamic_slice_in_dim(level_slot, offset, group_size, 0)
            modulus_group = lax.dynamic_slice_in_dim(modulus, offset, group_size, 0)
            valid = offset + jnp.arange(group_size, dtype=jnp.int32) < active_count
            window_disp = jax.vmap(
                lambda first_block: lax.dynamic_slice_in_dim(
                    disp_ext, first_block * block_rows, 2 * block_rows, 1
                )
            )(window_group)
            onehot = (slot_iota == conn_group[:, None, :]).astype(jnp.float32)
            slot_disp = jnp.einsum(
                "gcw,gws->gcs", window_disp, onehot, precision=lax.Precision.HIGHEST
            )
            slot_force = element_forces(slot_disp, modulus_group, stiffness)
            slot_force = jnp.where(valid[:, None, None], slot_force, 0.0)
            window_force = jnp.einsum(
                "gcs,gws->gcw", slot_force, onehot, precision=lax.Precision.HIGHEST
            )
            window_force = window_force.reshape(group_size, 3, 2, block_rows)
            totals = totals.at[level_group, :, window_group].add(window_force[:, :, 0])
            totals = totals.at[level_group, :, window_group + 1].add(window_force[:, :, 1])
            return totals

        group_total = (active_count + group_size - 1) // group_size
        level_force = lax.fori_loop(0, group_total, one_group, level_force)
        force_ext = jnp.sum(level_force, axis=0).reshape(3, extended_blocks * block_rows)
        outer_rims = jnp.concatenate(
            (force_ext[:, :block_rows], force_ext[:, -block_rows:]), axis=1
        )
        rim_terms = with_halo(outer_rims, (("region", 1),), block_rows)
        partial_force = force_ext[:, block_rows:-block_rows]
        partial_force = partial_force.at[:, :block_rows].add(rim_terms[:, :block_rows])
        partial_force = partial_force.at[:, -block_rows:].add(rim_terms[:, -block_rows:])
        force = sum_over(partial_force, "lane")
        disp_state = disp_full
        gap = gap_now - disp_state[0]
        total = sum_over(jnp.sum(contact * gap), "region")
        history.append(total / node_total)
        push = jnp.zeros_like(force).at[0].set(contact_stiffness * contact * gap)
        accel = (push - force) / mass[None, :]
        vel_state = vel_state + time_step * accel
        disp_state = disp_state + time_step * vel_state
        speed = speed - time_step * contact_stiffness * total / impactor_mass
        gap_now = gap_now + time_step * speed
        disp_full = disp_state
    return (disp_full, vel_state, jnp.stack(history))


def on_device(*arguments):
    regions = lax.axis_size("region")
    fast, flag = run_cycle(regions, *arguments)
    return lax.cond(flag == 0, lambda: fast, lambda: plain_cycle(*arguments))


def solution(mesh):
    in_specs = (
        P(None, "region"),
        P(None, "region"),
        P("region"),
        P("region"),
        P(("region", "lane"), None),
        P(),
        P(("region", "lane")),
        P(("region", "lane")),
        P(("region", "lane"), None),
    )
    out_specs = (P(None, "region"), P(None, "region"), P())
    return jax.shard_map(
        on_device, mesh=mesh, in_specs=in_specs, out_specs=out_specs, check_vma=False
    )
```

```python
import functools

import jax
import jax.numpy as jnp
from jax import lax
from jax.experimental import pallas as pl
from jax.experimental.pallas import tpu as pltpu
from jax.sharding import PartitionSpec as P

NB = 128
SUBSTEPS = 8
LANES = 8
FAR_FIRST = (4, 3, 5, 2, 6, 1, 7)
OWN = 8
DEPTH = 3
NODE_ROWS = 16
ANCHORS = OWN - 1 + 2 * DEPTH
ROWS = 160
PACK = 32
EDGE = 16

time_step = 0.05
contact_stiffness = 1.0
hardening = 2.0
impactor_ratio = 0.05
start_gap = 1.0
start_speed = 1.0
group_size = 8

f32, bf16, i32 = jnp.float32, jnp.bfloat16, jnp.int32


def iota(shape, dim):
    return lax.broadcasted_iota(i32, shape, dim)


def dot(a, b):
    return jnp.dot(a, b, preferred_element_type=f32)


def dot_t(a, b):
    return lax.dot_general(a, b, (((1,), (1,)), ((), ())), preferred_element_type=f32)


def split2(value):
    high = value.astype(bf16)
    return high, (value - high.astype(f32)).astype(bf16)


def split3(value):
    high = value.astype(bf16)
    rest = value - high.astype(f32)
    middle = rest.astype(bf16)
    return high, middle, (rest - middle.astype(f32)).astype(bf16)


def take(value, index):
    return jnp.take_along_axis(value, index, axis=1, mode="promise_in_bounds")


def row_of(ext):
    return jnp.where(ext < DEPTH, ext + OWN, jnp.where(ext < DEPTH + OWN, ext - DEPTH, ext))


def onehot(mask):
    return jnp.where(mask, 1.0, 0.0).astype(bf16)


def cycle_kernel(
    regions,
    disp_far, vel_far, mass_far, contact_far, modulus_far, stiff_far, level_far, window_far, conn_far,
    vel_out, disp_out, react_out, flag_out,
    disp_in, vel_in, mass_in, contact_in, modulus_in, stiff_in, level_in, window_in, conn_in,
    pack_out, pack_in, edge_out, edge_in, order_out, order_in, order_edge_out, order_edge_in,
    rim_out, rim_in, halo_out, halo_in,
    first_pay, first_a, first_b, pay, buf_a, buf_b, last_pay, last_a, last_b, react, disp_all,
    disp, vel, based, mass, contact, table, slot_cols, kron, tri,
    wab, back, keep_rows, strict, conn_idx, half, perm, end1, end2, modulus, level, held, state,
    send_sem, recv_sem, pay_send, first_recv, a_recv, b_recv, load_sem, halo_send, halo_recv, last_recv, vouch,
):
    r = lax.axis_index("region")
    lane = lax.axis_index("lane")
    core = lax.rem(r, 2)
    chip = r // 2
    chips = regions // 2
    up = lax.rem(r + 1, regions)
    down = lax.rem(r + regions - 1, regions)
    size_a = 2 * LANES
    spot_a = lane * 2 + core
    dt = time_step
    node_total = regions * LANES * OWN * NB
    impactor_mass = impactor_ratio * node_total

    def peer_a(k):
        return (chip * 2 + lax.rem(k, 2), k // 2)

    def peer_b(k):
        return (k * 2 + core, lane)

    def signal(device):
        pl.semaphore_signal(
            pltpu.get_barrier_semaphore(), inc=1, device_id=device,
            device_id_type=pl.DeviceIdType.MESH,
        )

    def shifted(spot, step, size):
        return lax.rem(spot + step, size)

    @pl.loop(1, size_a)
    def _(k):
        signal(peer_a(shifted(spot_a, k, size_a)))

    deep = min(chips, LANES)
    wide = chips // deep

    def along_x(k):
        return peer_b(lax.rem(chip // deep + k, wide) * deep + lax.rem(chip, deep))

    def along_z(k):
        return peer_b((chip // deep) * deep + lax.rem(chip + k, deep))

    for k in range(1, deep):
        signal(along_z(k))
    for k in range(1, wide):
        signal(along_x(k))

    @pl.when(lane == 0)
    def _():
        @pl.loop(0, LANES)
        def _(j):
            signal((down, j))

    @pl.when(lane == LANES - 1)
    def _():
        @pl.loop(0, LANES)
        def _(j):
            signal((up, j))

    def copy(src, dst, send, recv, device):
        return pltpu.make_async_remote_copy(
            src_ref=src, dst_ref=dst, send_sem=send, recv_sem=recv,
            device_id=device, device_id_type=pl.DeviceIdType.MESH,
        )

    def wait_bytes(ref, sem):
        pltpu.make_async_copy(ref, ref, sem).wait()

    loads = []
    for k, (far, here) in enumerate((
        (level_far, level_in), (window_far, window_in), (modulus_far, modulus_in),
        (conn_far, conn_in), (contact_far, contact_in), (mass_far, mass_in),
        (disp_far, disp_in), (vel_far, vel_in), (stiff_far, stiff_in),
    )):
        loads.append(pltpu.make_async_copy(far, here, load_sem.at[k]))
        loads[-1].start()
    for load in loads:
        load.wait()

    level_row = level_in[...].astype(f32)
    window_row = window_in[...].astype(f32)
    dest = iota((16, 64), 0)
    offsets = jnp.where(
        dest < LANES, (DEPTH - 1) - OWN * dest,
        jnp.where(dest == LANES, DEPTH - 1 - OWN * LANES, OWN + DEPTH - 1),
    ).astype(f32)
    anchor_all = window_row + offsets
    lowest = jnp.where(dest == LANES + 1, OWN + DEPTH - 1, 0).astype(f32)
    highest = jnp.where(dest == LANES, DEPTH - 1, ANCHORS - 1).astype(f32)
    wanted = jnp.where(
        (anchor_all >= lowest) & (anchor_all <= highest) & (dest < LANES + 2), 1.0, 0.0
    )
    before = onehot(iota((64, 64), 0) < iota((64, 64), 1))
    rank_key = jnp.where(wanted > 0.0, dot(wanted.astype(bf16), before), -1.0)
    count = jnp.sum(wanted, axis=1, keepdims=True)
    room = jnp.where(iota((16, 1), 0) < LANES, PACK, EDGE).astype(f32)
    overflow = jnp.max(jnp.where(count > room, 1.0, 0.0), axis=0, keepdims=True)
    picks = [
        onehot(iota((PACK, 64), 0).astype(f32) == rank_key[k : k + 1, :]) for k in range(LANES)
    ] + [
        onehot(iota((EDGE, 64), 0).astype(f32) == rank_key[k : k + 1, :])
        for k in (LANES, LANES + 1)
    ]
    pick = jnp.concatenate(picks, axis=0)
    conn_f = conn_in[...].astype(f32)
    picked = LANES * PACK + 2 * EDGE
    tiled = jnp.concatenate([modulus_in[...]] * 8, axis=0)
    chosen = sum(dot_t(pick, part) for part in split3(tiled))
    chosen = jnp.where(
        (iota((picked, NB), 0) & 7) == iota((picked, NB), 1) // 16, chosen, 0.0
    )
    grouped = jnp.sum(chosen.reshape(picked // 8, 8, NB), axis=1)
    facts = jnp.concatenate(
        [level_row, window_row, jnp.ones((1, 64), f32), jnp.zeros((5, 64), f32)], axis=0
    ).astype(bf16)
    chosen_conn = dot(pick, conn_f.astype(bf16))
    spot = iota((NB, 64), 0).astype(f32)

    def lane_rows(k, start, offset):
        key = jnp.where(rank_key[k : k + 1, :] >= 0.0, rank_key[k : k + 1, :] + start, -1.0)
        found = dot_t(facts, onehot(spot == key))
        return jnp.concatenate(
            [found[0:1, :], found[1:2, :] + float(offset) * found[2:3, :], jnp.zeros((2, NB), f32)],
            axis=0,
        )

    quarter = (PACK * lax.rem(lane, 4)).astype(f32)
    eighth = (EDGE * lane).astype(f32)
    for k in range(LANES):
        pack_out[k, :PACK, :] = chosen_conn[k * PACK : (k + 1) * PACK, :]
        pack_out[k, PACK : PACK + 4, :] = grouped[4 * k : 4 * k + 4, :]
        pack_out[k, PACK + 4 :, :] = lane_rows(k, quarter, DEPTH - 1 - OWN * k)
    for k, offset in ((0, DEPTH - 1 - OWN * LANES), (1, OWN + DEPTH - 1)):
        start = LANES * PACK + k * EDGE
        edge_out[k, :EDGE, :] = chosen_conn[start : start + EDGE, :]
        edge_out[k, EDGE : EDGE + 4, :] = jnp.concatenate(
            [grouped[start // 8 : start // 8 + 2, :], jnp.zeros((2, NB), f32)], axis=0
        )
        edge_out[k, EDGE + 4 :, :] = lane_rows(LANES + k, eighth, offset)

    def load_nodes(place, source_lane, first, number):
        start = pl.multiple_of(source_lane * (OWN * NB), OWN * NB)
        for j in range(number):
            part = pl.ds(start + (first + j) * NB, NB)
            for c in range(3):
                disp[c, place + j : place + j + 1, :] = disp_in[c : c + 1, part]
                vel[c, place + j : place + j + 1, :] = vel_in[c : c + 1, part]
        rows = pl.ds(pl.multiple_of(source_lane * OWN, OWN), OWN)
        mass[place : place + number, :] = mass_in[rows, :][first : first + number, :]
        contact[place : place + number, :] = contact_in[rows, :][first : first + number, :]

    left_row, right_row = OWN, OWN + DEPTH
    disp[...] = jnp.zeros_like(disp)
    vel[...] = jnp.zeros_like(vel)
    mass[...] = jnp.ones_like(mass)
    contact[...] = jnp.zeros_like(contact)
    load_nodes(0, lane, 0, OWN)

    own = pl.ds(0, OWN)
    own_contact = contact[own, :]
    own_mass = mass[own, :]
    push_rate = (dt * dt * contact_stiffness) * own_contact / own_mass
    sums = [
        jnp.sum(own_contact * (start_gap - disp[0, own, :]), axis=0, keepdims=True),
        jnp.sum(own_contact, axis=0, keepdims=True),
        jnp.sum(own_contact * push_rate, axis=0, keepdims=True),
    ]
    first_pay[...] = jnp.concatenate(sums, axis=0)
    first_a[spot_a] = first_pay[...]

    pl.semaphore_wait(pltpu.get_barrier_semaphore(), size_a - 1 + deep - 1 + wide - 1 + 2)
    for k in range(1, wide):
        pl.semaphore_signal(
            vouch, inc=1, device_id=along_x(k), device_id_type=pl.DeviceIdType.MESH
        )

    @pl.loop(1, size_a)
    def _(k):
        copy(
            first_pay, first_a.at[spot_a], pay_send.at[0], first_recv.at[0],
            peer_a(shifted(spot_a, k, size_a)),
        ).start()

    edge_up = copy(edge_out.at[0], edge_in.at[lane], send_sem.at[0], recv_sem.at[0], (up, 0))
    edge_down = copy(
        edge_out.at[1], edge_in.at[lane], send_sem.at[1], recv_sem.at[0], (down, LANES - 1)
    )
    edge_up.start()
    edge_down.start()

    for k in FAR_FIRST:
        there = shifted(lane, k, LANES)
        copy(
            pack_out.at[there], pack_in.at[lane], send_sem.at[3], recv_sem.at[2], (r, there)
        ).start()

    def load_rim(rim_lane, first):
        for j in range(DEPTH):
            at = (rim_lane * OWN + first + j) * NB
            part = slice(at, at + NB)
            for c in range(3):
                rim_out[c, j : j + 1, :] = disp_in[c : c + 1, part]
                rim_out[3 + c, j : j + 1, :] = vel_in[c : c + 1, part]
        rows = slice(rim_lane * OWN + first, rim_lane * OWN + first + DEPTH)
        rim_out[6, :, :] = mass_in[rows, :]
        rim_out[7, :, :] = contact_in[rows, :]

    @pl.when(lane == 0)
    def _():
        load_rim(LANES - 1, OWN - DEPTH)

    @pl.when(lane == LANES - 1)
    def _():
        load_rim(0, 0)

    rim_up = copy(rim_out, rim_in, send_sem.at[2], recv_sem.at[1], (up, 0))
    rim_down = copy(rim_out, rim_in, send_sem.at[2], recv_sem.at[1], (down, LANES - 1))

    @pl.when(lane == 0)
    def _():
        rim_up.start()

    @pl.when(lane == LANES - 1)
    def _():
        rim_down.start()

    pack_in[lane] = pack_out[lane]
    load_nodes(left_row, jnp.maximum(lane - 1, 0), OWN - DEPTH, DEPTH)
    load_nodes(right_row, jnp.minimum(lane + 1, LANES - 1), 0, DEPTH)

    lane64 = iota((64, NB), 1)
    keys = conn_f * float(NB) + lane64.astype(f32)
    span = 2
    while span <= NB:
        step = span // 2
        while step >= 1:
            other = take(keys, lane64 ^ step)
            keep_low = ((lane64 & step) == 0) == ((lane64 & span) == 0)
            keys = jnp.where(keep_low, jnp.minimum(keys, other), jnp.maximum(keys, other))
            step //= 2
        span *= 2
    order = (keys.astype(i32) & (NB - 1)).astype(f32)
    chosen_order = dot(pick, order.astype(bf16))
    for k in range(LANES):
        order_out[k] = chosen_order[k * PACK : (k + 1) * PACK, :]
    for k in range(2):
        start = LANES * PACK + k * EDGE
        order_edge_out[k] = chosen_order[start : start + EDGE, :]
    order_up = copy(
        order_edge_out.at[0], order_edge_in.at[lane], send_sem.at[7], recv_sem.at[6], (up, 0)
    )
    order_down = copy(
        order_edge_out.at[1], order_edge_in.at[lane], send_sem.at[8], recv_sem.at[6],
        (down, LANES - 1),
    )
    order_up.start()
    order_down.start()

    for k in FAR_FIRST:
        there = shifted(lane, k, LANES)
        copy(
            order_out.at[there], order_in.at[lane], send_sem.at[4], recv_sem.at[3], (r, there)
        ).start()

    order_in[lane] = order_out[lane]

    offered = LANES * (PACK + EDGE)
    strict[...] = onehot(iota((offered, offered), 0) < iota((offered, offered), 1))
    stiff = split2(stiff_in[...])
    at = iota((3 * NB, 24), 0)
    names = onehot((at // NB) * 8 + lax.rem(at, 8) == iota((3 * NB, 24), 1))
    row_element = lax.rem(iota((3 * NB, 3 * NB), 0), NB) // 8
    col_element = lax.rem(iota((3 * NB, 3 * NB), 1), NB) // 8
    same = row_element == col_element
    for part, places in ((stiff[0], (0, 1)), (stiff[1], (2,))):
        grown = dot_t(dot_t(names, part).astype(bf16), names)
        grown = jnp.where(same, grown, 0.0).astype(bf16)
        for at_place in places:
            kron[at_place * 3 * NB : (at_place + 1) * 3 * NB, :] = grown
    running = onehot(iota((NB, NB), 0) <= iota((NB, NB), 1))
    tri[0:NB, :] = running
    tri[NB:, :] = running

    @pl.when((lane != 0) & (lane != LANES - 1))
    def _():
        edge_in[...] = jnp.zeros_like(edge_in)
        order_edge_in[...] = jnp.zeros_like(order_edge_in)

    if wide > 1:
        pl.semaphore_wait(vouch, wide - 1)
    wait_bytes(first_a.at[pl.ds(0, size_a - 1)], first_recv.at[0])
    total = first_a[0]
    for k in range(1, size_a):
        total = total + first_a[k]
    first_b[chip] = total
    first_pay2 = first_b.at[chip]

    @pl.loop(1, chips)
    def _(k):
        copy(
            first_pay2, first_b.at[chip], pay_send.at[1], first_recv.at[1],
            peer_b(shifted(chip, k, chips)),
        ).start()

    @pl.when((lane == 0) | (lane == LANES - 1))
    def _():
        wait_bytes(edge_in, recv_sem.at[0])
        wait_bytes(rim_in, recv_sem.at[1])

    def unpack_rim(place):
        for c in range(3):
            disp[c, place : place + DEPTH, :] = rim_in[c]
            vel[c, place : place + DEPTH, :] = rim_in[3 + c]
        mass[place : place + DEPTH, :] = rim_in[6]
        contact[place : place + DEPTH, :] = rim_in[7]

    @pl.when(lane == 0)
    def _():
        unpack_rim(left_row)

    @pl.when(lane == LANES - 1)
    def _():
        unpack_rim(right_row)

    wait_bytes(pack_in.at[pl.ds(0, LANES - 1)], recv_sem.at[2])

    conn_rows = jnp.concatenate(
        [pack_in[j, :PACK, :] for j in range(LANES)] + [edge_in[j, :EDGE, :] for j in range(LANES)],
        axis=0,
    )
    shared = jnp.concatenate(
        [pack_in[j, PACK : PACK + 4, :] for j in range(LANES)]
        + [edge_in[j, EDGE : EDGE + 2, :] for j in range(LANES)],
        axis=0,
    )
    shared = jnp.broadcast_to(shared[:, None, :], (offered // 8, 8, NB)).reshape(offered, NB)
    moduli = take(shared, 16 * (iota((offered, NB), 0) & 7) + iota((offered, NB), 1) // 8)
    facts_in = jnp.concatenate(
        [
            sum(pack_in[j, PACK + 4 :, :] for j in range(4)),
            sum(pack_in[j, PACK + 4 :, :] for j in range(4, LANES)),
            sum(edge_in[j, EDGE + 4 :, :] for j in range(LANES)),
        ],
        axis=1,
    )
    levels_in = facts_in[0:1, :]
    anchors_in = facts_in[1:2, :]
    present = jnp.where(levels_in > 0.0, 1.0, 0.0) + jnp.zeros((8, offered), f32)
    key = jnp.where(present > 0.0, dot(present.astype(bf16), strict[...]), -1.0)[0:1, :]
    taken = jnp.sum(present[0:1, :], axis=1, keepdims=True)
    overflow = jnp.maximum(overflow, jnp.where(taken > float(ROWS), 1.0, 0.0))
    keep = onehot(iota((ROWS, offered), 0).astype(f32) == key)
    conn = dot(keep, conn_rows.astype(bf16))
    moduli_parts = split3(moduli)
    modulus[...] = sum(dot(keep, part) for part in moduli_parts)
    wide_levels = (levels_in + jnp.zeros((NB, offered), f32)).astype(bf16)
    wide_anchors = (anchors_in + jnp.zeros((NB, offered), f32)).astype(bf16)

    lane_no = iota((ROWS, NB), 1)
    level[...] = dot_t(keep, wide_levels).astype(i32) - 1
    anchor = dot_t(keep, wide_anchors).astype(i32)
    wab[:ROWS, :] = onehot((lane_no & 31) == row_of(anchor))
    wab[ROWS:, :] = onehot((lane_no & 31) == row_of(anchor + 1))
    anchor_row = dot_t(wide_anchors[:8, :], keep)[0:1, :].astype(i32)
    node_row = iota((NODE_ROWS, ROWS), 0)
    back_a = onehot(node_row == row_of(anchor_row))
    back_b = onehot(node_row == row_of(anchor_row + 1))
    back[...] = jnp.concatenate([back_a, back_b, back_a, back_b], axis=1)
    conn_i = conn.astype(i32)
    conn_idx[...] = conn_i & (NB - 1)
    half[...] = conn_i >> 7

    keep_rows[...] = keep
    held[...] = jnp.zeros_like(held)
    table[...] = jnp.zeros_like(table)

    zero_row = jnp.zeros((1, NB), f32)
    state[0:1, :] = zero_row + start_gap
    state[1:2, :] = zero_row + start_gap
    state[5:6, :] = jnp.where(overflow > 0.0, jnp.inf, 0.0) + zero_row

    def collect_first():
        wait_bytes(first_b.at[pl.ds(0, chips - 1)], first_recv.at[1])
        total = first_b[0]
        for k in range(1, chips):
            total = total + first_b[k]
        first = jnp.sum(total, axis=1, keepdims=True)
        reaction = first[0:1, :] + zero_row
        speed = start_speed - dt * contact_stiffness * reaction / impactor_mass
        state[1:2, :] = start_gap + dt * speed
        state[2:3, :] = speed
        state[3:4, :] = first[1:2, :] + zero_row
        state[4:5, :] = first[2:3, :] + zero_row
        react[0:1, :] = reaction / node_total

    first_lane = iota((ROWS, NB), 1) == 0

    def to_slots(fields):
        width = len(fields) * NB
        parts = [split3(field) for field in fields]
        for k in range(3):
            table[32 * k : 32 * k + NODE_ROWS, :width] = jnp.concatenate(
                [part[k] for part in parts], axis=1
            )
        both = dot(wab[...], table[:, :width])
        index = conn_idx[...]
        second = half[...] > 0
        slots = []
        for c in range(len(fields)):
            cols = slice(c * NB, (c + 1) * NB)
            slots.append(
                jnp.where(second, take(both[ROWS:, cols], index), take(both[:ROWS, cols], index))
            )
        return slots

    def receive_order():
        lane_no = iota((ROWS, NB), 1)

        @pl.when((lane == 0) | (lane == LANES - 1))
        def _():
            wait_bytes(order_edge_in, recv_sem.at[6])

        wait_bytes(order_in.at[pl.ds(0, LANES - 1)], recv_sem.at[3])
        order_rows = jnp.concatenate(
            [
                order_in[...].reshape(LANES * PACK, NB),
                order_edge_in[...].reshape(LANES * EDGE, NB),
            ],
            axis=0,
        )
        order = dot(keep_rows[...], order_rows.astype(bf16)).astype(i32)
        perm[...] = order
        nodes = take(half[...] * NB + conn_idx[...], order)
        for ref, base in ((end1, 0), (end2, NB)):
            target = lane_no + base
            found = jnp.zeros((ROWS, NB), i32)
            for step in (64, 32, 16, 8, 4, 2, 1, 0):
                probe = take(nodes, found + (step - 1 if step else 0))
                found = jnp.where(probe <= target, found + max(step, 1), found)
            ref[...] = found - 1

    def forces(s):
        top, rest = split2(jnp.concatenate(to_slots([disp[c] for c in range(3)]), axis=1))
        strain = dot(jnp.concatenate([top, rest, top], axis=1), kron[...])
        active = (level[...] & s) == 0
        mod = modulus[...]
        for c in range(3):
            g = strain[:, c * NB : (c + 1) * NB]
            fresh = mod * (g + hardening * g * g * g)
            held[c] = jnp.where(active, fresh, held[c])

        @pl.when(s == 0)
        def _():
            receive_order()

        order = perm[...]
        sorted_forces = []
        for c in range(3):
            sorted_forces.append(jnp.concatenate(split2(take(held[c], order)), axis=1))
        sums = dot(jnp.concatenate(sorted_forces, axis=0), tri[...])
        e1 = end1[...]
        e2 = end2[...]
        for c in range(3):
            part = sums[c * ROWS : (c + 1) * ROWS, :]
            upto1 = jnp.where(e1 >= 0, take(part, e1 & (NB - 1)), 0.0)
            upto2 = jnp.where(e2 >= 0, take(part, e2 & (NB - 1)), 0.0)
            prev1 = pltpu.roll(upto1, 1, 1)
            prev2 = pltpu.roll(upto2, 1, 1)
            f1 = split2(upto1 - jnp.where(first_lane, 0.0, prev1))
            f2 = split2(upto2 - jnp.where(first_lane, prev1, prev2))
            cols = slice(c * NB, (c + 1) * NB)
            slot_cols[0:ROWS, cols] = f1[0]
            slot_cols[ROWS : 2 * ROWS, cols] = f2[0]
            slot_cols[2 * ROWS : 3 * ROWS, cols] = f1[1]
            slot_cols[3 * ROWS :, cols] = f2[1]
        return dot(back[...], slot_cols[...])

    ahead = SUBSTEPS - 2

    def sum_ahead():
        centre = state[1:2, :]
        state[6:7, :] = centre
        weight = contact[...]
        inverse = 1.0 / mass[...]
        rate = (dt * contact_stiffness) * weight * inverse
        push = dt * rate
        start_vel = based[0] + centre * rate
        start_disp = [disp[0] + dt * start_vel] + [disp[c] + dt * based[c] for c in (1, 2)]
        owned = iota((NODE_ROWS, NB), 0) < OWN
        share = jnp.where(owned, dt * dt * weight * inverse, 0.0)
        slots = to_slots(start_disp + [push, share])
        top, rest = split2(jnp.concatenate(slots[:3], axis=1))
        g0 = dot(jnp.concatenate([top, rest, top], axis=1), kron[:, :NB])
        top, rest = split2(slots[3])
        first_block = jnp.concatenate(
            [kron[k * 3 * NB : k * 3 * NB + NB, :NB] for k in range(3)], axis=0
        )
        g1 = dot(jnp.concatenate([top, rest, top], axis=1), first_block)
        active = (level[...] & ahead) == 0
        scale = slots[4] * modulus[...]
        scale = jnp.where(active, scale, 0.0)
        kept = jnp.where(active, 0.0, slots[4] * held[0])
        terms = [
            kept + scale * (g0 + hardening * g0 * g0 * g0),
            scale * (g1 + 3.0 * hardening * g0 * g0 * g1),
            scale * (3.0 * hardening) * g0 * g1 * g1,
            scale * hardening * g1 * g1 * g1,
        ]
        nodal = [
            jnp.where(
                owned, weight * (start_gap - start_disp[0] - dt * start_vel + push * start_disp[0]), 0.0
            ),
            jnp.where(owned, weight * push * (push - 2.0), 0.0),
        ]
        rows = [jnp.sum(term, axis=0, keepdims=True) for term in terms]
        rows[0] = rows[0] + jnp.sum(nodal[0], axis=0, keepdims=True) + state[5:6, :]
        rows[1] = rows[1] + jnp.sum(nodal[1], axis=0, keepdims=True)
        last_pay[...] = jnp.concatenate(rows, axis=0)
        last_a[spot_a] = last_pay[...]

        @pl.loop(1, size_a)
        def _(k):
            copy(
                last_pay, last_a.at[spot_a], pay_send.at[4], last_recv.at[0],
                peer_a(shifted(spot_a, k, size_a)),
            ).start()

    def relay_last():
        wait_bytes(last_a.at[pl.ds(0, size_a - 1)], last_recv.at[0])
        value = last_a[0]
        for k in range(1, size_a):
            value = value + last_a[k]
        last_b[chip] = value

        @pl.loop(1, chips)
        def _(k):
            copy(
                last_b.at[chip], last_b.at[chip], pay_send.at[5], last_recv.at[1],
                peer_b(shifted(chip, k, chips)),
            ).start()

    def collect_last():
        wait_bytes(last_b.at[pl.ds(0, chips - 1)], last_recv.at[1])
        value = last_b[0]
        for k in range(1, chips):
            value = value + last_b[k]
        total = jnp.sum(value, axis=1, keepdims=True) + jnp.zeros((4, NB), f32)
        shift = state[7:8, :] - state[6:7, :]
        cubic = total[0:1] + shift * (total[1:2] + shift * (total[2:3] + shift * total[3:4]))
        reaction = (
            cubic + (state[1:2, :] - start_gap) * state[3:4, :] - state[0:1, :] * state[4:5, :]
        )
        react[SUBSTEPS - 1 :, :] = reaction / node_total

    def relay(s):
        wait_bytes(buf_a.at[s, pl.ds(0, size_a - 1)], a_recv.at[s])
        value = buf_a[s, 0]
        for k in range(1, size_a):
            value = value + buf_a[s, k]
        buf_b[s, chip] = value

        @pl.loop(1, chips)
        def _(k):
            copy(
                buf_b.at[s, chip], buf_b.at[s, chip], pay_send.at[3], b_recv.at[s],
                peer_b(shifted(chip, k, chips)),
            ).start()

    def collect(s):
        wait_bytes(buf_b.at[s, pl.ds(0, chips - 1)], b_recv.at[s])
        value = buf_b[s, 0]
        for k in range(1, chips):
            value = value + buf_b[s, k]
        total = jnp.sum(value, axis=1, keepdims=True) + zero_row
        before_z = state[0:1, :]
        now_z = state[1:2, :]
        reaction = total + (now_z - start_gap) * state[3:4, :] - before_z * state[4:5, :]
        react[pl.ds(s + 1, 1), :] = reaction / node_total
        speed = state[2:3, :] - dt * contact_stiffness * reaction / impactor_mass
        state[0:1, :] = now_z
        state[1:2, :] = now_z + dt * speed
        state[2:3, :] = speed

    left = (jnp.where(lane == 0, down, r), lax.rem(lane + LANES - 1, LANES))
    right = (jnp.where(lane == LANES - 1, up, r), lax.rem(lane + 1, LANES))

    def halo_copies(turn):
        return [
            copy(
                halo_out.at[turn, side], halo_in.at[turn, 1 - side],
                halo_send.at[turn, side], halo_recv.at[turn, 1 - side], there,
            )
            for side, there in ((0, left), (1, right))
        ]

    def substep(s):
        force = forces(s)
        since = lax.rem(s, DEPTH)
        row_no = iota((NODE_ROWS, NB), 0)
        ext_no = jnp.where(
            row_no < OWN, row_no + DEPTH, jnp.where(row_no < OWN + DEPTH, row_no - OWN, row_no)
        )
        margin = jnp.where(since == DEPTH - 1, 0, 1 + since)
        valid = (ext_no >= margin) & (ext_no < OWN + 2 * DEPTH - margin)
        weight = contact[...]
        inverse = 1.0 / mass[...]
        for c in range(3):
            pull = -force[:, c * NB : (c + 1) * NB]
            if c == 0:
                pull = pull - contact_stiffness * weight * disp[0]
            based[c] = vel[c] + dt * (pull * inverse)
        free = disp[0, own, :] + dt * based[0, own, :]
        part = jnp.sum(contact[own, :] * (start_gap - free), axis=0, keepdims=True)
        pay[s] = part + state[5:6, :]
        buf_a[s, spot_a] = pay[s]

        @pl.when(s < ahead)
        def _():
            @pl.loop(1, size_a)
            def _(k):
                copy(
                    pay.at[s], buf_a.at[s, spot_a], pay_send.at[2], a_recv.at[s],
                    peer_a(shifted(spot_a, k, size_a)),
                ).start()

        @pl.when((s == 2) | (s == 5))
        def _():
            turn = s // DEPTH
            for side, first in ((0, 0), (1, OWN - DEPTH)):
                for c in range(3):
                    halo_out[turn, side, c] = disp[c, first : first + DEPTH, :]
                    halo_out[turn, side, 3 + c] = based[c, first : first + DEPTH, :]
            moves = halo_copies(turn)
            for move in moves:
                move.start()

            @pl.loop(0, 3)
            def _(k):
                relay(s - 2 + k)

            for move in moves:
                move.wait_recv()
            for side, place in ((0, left_row), (1, right_row)):
                for c in range(3):
                    disp[c, place : place + DEPTH, :] = halo_in[turn, side, c]
                    based[c, place : place + DEPTH, :] = halo_in[turn, side, 3 + c]

        @pl.when(s == ahead - 1)
        def _():
            sum_ahead()

        @pl.when(s == 1)
        def _():
            collect_first()

        @pl.when(s >= 2)
        def _():
            collect(s - 2)

        @pl.when(s == ahead - 1)
        def _():
            state[7:8, :] = state[1:2, :]

        z_now = state[1:2, :]
        pushed = (dt * contact_stiffness) * z_now * (weight * inverse)
        for c in range(3):
            fresh = based[c] + pushed if c == 0 else based[c]
            vel[c] = jnp.where(valid, fresh, vel[c])
            disp[c] = jnp.where(valid, disp[c] + dt * fresh, disp[c])

    own_part = pl.ds(pl.multiple_of(lane * (OWN * NB), OWN * NB), OWN * NB)
    other_parts = pl.ds(0, (LANES - 1) * OWN * NB)

    def gather_out(source, ref, slot):
        start = pl.multiple_of(lane * (OWN * NB), OWN * NB)
        for j in range(OWN):
            for c in range(3):
                ref[c : c + 1, pl.ds(start + j * NB, NB)] = source[c, j : j + 1, :]

        for k in FAR_FIRST:
            there = (r, shifted(lane, k, LANES))
            copy(
                ref.at[:, own_part], ref.at[:, own_part], send_sem.at[5 + slot],
                recv_sem.at[4 + slot], there,
            ).start()

    @pl.loop(0, SUBSTEPS)
    def _(s):
        substep(s)

        @pl.when(s == SUBSTEPS - 2)
        def _():
            gather_out(disp, disp_all, 0)

    gather_out(vel, vel_out, 1)
    relay_last()
    wait_bytes(disp_all.at[:, other_parts], recv_sem.at[4])
    for s in range(SUBSTEPS - 1):
        react_out[s] = jnp.max(react[s : s + 1, :])
    wait_bytes(vel_out.at[:, other_parts], recv_sem.at[5])
    disp_out[...] = disp_all[...] + dt * vel_out[...]
    collect_last()
    react_out[SUBSTEPS - 1] = jnp.max(react[SUBSTEPS - 1 :, :])
    flag_out[0] = jnp.max(jnp.where(jnp.abs(react[...]) < jnp.inf, 0, 1))

    edge_up.wait_send()
    edge_down.wait_send()

    @pl.when((lane == 0) | (lane == LANES - 1))
    def _():
        rim_up.wait_send()

    order_up.wait_send()
    order_down.wait_send()
    for turn in range(2):
        for move in halo_copies(turn):
            move.wait_send()
    wait_bytes(pack_in.at[pl.ds(0, LANES - 1)], send_sem.at[3])
    wait_bytes(order_in.at[pl.ds(0, LANES - 1)], send_sem.at[4])
    wait_bytes(disp_all.at[:, other_parts], send_sem.at[5])
    wait_bytes(vel_out.at[:, other_parts], send_sem.at[6])
    wait_bytes(first_a.at[pl.ds(0, size_a - 1)], pay_send.at[0])
    wait_bytes(first_b.at[pl.ds(0, chips - 1)], pay_send.at[1])
    wait_bytes(buf_a.at[pl.ds(0, ahead), pl.ds(0, size_a - 1)], pay_send.at[2])
    wait_bytes(buf_b.at[pl.ds(0, ahead), pl.ds(0, chips - 1)], pay_send.at[3])
    wait_bytes(last_a.at[pl.ds(0, size_a - 1)], pay_send.at[4])
    wait_bytes(last_b.at[pl.ds(0, chips - 1)], pay_send.at[5])


def run_cycle(regions, init_disp, init_vel, mass, contact, modulus, stiffness, levels, windows, conn):
    chips = regions // 2
    vmem = pl.BlockSpec(memory_space=pltpu.VMEM)
    V = pltpu.VMEM
    vel, disp, react, flag = pl.pallas_call(
        functools.partial(cycle_kernel, regions),
        out_shape=(
            jax.ShapeDtypeStruct(init_vel.shape, f32),
            jax.ShapeDtypeStruct(init_disp.shape, f32),
            jax.ShapeDtypeStruct((SUBSTEPS,), f32),
            jax.ShapeDtypeStruct((1,), i32),
        ),
        in_specs=[pl.BlockSpec(memory_space=pltpu.HBM)] * 5
        + [vmem]
        + [pl.BlockSpec(memory_space=pltpu.HBM)] * 3,
        out_specs=[vmem] * 2 + [pl.BlockSpec(memory_space=pltpu.SMEM)] * 2,
        scratch_shapes=[
            V(init_disp.shape, f32), V(init_vel.shape, f32), V((LANES * OWN, NB), f32),
            V((LANES * OWN, NB), f32), V((16, 64), f32), V((24, 24), f32),
            V((1, 64), i32), V((1, 64), i32), V((64, NB), i32),
            V((LANES, PACK + 8, NB), f32), V((LANES, PACK + 8, NB), f32),
            V((2, EDGE + 8, NB), f32), V((LANES, EDGE + 8, NB), f32),
            V((LANES, PACK, NB), f32), V((LANES, PACK, NB), f32),
            V((2, EDGE, NB), f32), V((LANES, EDGE, NB), f32),
            V((8, DEPTH, NB), f32), V((8, DEPTH, NB), f32),
            V((2, 2, 6, DEPTH, NB), f32), V((2, 2, 6, DEPTH, NB), f32),
            V((3, NB), f32), V((2 * LANES, 3, NB), f32), V((chips, 3, NB), f32),
            V((SUBSTEPS, 1, NB), f32), V((SUBSTEPS, 2 * LANES, 1, NB), f32),
            V((SUBSTEPS, chips, 1, NB), f32),
            V((4, NB), f32), V((2 * LANES, 4, NB), f32), V((chips, 4, NB), f32),
            V((SUBSTEPS, NB), f32), V(init_disp.shape, f32),
            V((3, NODE_ROWS, NB), f32), V((3, NODE_ROWS, NB), f32), V((3, NODE_ROWS, NB), f32),
            V((NODE_ROWS, NB), f32), V((NODE_ROWS, NB), f32),
            V((NB, 5 * NB), bf16), V((4 * ROWS, 3 * NB), bf16),
            V((9 * NB, 3 * NB), bf16), V((2 * NB, NB), bf16),
            V((2 * ROWS, NB), bf16), V((NODE_ROWS, 4 * ROWS), bf16),
            V((ROWS, LANES * (PACK + EDGE)), bf16),
            V((LANES * (PACK + EDGE), LANES * (PACK + EDGE)), bf16),
            V((ROWS, NB), i32), V((ROWS, NB), i32), V((ROWS, NB), i32),
            V((ROWS, NB), i32), V((ROWS, NB), i32),
            V((ROWS, NB), f32), V((ROWS, NB), i32), V((3, ROWS, NB), f32), V((8, NB), f32),
            pltpu.SemaphoreType.DMA((9,)), pltpu.SemaphoreType.DMA((7,)),
            pltpu.SemaphoreType.DMA((6,)), pltpu.SemaphoreType.DMA((2,)),
            pltpu.SemaphoreType.DMA((SUBSTEPS,)), pltpu.SemaphoreType.DMA((SUBSTEPS,)),
            pltpu.SemaphoreType.DMA((9,)),
            pltpu.SemaphoreType.DMA((2, 2)), pltpu.SemaphoreType.DMA((2, 2)),
            pltpu.SemaphoreType.DMA((2,)), pltpu.SemaphoreType.REGULAR,
        ],
        compiler_params=pltpu.CompilerParams(
            collective_id=0, has_side_effects=True, vmem_limit_bytes=48 * 1024 * 1024
        ),
        name="crush_cycle",
    )(
        init_disp, init_vel, mass.reshape(-1, NB), contact.reshape(-1, NB), modulus.T, stiffness,
        levels.reshape(1, -1), windows.reshape(1, -1), conn,
    )
    return (disp, vel, react), flag[0]


def hand_over(disp_in, vel_in, react_in, disp_out, vel_out, react_out):
    disp_out[...] = disp_in[...]
    vel_out[...] = vel_in[...]
    for s in range(SUBSTEPS):
        react_out[s] = react_in[s]


def finish(results):
    vmem = pl.BlockSpec(memory_space=pltpu.VMEM)
    smem = pl.BlockSpec(memory_space=pltpu.SMEM)
    return pl.pallas_call(
        hand_over,
        out_shape=tuple(jax.ShapeDtypeStruct(x.shape, f32) for x in results),
        in_specs=[vmem, vmem, smem],
        out_specs=(vmem, vmem, smem),
        name="hand_over",
    )(*results)


def sum_over(value, axis):
    count = lax.axis_size(axis)
    step = 1
    while step < count:
        value = value + lax.ppermute(value, axis, [(i, i ^ step) for i in range(count)])
        step *= 2
    return value


def with_halo(array, sides, width):
    for axis, dim in sides:
        count, length = (lax.axis_size(axis), array.shape[dim])
        up = [(i, (i + 1) % count) for i in range(count)]
        down = [(j, i) for i, j in up]
        last = lax.slice_in_dim(array, length - width, length, axis=dim)
        initial = lax.slice_in_dim(array, 0, width, axis=dim)
        before = lax.ppermute(last, axis, up)
        after = lax.ppermute(initial, axis, down)
        array = jnp.concatenate([before, array, after], axis=dim)
    return array


def element_forces(slot_disp, block_modulus, stiffness):
    count = slot_disp.shape[0]
    elements = block_modulus.shape[1]
    vectors = (
        slot_disp.reshape(count, 3, elements, 8).transpose(0, 2, 1, 3).reshape(count, elements, 24)
    )
    strain = jnp.einsum("bek,jk->bej", vectors, stiffness, precision=lax.Precision.HIGHEST)
    result = block_modulus[:, :, None] * (strain + hardening * strain * strain * strain)
    return (
        result.reshape(count, elements, 3, 8).transpose(0, 2, 1, 3).reshape(count, 3, elements * 8)
    )


def plain_cycle(init_disp, init_vel, mass, contact, modulus, stiffness, levels, windows, conn):
    region_count = lax.axis_size("region")
    node_region = init_disp.shape[1]
    slot_count = conn.shape[1]
    block_rows = NB
    node_total = node_region * region_count
    impactor_mass = impactor_ratio * node_total
    extended_blocks = node_region // block_rows + 2
    block_order = jnp.argsort(levels, stable=True)
    conn = conn[block_order]
    windows = windows[block_order]
    levels = levels[block_order]
    modulus = modulus[block_order]
    level_slot = (
        (levels >= 2).astype(jnp.int32)
        + (levels >= 4).astype(jnp.int32)
        + (levels >= 8).astype(jnp.int32)
    )
    level_force = jnp.zeros((4, 3, extended_blocks, block_rows), jnp.float32)
    disp_full = init_disp
    disp_state = init_disp
    vel_state = init_vel
    gap_now = jnp.float32(start_gap)
    speed = jnp.float32(start_speed)
    history = []
    slot_iota = lax.broadcasted_iota(jnp.int32, (group_size, 2 * block_rows, slot_count), 1)
    for substep in range(SUBSTEPS):
        top_level = SUBSTEPS if substep == 0 else min(substep & -substep, SUBSTEPS)
        top_index = top_level.bit_length() - 1
        active_count = jnp.sum((levels <= top_level).astype(jnp.int32))
        level_force = level_force.at[: top_index + 1].set(0.0)
        disp_ext = with_halo(disp_full, (("region", 1),), block_rows)

        def one_group(group_index, totals):
            offset = group_index * group_size
            conn_group = lax.dynamic_slice_in_dim(conn, offset, group_size, 0)
            window_group = lax.dynamic_slice_in_dim(windows, offset, group_size, 0)
            level_group = lax.dynamic_slice_in_dim(level_slot, offset, group_size, 0)
            modulus_group = lax.dynamic_slice_in_dim(modulus, offset, group_size, 0)
            valid = offset + jnp.arange(group_size, dtype=jnp.int32) < active_count
            window_disp = jax.vmap(
                lambda first_block: lax.dynamic_slice_in_dim(
                    disp_ext, first_block * block_rows, 2 * block_rows, 1
                )
            )(window_group)
            onehot = (slot_iota == conn_group[:, None, :]).astype(jnp.float32)
            slot_disp = jnp.einsum(
                "gcw,gws->gcs", window_disp, onehot, precision=lax.Precision.HIGHEST
            )
            slot_force = element_forces(slot_disp, modulus_group, stiffness)
            slot_force = jnp.where(valid[:, None, None], slot_force, 0.0)
            window_force = jnp.einsum(
                "gcs,gws->gcw", slot_force, onehot, precision=lax.Precision.HIGHEST
            )
            window_force = window_force.reshape(group_size, 3, 2, block_rows)
            totals = totals.at[level_group, :, window_group].add(window_force[:, :, 0])
            totals = totals.at[level_group, :, window_group + 1].add(window_force[:, :, 1])
            return totals

        group_total = (active_count + group_size - 1) // group_size
        level_force = lax.fori_loop(0, group_total, one_group, level_force)
        force_ext = jnp.sum(level_force, axis=0).reshape(3, extended_blocks * block_rows)
        outer_rims = jnp.concatenate(
            (force_ext[:, :block_rows], force_ext[:, -block_rows:]), axis=1
        )
        rim_terms = with_halo(outer_rims, (("region", 1),), block_rows)
        partial_force = force_ext[:, block_rows:-block_rows]
        partial_force = partial_force.at[:, :block_rows].add(rim_terms[:, :block_rows])
        partial_force = partial_force.at[:, -block_rows:].add(rim_terms[:, -block_rows:])
        force = sum_over(partial_force, "lane")
        disp_state = disp_full
        gap = gap_now - disp_state[0]
        total = sum_over(jnp.sum(contact * gap), "region")
        history.append(total / node_total)
        push = jnp.zeros_like(force).at[0].set(contact_stiffness * contact * gap)
        accel = (push - force) / mass[None, :]
        vel_state = vel_state + time_step * accel
        disp_state = disp_state + time_step * vel_state
        speed = speed - time_step * contact_stiffness * total / impactor_mass
        gap_now = gap_now + time_step * speed
        disp_full = disp_state
    return (disp_full, vel_state, jnp.stack(history))


def on_device(*arguments):
    regions = lax.axis_size("region")
    fast, flag = run_cycle(regions, *arguments)
    return finish(lax.cond(flag == 0, lambda: fast, lambda: plain_cycle(*arguments)))


def solution(mesh):
    in_specs = (
        P(None, "region"),
        P(None, "region"),
        P("region"),
        P("region"),
        P(("region", "lane"), None),
        P(),
        P(("region", "lane")),
        P(("region", "lane")),
        P(("region", "lane"), None),
    )
    out_specs = (P(None, "region"), P(None, "region"), P())
    return jax.shard_map(
        on_device, mesh=mesh, in_specs=in_specs, out_specs=out_specs, check_vma=False
    )
```

```python
import functools

import jax
import jax.numpy as jnp
from jax import lax
from jax.experimental import pallas as pl
from jax.experimental.pallas import tpu as pltpu
from jax.sharding import PartitionSpec as P

NB = 128
SUBSTEPS = 8
LANES = 8
FAR_FIRST = (4, 3, 5, 2, 6, 1, 7)
OWN = 8
DEPTH = 3
NODE_ROWS = 16
ANCHORS = OWN - 1 + 2 * DEPTH
ROWS = 160
PACK = 32
EDGE = 16

time_step = 0.05
contact_stiffness = 1.0
hardening = 2.0
impactor_ratio = 0.05
start_gap = 1.0
start_speed = 1.0
group_size = 8

f32, bf16, i32 = jnp.float32, jnp.bfloat16, jnp.int32


def iota(shape, dim):
    return lax.broadcasted_iota(i32, shape, dim)


def dot(a, b):
    return jnp.dot(a, b, preferred_element_type=f32)


def dot_t(a, b):
    return lax.dot_general(a, b, (((1,), (1,)), ((), ())), preferred_element_type=f32)


def split2(value):
    high = value.astype(bf16)
    return high, (value - high.astype(f32)).astype(bf16)


def split3(value):
    high = value.astype(bf16)
    rest = value - high.astype(f32)
    middle = rest.astype(bf16)
    return high, middle, (rest - middle.astype(f32)).astype(bf16)


def take(value, index):
    return jnp.take_along_axis(value, index, axis=1, mode="promise_in_bounds")


def row_of(ext):
    return jnp.where(ext < DEPTH, ext + OWN, jnp.where(ext < DEPTH + OWN, ext - DEPTH, ext))


def tree_sum(values):
    values = list(values)
    while len(values) > 1:
        pairs = [a + b for a, b in zip(values[::2], values[1::2])]
        values = pairs + values[len(pairs) * 2 :]
    return values[0]


def onehot(mask):
    return jnp.where(mask, 1.0, 0.0).astype(bf16)


def cycle_kernel(
    regions,
    disp_far, vel_far, mass_far, contact_far, modulus_far, stiff_far, level_far, window_far, conn_far,
    vel_out, disp_out, react_out, flag_out,
    disp_in, vel_in, mass_in, contact_in, modulus_in, stiff_in, level_in, window_in, conn_in,
    pack_out, pack_in, edge_out, edge_in, order_out, order_in, order_edge_out, order_edge_in,
    rim_out, rim_in, halo_out, halo_in,
    first_pay, first_a, first_b, pay, buf_a, buf_b, last_pay, last_a, last_b, react, disp_all,
    disp, vel, based, mass, contact, table, slot_cols, kron, tri,
    wab, back, keep_rows, strict, conn_idx, half, perm, end1, end2, modulus, level, held, state,
    send_sem, recv_sem, pay_send, first_recv, a_recv, b_recv, load_sem, halo_send, halo_recv, last_recv, vouch,
):
    r = lax.axis_index("region")
    lane = lax.axis_index("lane")
    core = lax.rem(r, 2)
    chip = r // 2
    chips = regions // 2
    up = lax.rem(r + 1, regions)
    down = lax.rem(r + regions - 1, regions)
    size_a = 2 * LANES
    spot_a = lane * 2 + core
    dt = time_step
    node_total = regions * LANES * OWN * NB
    impactor_mass = impactor_ratio * node_total

    def peer_b(k):
        return (k * 2 + core, lane)

    deep = min(chips, LANES)
    wide = chips // deep

    def ring(step, size):
        return min(step, size - step)

    steps_a = sorted(
        ((y, c) for y in range(LANES) for c in range(2) if y or c),
        key=lambda step: (-ring(step[0], LANES), step),
    )
    steps_b = sorted(
        ((x, z) for x in range(wide) for z in range(deep) if x or z),
        key=lambda step: (-ring(step[0], wide) - ring(step[1], deep), step),
    )

    def members_a():
        for y, c in steps_a:
            yield (chip * 2 + lax.rem(core + c, 2), lax.rem(lane + y, LANES))

    def members_b():
        for x, z in steps_b:
            yield peer_b(
                lax.rem(chip // deep + x, wide) * deep + lax.rem(lax.rem(chip, deep) + z, deep)
            )

    def signal(device):
        pl.semaphore_signal(
            pltpu.get_barrier_semaphore(), inc=1, device_id=device,
            device_id_type=pl.DeviceIdType.MESH,
        )

    def shifted(spot, step, size):
        return lax.rem(spot + step, size)

    for there in members_a():
        signal(there)

    def along_x(k):
        return peer_b(lax.rem(chip // deep + k, wide) * deep + lax.rem(chip, deep))

    def along_z(k):
        return peer_b((chip // deep) * deep + lax.rem(chip + k, deep))

    for k in range(1, deep):
        signal(along_z(k))
    for k in range(1, wide):
        signal(along_x(k))

    @pl.when(lane == 0)
    def _():
        @pl.loop(0, LANES)
        def _(j):
            signal((down, j))

    @pl.when(lane == LANES - 1)
    def _():
        @pl.loop(0, LANES)
        def _(j):
            signal((up, j))

    def copy(src, dst, send, recv, device):
        return pltpu.make_async_remote_copy(
            src_ref=src, dst_ref=dst, send_sem=send, recv_sem=recv,
            device_id=device, device_id_type=pl.DeviceIdType.MESH,
        )

    def wait_bytes(ref, sem):
        pltpu.make_async_copy(ref, ref, sem).wait()

    loads = []
    for k, (far, here) in enumerate((
        (level_far, level_in), (window_far, window_in), (modulus_far, modulus_in),
        (conn_far, conn_in), (contact_far, contact_in), (mass_far, mass_in),
        (disp_far, disp_in), (vel_far, vel_in), (stiff_far, stiff_in),
    )):
        loads.append(pltpu.make_async_copy(far, here, load_sem.at[k]))
        loads[-1].start()
    for load in loads:
        load.wait()

    level_row = level_in[...].astype(f32)
    window_row = window_in[...].astype(f32)
    dest = iota((16, 64), 0)
    offsets = jnp.where(
        dest < LANES, (DEPTH - 1) - OWN * dest,
        jnp.where(dest == LANES, DEPTH - 1 - OWN * LANES, OWN + DEPTH - 1),
    ).astype(f32)
    anchor_all = window_row + offsets
    lowest = jnp.where(dest == LANES + 1, OWN + DEPTH - 1, 0).astype(f32)
    highest = jnp.where(dest == LANES, DEPTH - 1, ANCHORS - 1).astype(f32)
    wanted = jnp.where(
        (anchor_all >= lowest) & (anchor_all <= highest) & (dest < LANES + 2), 1.0, 0.0
    )
    before = onehot(iota((64, 64), 0) < iota((64, 64), 1))
    rank_key = jnp.where(wanted > 0.0, dot(wanted.astype(bf16), before), -1.0)
    count = jnp.sum(wanted, axis=1, keepdims=True)
    room = jnp.where(iota((16, 1), 0) < LANES, PACK, EDGE).astype(f32)
    overflow = jnp.max(jnp.where(count > room, 1.0, 0.0), axis=0, keepdims=True)
    picks = [
        onehot(iota((PACK, 64), 0).astype(f32) == rank_key[k : k + 1, :]) for k in range(LANES)
    ] + [
        onehot(iota((EDGE, 64), 0).astype(f32) == rank_key[k : k + 1, :])
        for k in (LANES, LANES + 1)
    ]
    pick = jnp.concatenate(picks, axis=0)
    conn_f = conn_in[...].astype(f32)
    picked = LANES * PACK + 2 * EDGE
    tiled = jnp.concatenate([modulus_in[...]] * 8, axis=0)
    chosen = sum(dot_t(pick, part) for part in split3(tiled))
    chosen = jnp.where(
        (iota((picked, NB), 0) & 7) == iota((picked, NB), 1) // 16, chosen, 0.0
    )
    grouped = jnp.sum(chosen.reshape(picked // 8, 8, NB), axis=1)
    facts = jnp.concatenate(
        [level_row, window_row, jnp.ones((1, 64), f32), jnp.zeros((5, 64), f32)], axis=0
    ).astype(bf16)
    chosen_conn = dot(pick, conn_f.astype(bf16))
    spot = iota((NB, 64), 0).astype(f32)

    def lane_rows(k, start, offset):
        key = jnp.where(rank_key[k : k + 1, :] >= 0.0, rank_key[k : k + 1, :] + start, -1.0)
        found = dot_t(facts, onehot(spot == key))
        return jnp.concatenate(
            [found[0:1, :], found[1:2, :] + float(offset) * found[2:3, :], jnp.zeros((2, NB), f32)],
            axis=0,
        )

    quarter = (PACK * lax.rem(lane, 4)).astype(f32)
    eighth = (EDGE * lane).astype(f32)
    for k in range(LANES):
        pack_out[k, :PACK, :] = chosen_conn[k * PACK : (k + 1) * PACK, :]
        pack_out[k, PACK : PACK + 4, :] = grouped[4 * k : 4 * k + 4, :]
        pack_out[k, PACK + 4 :, :] = lane_rows(k, quarter, DEPTH - 1 - OWN * k)
    for k, offset in ((0, DEPTH - 1 - OWN * LANES), (1, OWN + DEPTH - 1)):
        start = LANES * PACK + k * EDGE
        edge_out[k, :EDGE, :] = chosen_conn[start : start + EDGE, :]
        edge_out[k, EDGE : EDGE + 4, :] = jnp.concatenate(
            [grouped[start // 8 : start // 8 + 2, :], jnp.zeros((2, NB), f32)], axis=0
        )
        edge_out[k, EDGE + 4 :, :] = lane_rows(LANES + k, eighth, offset)

    def load_nodes(place, source_lane, first, number):
        start = pl.multiple_of(source_lane * (OWN * NB), OWN * NB)
        for j in range(number):
            part = pl.ds(start + (first + j) * NB, NB)
            for c in range(3):
                disp[c, place + j : place + j + 1, :] = disp_in[c : c + 1, part]
                vel[c, place + j : place + j + 1, :] = vel_in[c : c + 1, part]
        rows = pl.ds(pl.multiple_of(source_lane * OWN, OWN), OWN)
        mass[place : place + number, :] = mass_in[rows, :][first : first + number, :]
        contact[place : place + number, :] = contact_in[rows, :][first : first + number, :]

    left_row, right_row = OWN, OWN + DEPTH
    disp[...] = jnp.zeros_like(disp)
    vel[...] = jnp.zeros_like(vel)
    mass[...] = jnp.ones_like(mass)
    contact[...] = jnp.zeros_like(contact)
    load_nodes(0, lane, 0, OWN)

    own = pl.ds(0, OWN)
    own_contact = contact[own, :]
    own_mass = mass[own, :]
    push_rate = (dt * dt * contact_stiffness) * own_contact / own_mass
    sums = [
        jnp.sum(own_contact * (start_gap - disp[0, own, :]), axis=0, keepdims=True),
        jnp.sum(own_contact, axis=0, keepdims=True),
        jnp.sum(own_contact * push_rate, axis=0, keepdims=True),
    ]
    first_pay[...] = jnp.concatenate(sums, axis=0)
    first_a[spot_a] = first_pay[...]

    pl.semaphore_wait(pltpu.get_barrier_semaphore(), size_a - 1 + deep - 1 + wide - 1 + 2)
    for k in range(1, wide):
        pl.semaphore_signal(
            vouch, inc=1, device_id=along_x(k), device_id_type=pl.DeviceIdType.MESH
        )

    for there in members_a():
        copy(
            first_pay, first_a.at[spot_a], pay_send.at[0], first_recv.at[0], there
        ).start()

    edge_up = copy(edge_out.at[0], edge_in.at[lane], send_sem.at[0], recv_sem.at[0], (up, 0))
    edge_down = copy(
        edge_out.at[1], edge_in.at[lane], send_sem.at[1], recv_sem.at[0], (down, LANES - 1)
    )
    edge_up.start()
    edge_down.start()

    for k in FAR_FIRST:
        there = shifted(lane, k, LANES)
        copy(
            pack_out.at[there], pack_in.at[lane], send_sem.at[3], recv_sem.at[2], (r, there)
        ).start()

    def load_rim(rim_lane, first):
        for j in range(DEPTH):
            at = (rim_lane * OWN + first + j) * NB
            part = slice(at, at + NB)
            for c in range(3):
                rim_out[c, j : j + 1, :] = disp_in[c : c + 1, part]
                rim_out[3 + c, j : j + 1, :] = vel_in[c : c + 1, part]
        rows = slice(rim_lane * OWN + first, rim_lane * OWN + first + DEPTH)
        rim_out[6, :, :] = mass_in[rows, :]
        rim_out[7, :, :] = contact_in[rows, :]

    @pl.when(lane == 0)
    def _():
        load_rim(LANES - 1, OWN - DEPTH)

    @pl.when(lane == LANES - 1)
    def _():
        load_rim(0, 0)

    rim_up = copy(rim_out, rim_in, send_sem.at[2], recv_sem.at[1], (up, 0))
    rim_down = copy(rim_out, rim_in, send_sem.at[2], recv_sem.at[1], (down, LANES - 1))

    @pl.when(lane == 0)
    def _():
        rim_up.start()

    @pl.when(lane == LANES - 1)
    def _():
        rim_down.start()

    pack_in[lane] = pack_out[lane]
    load_nodes(left_row, jnp.maximum(lane - 1, 0), OWN - DEPTH, DEPTH)
    load_nodes(right_row, jnp.minimum(lane + 1, LANES - 1), 0, DEPTH)

    lane64 = iota((64, NB), 1)
    keys = conn_f * float(NB) + lane64.astype(f32)
    span = 2
    while span <= NB:
        step = span // 2
        while step >= 1:
            other = take(keys, lane64 ^ step)
            keep_low = ((lane64 & step) == 0) == ((lane64 & span) == 0)
            keys = jnp.where(keep_low, jnp.minimum(keys, other), jnp.maximum(keys, other))
            step //= 2
        span *= 2
    order = (keys.astype(i32) & (NB - 1)).astype(f32)
    chosen_order = dot(pick, order.astype(bf16))
    for k in range(LANES):
        order_out[k] = chosen_order[k * PACK : (k + 1) * PACK, :]
    for k in range(2):
        start = LANES * PACK + k * EDGE
        order_edge_out[k] = chosen_order[start : start + EDGE, :]
    order_up = copy(
        order_edge_out.at[0], order_edge_in.at[lane], send_sem.at[7], recv_sem.at[6], (up, 0)
    )
    order_down = copy(
        order_edge_out.at[1], order_edge_in.at[lane], send_sem.at[8], recv_sem.at[6],
        (down, LANES - 1),
    )
    order_up.start()
    order_down.start()

    for k in FAR_FIRST:
        there = shifted(lane, k, LANES)
        copy(
            order_out.at[there], order_in.at[lane], send_sem.at[4], recv_sem.at[3], (r, there)
        ).start()

    order_in[lane] = order_out[lane]

    offered = LANES * (PACK + EDGE)
    strict[...] = onehot(iota((offered, offered), 0) < iota((offered, offered), 1))
    stiff = split2(stiff_in[...])
    at = iota((3 * NB, 24), 0)
    names = onehot((at // NB) * 8 + lax.rem(at, 8) == iota((3 * NB, 24), 1))
    row_element = lax.rem(iota((3 * NB, 3 * NB), 0), NB) // 8
    col_element = lax.rem(iota((3 * NB, 3 * NB), 1), NB) // 8
    same = row_element == col_element
    for part, places in ((stiff[0], (0, 1)), (stiff[1], (2,))):
        grown = dot_t(dot_t(names, part).astype(bf16), names)
        grown = jnp.where(same, grown, 0.0).astype(bf16)
        for at_place in places:
            kron[at_place * 3 * NB : (at_place + 1) * 3 * NB, :] = grown
    running = onehot(iota((NB, NB), 0) <= iota((NB, NB), 1))
    tri[0:NB, :] = running
    tri[NB:, :] = running

    @pl.when((lane != 0) & (lane != LANES - 1))
    def _():
        edge_in[...] = jnp.zeros_like(edge_in)
        order_edge_in[...] = jnp.zeros_like(order_edge_in)

    if wide > 1:
        pl.semaphore_wait(vouch, wide - 1)
    wait_bytes(first_a.at[pl.ds(0, size_a - 1)], first_recv.at[0])
    total = tree_sum(first_a[k] for k in range(size_a))
    first_b[chip] = total
    first_pay2 = first_b.at[chip]

    for there in members_b():
        copy(
            first_pay2, first_b.at[chip], pay_send.at[1], first_recv.at[1], there
        ).start()

    @pl.when((lane == 0) | (lane == LANES - 1))
    def _():
        wait_bytes(edge_in, recv_sem.at[0])
        wait_bytes(rim_in, recv_sem.at[1])

    def unpack_rim(place):
        for c in range(3):
            disp[c, place : place + DEPTH, :] = rim_in[c]
            vel[c, place : place + DEPTH, :] = rim_in[3 + c]
        mass[place : place + DEPTH, :] = rim_in[6]
        contact[place : place + DEPTH, :] = rim_in[7]

    @pl.when(lane == 0)
    def _():
        unpack_rim(left_row)

    @pl.when(lane == LANES - 1)
    def _():
        unpack_rim(right_row)

    wait_bytes(pack_in.at[pl.ds(0, LANES - 1)], recv_sem.at[2])

    conn_rows = jnp.concatenate(
        [pack_in[j, :PACK, :] for j in range(LANES)] + [edge_in[j, :EDGE, :] for j in range(LANES)],
        axis=0,
    )
    shared = jnp.concatenate(
        [pack_in[j, PACK : PACK + 4, :] for j in range(LANES)]
        + [edge_in[j, EDGE : EDGE + 2, :] for j in range(LANES)],
        axis=0,
    )
    shared = jnp.broadcast_to(shared[:, None, :], (offered // 8, 8, NB)).reshape(offered, NB)
    moduli = take(shared, 16 * (iota((offered, NB), 0) & 7) + iota((offered, NB), 1) // 8)
    facts_in = jnp.concatenate(
        [
            sum(pack_in[j, PACK + 4 :, :] for j in range(4)),
            sum(pack_in[j, PACK + 4 :, :] for j in range(4, LANES)),
            sum(edge_in[j, EDGE + 4 :, :] for j in range(LANES)),
        ],
        axis=1,
    )
    levels_in = facts_in[0:1, :]
    anchors_in = facts_in[1:2, :]
    present = jnp.where(levels_in > 0.0, 1.0, 0.0) + jnp.zeros((8, offered), f32)
    key = jnp.where(present > 0.0, dot(present.astype(bf16), strict[...]), -1.0)[0:1, :]
    taken = jnp.sum(present[0:1, :], axis=1, keepdims=True)
    overflow = jnp.maximum(overflow, jnp.where(taken > float(ROWS), 1.0, 0.0))
    keep = onehot(iota((ROWS, offered), 0).astype(f32) == key)
    conn = dot(keep, conn_rows.astype(bf16))
    moduli_parts = split3(moduli)
    modulus[...] = sum(dot(keep, part) for part in moduli_parts)
    wide_levels = (levels_in + jnp.zeros((NB, offered), f32)).astype(bf16)
    wide_anchors = (anchors_in + jnp.zeros((NB, offered), f32)).astype(bf16)

    lane_no = iota((ROWS, NB), 1)
    level[...] = dot_t(keep, wide_levels).astype(i32) - 1
    anchor = dot_t(keep, wide_anchors).astype(i32)
    wab[:ROWS, :] = onehot((lane_no & 31) == row_of(anchor))
    wab[ROWS:, :] = onehot((lane_no & 31) == row_of(anchor + 1))
    anchor_row = dot_t(wide_anchors[:8, :], keep)[0:1, :].astype(i32)
    node_row = iota((NODE_ROWS, ROWS), 0)
    back_a = onehot(node_row == row_of(anchor_row))
    back_b = onehot(node_row == row_of(anchor_row + 1))
    back[...] = jnp.concatenate([back_a, back_b, back_a, back_b], axis=1)
    conn_i = conn.astype(i32)
    conn_idx[...] = conn_i & (NB - 1)
    half[...] = conn_i >> 7

    keep_rows[...] = keep
    held[...] = jnp.zeros_like(held)
    table[...] = jnp.zeros_like(table)

    zero_row = jnp.zeros((1, NB), f32)
    state[0:1, :] = zero_row + start_gap
    state[1:2, :] = zero_row + start_gap
    state[5:6, :] = jnp.where(overflow > 0.0, jnp.inf, 0.0) + zero_row

    def collect_first():
        wait_bytes(first_b.at[pl.ds(0, chips - 1)], first_recv.at[1])
        total = tree_sum(first_b[k] for k in range(chips))
        first = jnp.sum(total, axis=1, keepdims=True)
        reaction = first[0:1, :] + zero_row
        speed = start_speed - dt * contact_stiffness * reaction / impactor_mass
        state[1:2, :] = start_gap + dt * speed
        state[2:3, :] = speed
        state[3:4, :] = first[1:2, :] + zero_row
        state[4:5, :] = first[2:3, :] + zero_row
        react[0:1, :] = reaction / node_total

    first_lane = iota((ROWS, NB), 1) == 0

    def to_slots(fields):
        width = len(fields) * NB
        parts = [split3(field) for field in fields]
        for k in range(3):
            table[32 * k : 32 * k + NODE_ROWS, :width] = jnp.concatenate(
                [part[k] for part in parts], axis=1
            )
        both = dot(wab[...], table[:, :width])
        index = conn_idx[...]
        second = half[...] > 0
        slots = []
        for c in range(len(fields)):
            cols = slice(c * NB, (c + 1) * NB)
            slots.append(
                jnp.where(second, take(both[ROWS:, cols], index), take(both[:ROWS, cols], index))
            )
        return slots

    def receive_order():
        lane_no = iota((ROWS, NB), 1)

        @pl.when((lane == 0) | (lane == LANES - 1))
        def _():
            wait_bytes(order_edge_in, recv_sem.at[6])

        wait_bytes(order_in.at[pl.ds(0, LANES - 1)], recv_sem.at[3])
        order_rows = jnp.concatenate(
            [
                order_in[...].reshape(LANES * PACK, NB),
                order_edge_in[...].reshape(LANES * EDGE, NB),
            ],
            axis=0,
        )
        order = dot(keep_rows[...], order_rows.astype(bf16)).astype(i32)
        perm[...] = order
        nodes = take(half[...] * NB + conn_idx[...], order)
        for ref, base in ((end1, 0), (end2, NB)):
            target = lane_no + base
            found = jnp.zeros((ROWS, NB), i32)
            for step in (64, 32, 16, 8, 4, 2, 1, 0):
                probe = take(nodes, found + (step - 1 if step else 0))
                found = jnp.where(probe <= target, found + max(step, 1), found)
            ref[...] = found - 1

    def forces(s):
        top, rest = split2(jnp.concatenate(to_slots([disp[c] for c in range(3)]), axis=1))
        strain = dot(jnp.concatenate([top, rest, top], axis=1), kron[...])
        active = (level[...] & s) == 0
        mod = modulus[...]
        for c in range(3):
            g = strain[:, c * NB : (c + 1) * NB]
            fresh = mod * (g + hardening * g * g * g)
            held[c] = jnp.where(active, fresh, held[c])

        @pl.when(s == 0)
        def _():
            receive_order()

        order = perm[...]
        sorted_forces = []
        for c in range(3):
            sorted_forces.append(jnp.concatenate(split2(take(held[c], order)), axis=1))
        sums = dot(jnp.concatenate(sorted_forces, axis=0), tri[...])
        e1 = end1[...]
        e2 = end2[...]
        for c in range(3):
            part = sums[c * ROWS : (c + 1) * ROWS, :]
            upto1 = jnp.where(e1 >= 0, take(part, e1 & (NB - 1)), 0.0)
            upto2 = jnp.where(e2 >= 0, take(part, e2 & (NB - 1)), 0.0)
            prev1 = pltpu.roll(upto1, 1, 1)
            prev2 = pltpu.roll(upto2, 1, 1)
            f1 = split2(upto1 - jnp.where(first_lane, 0.0, prev1))
            f2 = split2(upto2 - jnp.where(first_lane, prev1, prev2))
            cols = slice(c * NB, (c + 1) * NB)
            slot_cols[0:ROWS, cols] = f1[0]
            slot_cols[ROWS : 2 * ROWS, cols] = f2[0]
            slot_cols[2 * ROWS : 3 * ROWS, cols] = f1[1]
            slot_cols[3 * ROWS :, cols] = f2[1]
        return dot(back[...], slot_cols[...])

    ahead = SUBSTEPS - 2

    def sum_ahead():
        centre = state[1:2, :]
        state[6:7, :] = centre
        weight = contact[...]
        inverse = 1.0 / mass[...]
        rate = (dt * contact_stiffness) * weight * inverse
        push = dt * rate
        start_vel = based[0] + centre * rate
        start_disp = [disp[0] + dt * start_vel] + [disp[c] + dt * based[c] for c in (1, 2)]
        owned = iota((NODE_ROWS, NB), 0) < OWN
        share = jnp.where(owned, dt * dt * weight * inverse, 0.0)
        slots = to_slots(start_disp + [push, share])
        top, rest = split2(jnp.concatenate(slots[:3], axis=1))
        g0 = dot(jnp.concatenate([top, rest, top], axis=1), kron[:, :NB])
        top, rest = split2(slots[3])
        first_block = jnp.concatenate(
            [kron[k * 3 * NB : k * 3 * NB + NB, :NB] for k in range(3)], axis=0
        )
        g1 = dot(jnp.concatenate([top, rest, top], axis=1), first_block)
        active = (level[...] & ahead) == 0
        scale = slots[4] * modulus[...]
        scale = jnp.where(active, scale, 0.0)
        kept = jnp.where(active, 0.0, slots[4] * held[0])
        terms = [
            kept + scale * (g0 + hardening * g0 * g0 * g0),
            scale * (g1 + 3.0 * hardening * g0 * g0 * g1),
            scale * (3.0 * hardening) * g0 * g1 * g1,
            scale * hardening * g1 * g1 * g1,
        ]
        nodal = [
            jnp.where(
                owned, weight * (start_gap - start_disp[0] - dt * start_vel + push * start_disp[0]), 0.0
            ),
            jnp.where(owned, weight * push * (push - 2.0), 0.0),
        ]
        rows = [jnp.sum(term, axis=0, keepdims=True) for term in terms]
        rows[0] = rows[0] + jnp.sum(nodal[0], axis=0, keepdims=True) + state[5:6, :]
        rows[1] = rows[1] + jnp.sum(nodal[1], axis=0, keepdims=True)
        last_pay[...] = jnp.concatenate(rows, axis=0)
        last_a[spot_a] = last_pay[...]

        for there in members_a():
            copy(
                last_pay, last_a.at[spot_a], pay_send.at[4], last_recv.at[0], there
            ).start()

    def relay_last():
        wait_bytes(last_a.at[pl.ds(0, size_a - 1)], last_recv.at[0])
        value = tree_sum(last_a[k] for k in range(size_a))
        last_b[chip] = value

        for there in members_b():
            copy(
                last_b.at[chip], last_b.at[chip], pay_send.at[5], last_recv.at[1], there
            ).start()

    def collect_last():
        wait_bytes(last_b.at[pl.ds(0, chips - 1)], last_recv.at[1])
        value = tree_sum(last_b[k] for k in range(chips))
        total = jnp.sum(value, axis=1, keepdims=True) + jnp.zeros((4, NB), f32)
        shift = state[7:8, :] - state[6:7, :]
        cubic = total[0:1] + shift * (total[1:2] + shift * (total[2:3] + shift * total[3:4]))
        reaction = (
            cubic + (state[1:2, :] - start_gap) * state[3:4, :] - state[0:1, :] * state[4:5, :]
        )
        react[SUBSTEPS - 1 :, :] = reaction / node_total

    def relay(s):
        wait_bytes(buf_a.at[s, pl.ds(0, size_a - 1)], a_recv.at[s])
        value = tree_sum(buf_a[s, k] for k in range(size_a))
        buf_b[s, chip] = value

        for there in members_b():
            copy(
                buf_b.at[s, chip], buf_b.at[s, chip], pay_send.at[3], b_recv.at[s], there
            ).start()

    def collect(s):
        wait_bytes(buf_b.at[s, pl.ds(0, chips - 1)], b_recv.at[s])
        value = tree_sum(buf_b[s, k] for k in range(chips))
        total = jnp.sum(value, axis=1, keepdims=True) + zero_row
        before_z = state[0:1, :]
        now_z = state[1:2, :]
        reaction = total + (now_z - start_gap) * state[3:4, :] - before_z * state[4:5, :]
        react[pl.ds(s + 1, 1), :] = reaction / node_total
        speed = state[2:3, :] - dt * contact_stiffness * reaction / impactor_mass
        state[0:1, :] = now_z
        state[1:2, :] = now_z + dt * speed
        state[2:3, :] = speed

    left = (jnp.where(lane == 0, down, r), lax.rem(lane + LANES - 1, LANES))
    right = (jnp.where(lane == LANES - 1, up, r), lax.rem(lane + 1, LANES))

    def halo_copies(turn):
        return [
            copy(
                halo_out.at[turn, side], halo_in.at[turn, 1 - side],
                halo_send.at[turn, side], halo_recv.at[turn, 1 - side], there,
            )
            for side, there in ((0, left), (1, right))
        ]

    def substep(s):
        force = forces(s)
        since = lax.rem(s, DEPTH)
        row_no = iota((NODE_ROWS, NB), 0)
        ext_no = jnp.where(
            row_no < OWN, row_no + DEPTH, jnp.where(row_no < OWN + DEPTH, row_no - OWN, row_no)
        )
        margin = jnp.where(since == DEPTH - 1, 0, 1 + since)
        valid = (ext_no >= margin) & (ext_no < OWN + 2 * DEPTH - margin)
        weight = contact[...]
        inverse = 1.0 / mass[...]
        for c in range(3):
            pull = -force[:, c * NB : (c + 1) * NB]
            if c == 0:
                pull = pull - contact_stiffness * weight * disp[0]
            based[c] = vel[c] + dt * (pull * inverse)
        free = disp[0, own, :] + dt * based[0, own, :]
        part = jnp.sum(contact[own, :] * (start_gap - free), axis=0, keepdims=True)
        pay[s] = part + state[5:6, :]
        buf_a[s, spot_a] = pay[s]

        @pl.when(s < ahead)
        def _():
            for there in members_a():
                copy(
                    pay.at[s], buf_a.at[s, spot_a], pay_send.at[2], a_recv.at[s], there
                ).start()

        @pl.when((s == 2) | (s == 5))
        def _():
            turn = s // DEPTH
            for side, first in ((0, 0), (1, OWN - DEPTH)):
                for c in range(3):
                    halo_out[turn, side, c] = disp[c, first : first + DEPTH, :]
                    halo_out[turn, side, 3 + c] = based[c, first : first + DEPTH, :]
            moves = halo_copies(turn)
            for move in moves:
                move.start()

            @pl.loop(0, 3)
            def _(k):
                relay(s - 2 + k)

            for move in moves:
                move.wait_recv()
            for side, place in ((0, left_row), (1, right_row)):
                for c in range(3):
                    disp[c, place : place + DEPTH, :] = halo_in[turn, side, c]
                    based[c, place : place + DEPTH, :] = halo_in[turn, side, 3 + c]

        @pl.when(s == ahead - 1)
        def _():
            sum_ahead()

        @pl.when(s == 1)
        def _():
            collect_first()

        @pl.when(s >= 2)
        def _():
            collect(s - 2)

        @pl.when(s == ahead - 1)
        def _():
            state[7:8, :] = state[1:2, :]

        z_now = state[1:2, :]
        pushed = (dt * contact_stiffness) * z_now * (weight * inverse)
        for c in range(3):
            fresh = based[c] + pushed if c == 0 else based[c]
            vel[c] = jnp.where(valid, fresh, vel[c])
            disp[c] = jnp.where(valid, disp[c] + dt * fresh, disp[c])

    own_part = pl.ds(pl.multiple_of(lane * (OWN * NB), OWN * NB), OWN * NB)
    other_parts = pl.ds(0, (LANES - 1) * OWN * NB)

    def gather_out(source, ref, slot):
        start = pl.multiple_of(lane * (OWN * NB), OWN * NB)
        for j in range(OWN):
            for c in range(3):
                ref[c : c + 1, pl.ds(start + j * NB, NB)] = source[c, j : j + 1, :]

        for k in FAR_FIRST:
            there = (r, shifted(lane, k, LANES))
            copy(
                ref.at[:, own_part], ref.at[:, own_part], send_sem.at[5 + slot],
                recv_sem.at[4 + slot], there,
            ).start()

    @pl.loop(0, SUBSTEPS)
    def _(s):
        substep(s)

        @pl.when(s == SUBSTEPS - 2)
        def _():
            gather_out(disp, disp_all, 0)

    gather_out(vel, vel_out, 1)
    relay_last()
    wait_bytes(disp_all.at[:, other_parts], recv_sem.at[4])
    for s in range(SUBSTEPS - 1):
        react_out[s] = jnp.max(react[s : s + 1, :])
    unfit = jnp.max(jnp.where(jnp.abs(react[: SUBSTEPS - 1, :]) < jnp.inf, 0, 1))
    wait_bytes(vel_out.at[:, other_parts], recv_sem.at[5])
    disp_out[...] = disp_all[...] + dt * vel_out[...]
    collect_last()
    last = jnp.max(react[SUBSTEPS - 1 :, :])
    react_out[SUBSTEPS - 1] = last
    flag_out[0] = jnp.maximum(unfit, jnp.where(jnp.abs(last) < jnp.inf, 0, 1))

    edge_up.wait_send()
    edge_down.wait_send()

    @pl.when((lane == 0) | (lane == LANES - 1))
    def _():
        rim_up.wait_send()

    order_up.wait_send()
    order_down.wait_send()
    for turn in range(2):
        for move in halo_copies(turn):
            move.wait_send()
    wait_bytes(pack_in.at[pl.ds(0, LANES - 1)], send_sem.at[3])
    wait_bytes(order_in.at[pl.ds(0, LANES - 1)], send_sem.at[4])
    wait_bytes(disp_all.at[:, other_parts], send_sem.at[5])
    wait_bytes(vel_out.at[:, other_parts], send_sem.at[6])
    wait_bytes(first_a.at[pl.ds(0, size_a - 1)], pay_send.at[0])
    wait_bytes(first_b.at[pl.ds(0, chips - 1)], pay_send.at[1])
    wait_bytes(buf_a.at[pl.ds(0, ahead), pl.ds(0, size_a - 1)], pay_send.at[2])
    wait_bytes(buf_b.at[pl.ds(0, ahead), pl.ds(0, chips - 1)], pay_send.at[3])
    wait_bytes(last_a.at[pl.ds(0, size_a - 1)], pay_send.at[4])
    wait_bytes(last_b.at[pl.ds(0, chips - 1)], pay_send.at[5])


def run_cycle(regions, init_disp, init_vel, mass, contact, modulus, stiffness, levels, windows, conn):
    chips = regions // 2
    vmem = pl.BlockSpec(memory_space=pltpu.VMEM)
    V = pltpu.VMEM
    vel, disp, react, flag = pl.pallas_call(
        functools.partial(cycle_kernel, regions),
        out_shape=(
            jax.ShapeDtypeStruct(init_vel.shape, f32),
            jax.ShapeDtypeStruct(init_disp.shape, f32),
            jax.ShapeDtypeStruct((SUBSTEPS,), f32),
            jax.ShapeDtypeStruct((1,), i32),
        ),
        in_specs=[pl.BlockSpec(memory_space=pltpu.HBM)] * 5
        + [vmem]
        + [pl.BlockSpec(memory_space=pltpu.HBM)] * 3,
        out_specs=[vmem] * 2 + [pl.BlockSpec(memory_space=pltpu.SMEM)] * 2,
        scratch_shapes=[
            V(init_disp.shape, f32), V(init_vel.shape, f32), V((LANES * OWN, NB), f32),
            V((LANES * OWN, NB), f32), V((16, 64), f32), V((24, 24), f32),
            V((1, 64), i32), V((1, 64), i32), V((64, NB), i32),
            V((LANES, PACK + 8, NB), f32), V((LANES, PACK + 8, NB), f32),
            V((2, EDGE + 8, NB), f32), V((LANES, EDGE + 8, NB), f32),
            V((LANES, PACK, NB), f32), V((LANES, PACK, NB), f32),
            V((2, EDGE, NB), f32), V((LANES, EDGE, NB), f32),
            V((8, DEPTH, NB), f32), V((8, DEPTH, NB), f32),
            V((2, 2, 6, DEPTH, NB), f32), V((2, 2, 6, DEPTH, NB), f32),
            V((3, NB), f32), V((2 * LANES, 3, NB), f32), V((chips, 3, NB), f32),
            V((SUBSTEPS, 1, NB), f32), V((SUBSTEPS, 2 * LANES, 1, NB), f32),
            V((SUBSTEPS, chips, 1, NB), f32),
            V((4, NB), f32), V((2 * LANES, 4, NB), f32), V((chips, 4, NB), f32),
            V((SUBSTEPS, NB), f32), V(init_disp.shape, f32),
            V((3, NODE_ROWS, NB), f32), V((3, NODE_ROWS, NB), f32), V((3, NODE_ROWS, NB), f32),
            V((NODE_ROWS, NB), f32), V((NODE_ROWS, NB), f32),
            V((NB, 5 * NB), bf16), V((4 * ROWS, 3 * NB), bf16),
            V((9 * NB, 3 * NB), bf16), V((2 * NB, NB), bf16),
            V((2 * ROWS, NB), bf16), V((NODE_ROWS, 4 * ROWS), bf16),
            V((ROWS, LANES * (PACK + EDGE)), bf16),
            V((LANES * (PACK + EDGE), LANES * (PACK + EDGE)), bf16),
            V((ROWS, NB), i32), V((ROWS, NB), i32), V((ROWS, NB), i32),
            V((ROWS, NB), i32), V((ROWS, NB), i32),
            V((ROWS, NB), f32), V((ROWS, NB), i32), V((3, ROWS, NB), f32), V((8, NB), f32),
            pltpu.SemaphoreType.DMA((9,)), pltpu.SemaphoreType.DMA((7,)),
            pltpu.SemaphoreType.DMA((6,)), pltpu.SemaphoreType.DMA((2,)),
            pltpu.SemaphoreType.DMA((SUBSTEPS,)), pltpu.SemaphoreType.DMA((SUBSTEPS,)),
            pltpu.SemaphoreType.DMA((9,)),
            pltpu.SemaphoreType.DMA((2, 2)), pltpu.SemaphoreType.DMA((2, 2)),
            pltpu.SemaphoreType.DMA((2,)), pltpu.SemaphoreType.REGULAR,
        ],
        compiler_params=pltpu.CompilerParams(
            collective_id=0, has_side_effects=True, vmem_limit_bytes=48 * 1024 * 1024
        ),
        name="crush_cycle",
    )(
        init_disp, init_vel, mass.reshape(-1, NB), contact.reshape(-1, NB), modulus.T, stiffness,
        levels.reshape(1, -1), windows.reshape(1, -1), conn,
    )
    return (disp, vel, react), flag[0]


def hand_over(disp_in, vel_in, react_in, disp_out, vel_out, react_out):
    disp_out[...] = disp_in[...]
    vel_out[...] = vel_in[...]
    for s in range(SUBSTEPS):
        react_out[s] = react_in[s]


def finish(results):
    vmem = pl.BlockSpec(memory_space=pltpu.VMEM)
    smem = pl.BlockSpec(memory_space=pltpu.SMEM)
    return pl.pallas_call(
        hand_over,
        out_shape=tuple(jax.ShapeDtypeStruct(x.shape, f32) for x in results),
        in_specs=[vmem, vmem, smem],
        out_specs=(vmem, vmem, smem),
        name="hand_over",
    )(*results)


def sum_over(value, axis):
    count = lax.axis_size(axis)
    step = 1
    while step < count:
        value = value + lax.ppermute(value, axis, [(i, i ^ step) for i in range(count)])
        step *= 2
    return value


def with_halo(array, sides, width):
    for axis, dim in sides:
        count, length = (lax.axis_size(axis), array.shape[dim])
        up = [(i, (i + 1) % count) for i in range(count)]
        down = [(j, i) for i, j in up]
        last = lax.slice_in_dim(array, length - width, length, axis=dim)
        initial = lax.slice_in_dim(array, 0, width, axis=dim)
        before = lax.ppermute(last, axis, up)
        after = lax.ppermute(initial, axis, down)
        array = jnp.concatenate([before, array, after], axis=dim)
    return array


def element_forces(slot_disp, block_modulus, stiffness):
    count = slot_disp.shape[0]
    elements = block_modulus.shape[1]
    vectors = (
        slot_disp.reshape(count, 3, elements, 8).transpose(0, 2, 1, 3).reshape(count, elements, 24)
    )
    strain = jnp.einsum("bek,jk->bej", vectors, stiffness, precision=lax.Precision.HIGHEST)
    result = block_modulus[:, :, None] * (strain + hardening * strain * strain * strain)
    return (
        result.reshape(count, elements, 3, 8).transpose(0, 2, 1, 3).reshape(count, 3, elements * 8)
    )


def plain_cycle(init_disp, init_vel, mass, contact, modulus, stiffness, levels, windows, conn):
    region_count = lax.axis_size("region")
    node_region = init_disp.shape[1]
    slot_count = conn.shape[1]
    block_rows = NB
    node_total = node_region * region_count
    impactor_mass = impactor_ratio * node_total
    extended_blocks = node_region // block_rows + 2
    block_order = jnp.argsort(levels, stable=True)
    conn = conn[block_order]
    windows = windows[block_order]
    levels = levels[block_order]
    modulus = modulus[block_order]
    level_slot = (
        (levels >= 2).astype(jnp.int32)
        + (levels >= 4).astype(jnp.int32)
        + (levels >= 8).astype(jnp.int32)
    )
    level_force = jnp.zeros((4, 3, extended_blocks, block_rows), jnp.float32)
    disp_full = init_disp
    disp_state = init_disp
    vel_state = init_vel
    gap_now = jnp.float32(start_gap)
    speed = jnp.float32(start_speed)
    history = []
    slot_iota = lax.broadcasted_iota(jnp.int32, (group_size, 2 * block_rows, slot_count), 1)
    for substep in range(SUBSTEPS):
        top_level = SUBSTEPS if substep == 0 else min(substep & -substep, SUBSTEPS)
        top_index = top_level.bit_length() - 1
        active_count = jnp.sum((levels <= top_level).astype(jnp.int32))
        level_force = level_force.at[: top_index + 1].set(0.0)
        disp_ext = with_halo(disp_full, (("region", 1),), block_rows)

        def one_group(group_index, totals):
            offset = group_index * group_size
            conn_group = lax.dynamic_slice_in_dim(conn, offset, group_size, 0)
            window_group = lax.dynamic_slice_in_dim(windows, offset, group_size, 0)
            level_group = lax.dynamic_slice_in_dim(level_slot, offset, group_size, 0)
            modulus_group = lax.dynamic_slice_in_dim(modulus, offset, group_size, 0)
            valid = offset + jnp.arange(group_size, dtype=jnp.int32) < active_count
            window_disp = jax.vmap(
                lambda first_block: lax.dynamic_slice_in_dim(
                    disp_ext, first_block * block_rows, 2 * block_rows, 1
                )
            )(window_group)
            onehot = (slot_iota == conn_group[:, None, :]).astype(jnp.float32)
            slot_disp = jnp.einsum(
                "gcw,gws->gcs", window_disp, onehot, precision=lax.Precision.HIGHEST
            )
            slot_force = element_forces(slot_disp, modulus_group, stiffness)
            slot_force = jnp.where(valid[:, None, None], slot_force, 0.0)
            window_force = jnp.einsum(
                "gcs,gws->gcw", slot_force, onehot, precision=lax.Precision.HIGHEST
            )
            window_force = window_force.reshape(group_size, 3, 2, block_rows)
            totals = totals.at[level_group, :, window_group].add(window_force[:, :, 0])
            totals = totals.at[level_group, :, window_group + 1].add(window_force[:, :, 1])
            return totals

        group_total = (active_count + group_size - 1) // group_size
        level_force = lax.fori_loop(0, group_total, one_group, level_force)
        force_ext = jnp.sum(level_force, axis=0).reshape(3, extended_blocks * block_rows)
        outer_rims = jnp.concatenate(
            (force_ext[:, :block_rows], force_ext[:, -block_rows:]), axis=1
        )
        rim_terms = with_halo(outer_rims, (("region", 1),), block_rows)
        partial_force = force_ext[:, block_rows:-block_rows]
        partial_force = partial_force.at[:, :block_rows].add(rim_terms[:, :block_rows])
        partial_force = partial_force.at[:, -block_rows:].add(rim_terms[:, -block_rows:])
        force = sum_over(partial_force, "lane")
        disp_state = disp_full
        gap = gap_now - disp_state[0]
        total = sum_over(jnp.sum(contact * gap), "region")
        history.append(total / node_total)
        push = jnp.zeros_like(force).at[0].set(contact_stiffness * contact * gap)
        accel = (push - force) / mass[None, :]
        vel_state = vel_state + time_step * accel
        disp_state = disp_state + time_step * vel_state
        speed = speed - time_step * contact_stiffness * total / impactor_mass
        gap_now = gap_now + time_step * speed
        disp_full = disp_state
    return (disp_full, vel_state, jnp.stack(history))


def on_device(*arguments):
    regions = lax.axis_size("region")
    fast, flag = run_cycle(regions, *arguments)
    return finish(lax.cond(flag == 0, lambda: fast, lambda: plain_cycle(*arguments)))


def solution(mesh):
    in_specs = (
        P(None, "region"),
        P(None, "region"),
        P("region"),
        P("region"),
        P(("region", "lane"), None),
        P(),
        P(("region", "lane")),
        P(("region", "lane")),
        P(("region", "lane"), None),
    )
    out_specs = (P(None, "region"), P(None, "region"), P())
    return jax.shard_map(
        on_device, mesh=mesh, in_specs=in_specs, out_specs=out_specs, check_vma=False
    )
```

```python
import functools

import jax
import jax.numpy as jnp
from jax import lax
from jax.experimental import pallas as pl
from jax.experimental.pallas import tpu as pltpu
from jax.sharding import PartitionSpec as P

NB = 128
SUBSTEPS = 8
LANES = 8
FAR_FIRST = (4, 3, 5, 2, 6, 1, 7)
OWN = 8
DEPTH = 3
NODE_ROWS = 16
ANCHORS = OWN - 1 + 2 * DEPTH
ROWS = 160
PACK = 32
EDGE = 16

time_step = 0.05
contact_stiffness = 1.0
hardening = 2.0
impactor_ratio = 0.05
start_gap = 1.0
start_speed = 1.0
group_size = 8

f32, bf16, i32 = jnp.float32, jnp.bfloat16, jnp.int32


def iota(shape, dim):
    return lax.broadcasted_iota(i32, shape, dim)


def dot(a, b):
    return jnp.dot(a, b, preferred_element_type=f32)


def dot_t(a, b):
    return lax.dot_general(a, b, (((1,), (1,)), ((), ())), preferred_element_type=f32)


def split2(value):
    high = value.astype(bf16)
    return high, (value - high.astype(f32)).astype(bf16)


def split3(value):
    high = value.astype(bf16)
    rest = value - high.astype(f32)
    middle = rest.astype(bf16)
    return high, middle, (rest - middle.astype(f32)).astype(bf16)


def take(value, index):
    return jnp.take_along_axis(value, index, axis=1, mode="promise_in_bounds")


def row_of(ext):
    return jnp.where(ext < DEPTH, ext + OWN, jnp.where(ext < DEPTH + OWN, ext - DEPTH, ext))


def tree_sum(values):
    values = list(values)
    while len(values) > 1:
        pairs = [a + b for a, b in zip(values[::2], values[1::2])]
        values = pairs + values[len(pairs) * 2 :]
    return values[0]


def onehot(mask):
    return jnp.where(mask, 1.0, 0.0).astype(bf16)


def cycle_kernel(
    regions,
    disp_far, vel_far, mass_far, contact_far, modulus_far, stiff_far, level_far, window_far, conn_far,
    vel_out, disp_out, react_out, flag_out,
    disp_in, vel_in, mass_in, contact_in, modulus_in, stiff_in, level_in, window_in, conn_in,
    pack_out, pack_in, edge_out, edge_in, order_out, order_in, order_edge_out, order_edge_in,
    rim_out, rim_in, halo_out, halo_in,
    first_pay, first_a, first_b, pay, buf_a, buf_b, last_pay, last_a, last_b, react, disp_all,
    disp, vel, based, mass, contact, table, slot_cols, kron, tri,
    wab, back, keep_rows, strict, conn_idx, half, perm, end1, end2, modulus, level, held, state,
    send_sem, recv_sem, pay_send, first_recv, a_recv, b_recv, load_sem, halo_send, halo_recv, last_recv, vouch,
):
    r = lax.axis_index("region")
    lane = lax.axis_index("lane")
    core = lax.rem(r, 2)
    chip = r // 2
    chips = regions // 2
    up = lax.rem(r + 1, regions)
    down = lax.rem(r + regions - 1, regions)
    size_a = 2 * LANES
    spot_a = lane * 2 + core
    dt = time_step
    node_total = regions * LANES * OWN * NB
    impactor_mass = impactor_ratio * node_total

    def peer_b(k):
        return (k * 2 + core, lane)

    deep = min(chips, LANES)
    wide = chips // deep

    def ring(step, size):
        return min(step, size - step)

    steps_a = sorted(
        ((y, c) for y in range(LANES) for c in range(2) if y or c),
        key=lambda step: (-ring(step[0], LANES), step),
    )
    steps_b = sorted(
        ((x, z) for x in range(wide) for z in range(deep) if x or z),
        key=lambda step: (-ring(step[0], wide) - ring(step[1], deep), step),
    )

    def members_a():
        for y, c in steps_a:
            yield (chip * 2 + lax.rem(core + c, 2), lax.rem(lane + y, LANES))

    def members_b():
        for x, z in steps_b:
            yield peer_b(
                lax.rem(chip // deep + x, wide) * deep + lax.rem(lax.rem(chip, deep) + z, deep)
            )

    def signal(device):
        pl.semaphore_signal(
            pltpu.get_barrier_semaphore(), inc=1, device_id=device,
            device_id_type=pl.DeviceIdType.MESH,
        )

    def shifted(spot, step, size):
        return lax.rem(spot + step, size)

    for there in members_a():
        signal(there)

    def along_x(k):
        return peer_b(lax.rem(chip // deep + k, wide) * deep + lax.rem(chip, deep))

    def along_z(k):
        return peer_b((chip // deep) * deep + lax.rem(chip + k, deep))

    for k in range(1, deep):
        signal(along_z(k))
    for k in range(1, wide):
        signal(along_x(k))

    @pl.when(lane == 0)
    def _():
        @pl.loop(0, LANES)
        def _(j):
            signal((down, j))

    @pl.when(lane == LANES - 1)
    def _():
        @pl.loop(0, LANES)
        def _(j):
            signal((up, j))

    def copy(src, dst, send, recv, device):
        return pltpu.make_async_remote_copy(
            src_ref=src, dst_ref=dst, send_sem=send, recv_sem=recv,
            device_id=device, device_id_type=pl.DeviceIdType.MESH,
        )

    def wait_bytes(ref, sem):
        pltpu.make_async_copy(ref, ref, sem).wait()

    loads = []
    for k, (far, here) in enumerate((
        (level_far, level_in), (window_far, window_in), (modulus_far, modulus_in),
        (conn_far, conn_in), (contact_far, contact_in), (mass_far, mass_in),
        (disp_far, disp_in), (vel_far, vel_in), (stiff_far, stiff_in),
    )):
        loads.append(pltpu.make_async_copy(far, here, load_sem.at[k]))
        loads[-1].start()
    for load in loads:
        load.wait()

    level_row = level_in[...].astype(f32)
    window_row = window_in[...].astype(f32)
    dest = iota((16, 64), 0)
    offsets = jnp.where(
        dest < LANES, (DEPTH - 1) - OWN * dest,
        jnp.where(dest == LANES, DEPTH - 1 - OWN * LANES, OWN + DEPTH - 1),
    ).astype(f32)
    anchor_all = window_row + offsets
    lowest = jnp.where(dest == LANES + 1, OWN + DEPTH - 1, 0).astype(f32)
    highest = jnp.where(dest == LANES, DEPTH - 1, ANCHORS - 1).astype(f32)
    wanted = jnp.where(
        (anchor_all >= lowest) & (anchor_all <= highest) & (dest < LANES + 2), 1.0, 0.0
    )
    before = onehot(iota((64, 64), 0) < iota((64, 64), 1))
    rank_key = jnp.where(wanted > 0.0, dot(wanted.astype(bf16), before), -1.0)
    count = jnp.sum(wanted, axis=1, keepdims=True)
    room = jnp.where(iota((16, 1), 0) < LANES, PACK, EDGE).astype(f32)
    overflow = jnp.max(jnp.where(count > room, 1.0, 0.0), axis=0, keepdims=True)
    picks = [
        onehot(iota((PACK, 64), 0).astype(f32) == rank_key[k : k + 1, :]) for k in range(LANES)
    ] + [
        onehot(iota((EDGE, 64), 0).astype(f32) == rank_key[k : k + 1, :])
        for k in (LANES, LANES + 1)
    ]
    pick = jnp.concatenate(picks, axis=0)
    conn_f = conn_in[...].astype(f32)
    picked = LANES * PACK + 2 * EDGE
    tiled = jnp.concatenate([modulus_in[...]] * 8, axis=0)
    chosen = sum(dot_t(pick, part) for part in split3(tiled))
    chosen = jnp.where(
        (iota((picked, NB), 0) & 7) == iota((picked, NB), 1) // 16, chosen, 0.0
    )
    grouped = jnp.sum(chosen.reshape(picked // 8, 8, NB), axis=1)
    facts = jnp.concatenate(
        [level_row, window_row, jnp.ones((1, 64), f32), jnp.zeros((5, 64), f32)], axis=0
    ).astype(bf16)
    chosen_conn = dot(pick, conn_f.astype(bf16))
    spot = iota((NB, 64), 0).astype(f32)

    def lane_rows(k, start, offset):
        key = jnp.where(rank_key[k : k + 1, :] >= 0.0, rank_key[k : k + 1, :] + start, -1.0)
        found = dot_t(facts, onehot(spot == key))
        return jnp.concatenate(
            [found[0:1, :], found[1:2, :] + float(offset) * found[2:3, :], jnp.zeros((2, NB), f32)],
            axis=0,
        )

    quarter = (PACK * lax.rem(lane, 4)).astype(f32)
    eighth = (EDGE * lane).astype(f32)
    for k in range(LANES):
        pack_out[k, :PACK, :] = chosen_conn[k * PACK : (k + 1) * PACK, :]
        pack_out[k, PACK : PACK + 4, :] = grouped[4 * k : 4 * k + 4, :]
        pack_out[k, PACK + 4 :, :] = lane_rows(k, quarter, DEPTH - 1 - OWN * k)
    for k, offset in ((0, DEPTH - 1 - OWN * LANES), (1, OWN + DEPTH - 1)):
        start = LANES * PACK + k * EDGE
        edge_out[k, :EDGE, :] = chosen_conn[start : start + EDGE, :]
        edge_out[k, EDGE : EDGE + 4, :] = jnp.concatenate(
            [grouped[start // 8 : start // 8 + 2, :], jnp.zeros((2, NB), f32)], axis=0
        )
        edge_out[k, EDGE + 4 :, :] = lane_rows(LANES + k, eighth, offset)

    def load_nodes(place, source_lane, first, number):
        start = pl.multiple_of(source_lane * (OWN * NB), OWN * NB)
        for j in range(number):
            part = pl.ds(start + (first + j) * NB, NB)
            for c in range(3):
                disp[c, place + j : place + j + 1, :] = disp_in[c : c + 1, part]
                vel[c, place + j : place + j + 1, :] = vel_in[c : c + 1, part]
        rows = pl.ds(pl.multiple_of(source_lane * OWN, OWN), OWN)
        mass[place : place + number, :] = mass_in[rows, :][first : first + number, :]
        contact[place : place + number, :] = contact_in[rows, :][first : first + number, :]

    left_row, right_row = OWN, OWN + DEPTH
    disp[...] = jnp.zeros_like(disp)
    vel[...] = jnp.zeros_like(vel)
    mass[...] = jnp.ones_like(mass)
    contact[...] = jnp.zeros_like(contact)
    load_nodes(0, lane, 0, OWN)

    own = pl.ds(0, OWN)
    own_contact = contact[own, :]
    own_mass = mass[own, :]
    push_rate = (dt * dt * contact_stiffness) * own_contact / own_mass
    sums = [
        jnp.sum(own_contact * (start_gap - disp[0, own, :]), axis=0, keepdims=True),
        jnp.sum(own_contact, axis=0, keepdims=True),
        jnp.sum(own_contact * push_rate, axis=0, keepdims=True),
    ]
    first_pay[...] = jnp.concatenate(sums, axis=0)
    first_a[spot_a] = first_pay[...]

    pl.semaphore_wait(pltpu.get_barrier_semaphore(), size_a - 1 + deep - 1 + wide - 1 + 2)
    for k in range(1, wide):
        pl.semaphore_signal(
            vouch, inc=1, device_id=along_x(k), device_id_type=pl.DeviceIdType.MESH
        )

    edge_up = copy(edge_out.at[0], edge_in.at[lane], send_sem.at[0], recv_sem.at[0], (up, 0))
    edge_down = copy(
        edge_out.at[1], edge_in.at[lane], send_sem.at[1], recv_sem.at[0], (down, LANES - 1)
    )
    edge_up.start()
    edge_down.start()
    for there in members_a():
        copy(
            first_pay, first_a.at[spot_a], pay_send.at[0], first_recv.at[0], there
        ).start()

    for k in FAR_FIRST:
        there = shifted(lane, k, LANES)
        copy(
            pack_out.at[there], pack_in.at[lane], send_sem.at[3], recv_sem.at[2], (r, there)
        ).start()

    def load_rim(rim_lane, first):
        for j in range(DEPTH):
            at = (rim_lane * OWN + first + j) * NB
            part = slice(at, at + NB)
            for c in range(3):
                rim_out[c, j : j + 1, :] = disp_in[c : c + 1, part]
                rim_out[3 + c, j : j + 1, :] = vel_in[c : c + 1, part]
        rows = slice(rim_lane * OWN + first, rim_lane * OWN + first + DEPTH)
        rim_out[6, :, :] = mass_in[rows, :]
        rim_out[7, :, :] = contact_in[rows, :]

    @pl.when(lane == 0)
    def _():
        load_rim(LANES - 1, OWN - DEPTH)

    @pl.when(lane == LANES - 1)
    def _():
        load_rim(0, 0)

    rim_up = copy(rim_out, rim_in, send_sem.at[2], recv_sem.at[1], (up, 0))
    rim_down = copy(rim_out, rim_in, send_sem.at[2], recv_sem.at[1], (down, LANES - 1))

    @pl.when(lane == 0)
    def _():
        rim_up.start()

    @pl.when(lane == LANES - 1)
    def _():
        rim_down.start()

    pack_in[lane] = pack_out[lane]
    load_nodes(left_row, jnp.maximum(lane - 1, 0), OWN - DEPTH, DEPTH)
    load_nodes(right_row, jnp.minimum(lane + 1, LANES - 1), 0, DEPTH)

    lane64 = iota((64, NB), 1)
    keys = conn_f * float(NB) + lane64.astype(f32)
    span = 2
    while span <= NB:
        step = span // 2
        while step >= 1:
            other = take(keys, lane64 ^ step)
            keep_low = ((lane64 & step) == 0) == ((lane64 & span) == 0)
            keys = jnp.where(keep_low, jnp.minimum(keys, other), jnp.maximum(keys, other))
            step //= 2
        span *= 2
    order = (keys.astype(i32) & (NB - 1)).astype(f32)
    chosen_order = dot(pick, order.astype(bf16))
    for k in range(LANES):
        order_out[k] = chosen_order[k * PACK : (k + 1) * PACK, :]
    for k in range(2):
        start = LANES * PACK + k * EDGE
        order_edge_out[k] = chosen_order[start : start + EDGE, :]
    order_up = copy(
        order_edge_out.at[0], order_edge_in.at[lane], send_sem.at[7], recv_sem.at[6], (up, 0)
    )
    order_down = copy(
        order_edge_out.at[1], order_edge_in.at[lane], send_sem.at[8], recv_sem.at[6],
        (down, LANES - 1),
    )
    order_up.start()
    order_down.start()

    for k in FAR_FIRST:
        there = shifted(lane, k, LANES)
        copy(
            order_out.at[there], order_in.at[lane], send_sem.at[4], recv_sem.at[3], (r, there)
        ).start()

    order_in[lane] = order_out[lane]

    offered = LANES * (PACK + EDGE)
    strict[...] = onehot(iota((offered, offered), 0) < iota((offered, offered), 1))
    stiff = split2(stiff_in[...])
    at = iota((3 * NB, 24), 0)
    names = onehot((at // NB) * 8 + lax.rem(at, 8) == iota((3 * NB, 24), 1))
    row_element = lax.rem(iota((3 * NB, 3 * NB), 0), NB) // 8
    col_element = lax.rem(iota((3 * NB, 3 * NB), 1), NB) // 8
    same = row_element == col_element
    for part, places in ((stiff[0], (0, 1)), (stiff[1], (2,))):
        grown = dot_t(dot_t(names, part).astype(bf16), names)
        grown = jnp.where(same, grown, 0.0).astype(bf16)
        for at_place in places:
            kron[at_place * 3 * NB : (at_place + 1) * 3 * NB, :] = grown
    running = onehot(iota((NB, NB), 0) <= iota((NB, NB), 1))
    tri[0:NB, :] = running
    tri[NB:, :] = running

    @pl.when((lane != 0) & (lane != LANES - 1))
    def _():
        edge_in[...] = jnp.zeros_like(edge_in)
        order_edge_in[...] = jnp.zeros_like(order_edge_in)

    if wide > 1:
        pl.semaphore_wait(vouch, wide - 1)
    wait_bytes(first_a.at[pl.ds(0, size_a - 1)], first_recv.at[0])
    total = tree_sum(first_a[k] for k in range(size_a))
    first_b[chip] = total
    first_pay2 = first_b.at[chip]

    for there in members_b():
        copy(
            first_pay2, first_b.at[chip], pay_send.at[1], first_recv.at[1], there
        ).start()

    @pl.when((lane == 0) | (lane == LANES - 1))
    def _():
        wait_bytes(edge_in, recv_sem.at[0])
        wait_bytes(rim_in, recv_sem.at[1])

    def unpack_rim(place):
        for c in range(3):
            disp[c, place : place + DEPTH, :] = rim_in[c]
            vel[c, place : place + DEPTH, :] = rim_in[3 + c]
        mass[place : place + DEPTH, :] = rim_in[6]
        contact[place : place + DEPTH, :] = rim_in[7]

    @pl.when(lane == 0)
    def _():
        unpack_rim(left_row)

    @pl.when(lane == LANES - 1)
    def _():
        unpack_rim(right_row)

    wait_bytes(pack_in.at[pl.ds(0, LANES - 1)], recv_sem.at[2])

    conn_rows = jnp.concatenate(
        [pack_in[j, :PACK, :] for j in range(LANES)] + [edge_in[j, :EDGE, :] for j in range(LANES)],
        axis=0,
    )
    shared = jnp.concatenate(
        [pack_in[j, PACK : PACK + 4, :] for j in range(LANES)]
        + [edge_in[j, EDGE : EDGE + 2, :] for j in range(LANES)],
        axis=0,
    )
    shared = jnp.broadcast_to(shared[:, None, :], (offered // 8, 8, NB)).reshape(offered, NB)
    moduli = take(shared, 16 * (iota((offered, NB), 0) & 7) + iota((offered, NB), 1) // 8)
    facts_in = jnp.concatenate(
        [
            sum(pack_in[j, PACK + 4 :, :] for j in range(4)),
            sum(pack_in[j, PACK + 4 :, :] for j in range(4, LANES)),
            sum(edge_in[j, EDGE + 4 :, :] for j in range(LANES)),
        ],
        axis=1,
    )
    levels_in = facts_in[0:1, :]
    anchors_in = facts_in[1:2, :]
    present = jnp.where(levels_in > 0.0, 1.0, 0.0) + jnp.zeros((8, offered), f32)
    key = jnp.where(present > 0.0, dot(present.astype(bf16), strict[...]), -1.0)[0:1, :]
    taken = jnp.sum(present[0:1, :], axis=1, keepdims=True)
    overflow = jnp.maximum(overflow, jnp.where(taken > float(ROWS), 1.0, 0.0))
    keep = onehot(iota((ROWS, offered), 0).astype(f32) == key)
    conn = dot(keep, conn_rows.astype(bf16))
    moduli_parts = split3(moduli)
    modulus[...] = sum(dot(keep, part) for part in moduli_parts)
    wide_levels = (levels_in + jnp.zeros((NB, offered), f32)).astype(bf16)
    wide_anchors = (anchors_in + jnp.zeros((NB, offered), f32)).astype(bf16)

    lane_no = iota((ROWS, NB), 1)
    level[...] = dot_t(keep, wide_levels).astype(i32) - 1
    anchor = dot_t(keep, wide_anchors).astype(i32)
    wab[:ROWS, :] = onehot((lane_no & 31) == row_of(anchor))
    wab[ROWS:, :] = onehot((lane_no & 31) == row_of(anchor + 1))
    anchor_row = dot_t(wide_anchors[:8, :], keep)[0:1, :].astype(i32)
    node_row = iota((NODE_ROWS, ROWS), 0)
    back_a = onehot(node_row == row_of(anchor_row))
    back_b = onehot(node_row == row_of(anchor_row + 1))
    back[...] = jnp.concatenate([back_a, back_b, back_a, back_b], axis=1)
    conn_i = conn.astype(i32)
    conn_idx[...] = conn_i & (NB - 1)
    half[...] = conn_i >> 7

    keep_rows[...] = keep
    held[...] = jnp.zeros_like(held)
    table[...] = jnp.zeros_like(table)

    zero_row = jnp.zeros((1, NB), f32)
    state[0:1, :] = zero_row + start_gap
    state[1:2, :] = zero_row + start_gap
    state[5:6, :] = jnp.where(overflow > 0.0, jnp.inf, 0.0) + zero_row

    def collect_first():
        wait_bytes(first_b.at[pl.ds(0, chips - 1)], first_recv.at[1])
        total = tree_sum(first_b[k] for k in range(chips))
        first = jnp.sum(total, axis=1, keepdims=True)
        reaction = first[0:1, :] + zero_row
        speed = start_speed - dt * contact_stiffness * reaction / impactor_mass
        state[1:2, :] = start_gap + dt * speed
        state[2:3, :] = speed
        state[3:4, :] = first[1:2, :] + zero_row
        state[4:5, :] = first[2:3, :] + zero_row
        react[0:1, :] = reaction / node_total

    first_lane = iota((ROWS, NB), 1) == 0

    def to_slots(fields):
        width = len(fields) * NB
        parts = [split3(field) for field in fields]
        for k in range(3):
            table[32 * k : 32 * k + NODE_ROWS, :width] = jnp.concatenate(
                [part[k] for part in parts], axis=1
            )
        both = dot(wab[...], table[:, :width])
        index = conn_idx[...]
        second = half[...] > 0
        slots = []
        for c in range(len(fields)):
            cols = slice(c * NB, (c + 1) * NB)
            slots.append(
                jnp.where(second, take(both[ROWS:, cols], index), take(both[:ROWS, cols], index))
            )
        return slots

    def receive_order():
        lane_no = iota((ROWS, NB), 1)

        @pl.when((lane == 0) | (lane == LANES - 1))
        def _():
            wait_bytes(order_edge_in, recv_sem.at[6])

        wait_bytes(order_in.at[pl.ds(0, LANES - 1)], recv_sem.at[3])
        order_rows = jnp.concatenate(
            [
                order_in[...].reshape(LANES * PACK, NB),
                order_edge_in[...].reshape(LANES * EDGE, NB),
            ],
            axis=0,
        )
        order = dot(keep_rows[...], order_rows.astype(bf16)).astype(i32)
        perm[...] = order
        nodes = take(half[...] * NB + conn_idx[...], order)
        for ref, base in ((end1, 0), (end2, NB)):
            target = lane_no + base
            found = jnp.zeros((ROWS, NB), i32)
            for step in (64, 32, 16, 8, 4, 2, 1, 0):
                probe = take(nodes, found + (step - 1 if step else 0))
                found = jnp.where(probe <= target, found + max(step, 1), found)
            ref[...] = found - 1

    def forces(s):
        top, rest = split2(jnp.concatenate(to_slots([disp[c] for c in range(3)]), axis=1))
        strain = dot(jnp.concatenate([top, rest, top], axis=1), kron[...])
        active = (level[...] & s) == 0
        mod = modulus[...]
        for c in range(3):
            g = strain[:, c * NB : (c + 1) * NB]
            fresh = mod * (g + hardening * g * g * g)
            held[c] = jnp.where(active, fresh, held[c])

        @pl.when(s == 0)
        def _():
            receive_order()

        order = perm[...]
        sorted_forces = []
        for c in range(3):
            sorted_forces.append(jnp.concatenate(split2(take(held[c], order)), axis=1))
        sums = dot(jnp.concatenate(sorted_forces, axis=0), tri[...])
        e1 = end1[...]
        e2 = end2[...]
        for c in range(3):
            part = sums[c * ROWS : (c + 1) * ROWS, :]
            upto1 = jnp.where(e1 >= 0, take(part, e1 & (NB - 1)), 0.0)
            upto2 = jnp.where(e2 >= 0, take(part, e2 & (NB - 1)), 0.0)
            prev1 = pltpu.roll(upto1, 1, 1)
            prev2 = pltpu.roll(upto2, 1, 1)
            f1 = split2(upto1 - jnp.where(first_lane, 0.0, prev1))
            f2 = split2(upto2 - jnp.where(first_lane, prev1, prev2))
            cols = slice(c * NB, (c + 1) * NB)
            slot_cols[0:ROWS, cols] = f1[0]
            slot_cols[ROWS : 2 * ROWS, cols] = f2[0]
            slot_cols[2 * ROWS : 3 * ROWS, cols] = f1[1]
            slot_cols[3 * ROWS :, cols] = f2[1]
        return dot(back[...], slot_cols[...])

    ahead = SUBSTEPS - 2

    def sum_ahead():
        centre = state[1:2, :]
        state[6:7, :] = centre
        weight = contact[...]
        inverse = 1.0 / mass[...]
        rate = (dt * contact_stiffness) * weight * inverse
        push = dt * rate
        start_vel = based[0] + centre * rate
        start_disp = [disp[0] + dt * start_vel] + [disp[c] + dt * based[c] for c in (1, 2)]
        owned = iota((NODE_ROWS, NB), 0) < OWN
        share = jnp.where(owned, dt * dt * weight * inverse, 0.0)
        slots = to_slots(start_disp + [push, share])
        top, rest = split2(jnp.concatenate(slots[:3], axis=1))
        g0 = dot(jnp.concatenate([top, rest, top], axis=1), kron[:, :NB])
        top, rest = split2(slots[3])
        first_block = jnp.concatenate(
            [kron[k * 3 * NB : k * 3 * NB + NB, :NB] for k in range(3)], axis=0
        )
        g1 = dot(jnp.concatenate([top, rest, top], axis=1), first_block)
        active = (level[...] & ahead) == 0
        scale = slots[4] * modulus[...]
        scale = jnp.where(active, scale, 0.0)
        kept = jnp.where(active, 0.0, slots[4] * held[0])
        terms = [
            kept + scale * (g0 + hardening * g0 * g0 * g0),
            scale * (g1 + 3.0 * hardening * g0 * g0 * g1),
            scale * (3.0 * hardening) * g0 * g1 * g1,
            scale * hardening * g1 * g1 * g1,
        ]
        nodal = [
            jnp.where(
                owned, weight * (start_gap - start_disp[0] - dt * start_vel + push * start_disp[0]), 0.0
            ),
            jnp.where(owned, weight * push * (push - 2.0), 0.0),
        ]
        rows = [jnp.sum(term, axis=0, keepdims=True) for term in terms]
        rows[0] = rows[0] + jnp.sum(nodal[0], axis=0, keepdims=True) + state[5:6, :]
        rows[1] = rows[1] + jnp.sum(nodal[1], axis=0, keepdims=True)
        last_pay[...] = jnp.concatenate(rows, axis=0)
        last_a[spot_a] = last_pay[...]

        for there in members_a():
            copy(
                last_pay, last_a.at[spot_a], pay_send.at[4], last_recv.at[0], there
            ).start()

    def relay_last():
        wait_bytes(last_a.at[pl.ds(0, size_a - 1)], last_recv.at[0])
        value = tree_sum(last_a[k] for k in range(size_a))
        last_b[chip] = value

        for there in members_b():
            copy(
                last_b.at[chip], last_b.at[chip], pay_send.at[5], last_recv.at[1], there
            ).start()

    def collect_last():
        wait_bytes(last_b.at[pl.ds(0, chips - 1)], last_recv.at[1])
        value = tree_sum(last_b[k] for k in range(chips))
        total = jnp.sum(value, axis=1, keepdims=True) + jnp.zeros((4, NB), f32)
        shift = state[7:8, :] - state[6:7, :]
        cubic = total[0:1] + shift * (total[1:2] + shift * (total[2:3] + shift * total[3:4]))
        reaction = (
            cubic + (state[1:2, :] - start_gap) * state[3:4, :] - state[0:1, :] * state[4:5, :]
        )
        react[SUBSTEPS - 1 :, :] = reaction / node_total

    def relay(s):
        wait_bytes(buf_a.at[s, pl.ds(0, size_a - 1)], a_recv.at[s])
        value = tree_sum(buf_a[s, k] for k in range(size_a))
        buf_b[s, chip] = value

        for there in members_b():
            copy(
                buf_b.at[s, chip], buf_b.at[s, chip], pay_send.at[3], b_recv.at[s], there
            ).start()

    def collect(s):
        wait_bytes(buf_b.at[s, pl.ds(0, chips - 1)], b_recv.at[s])
        value = tree_sum(buf_b[s, k] for k in range(chips))
        total = jnp.sum(value, axis=1, keepdims=True) + zero_row
        before_z = state[0:1, :]
        now_z = state[1:2, :]
        reaction = total + (now_z - start_gap) * state[3:4, :] - before_z * state[4:5, :]
        react[pl.ds(s + 1, 1), :] = reaction / node_total
        speed = state[2:3, :] - dt * contact_stiffness * reaction / impactor_mass
        state[0:1, :] = now_z
        state[1:2, :] = now_z + dt * speed
        state[2:3, :] = speed

    left = (jnp.where(lane == 0, down, r), lax.rem(lane + LANES - 1, LANES))
    right = (jnp.where(lane == LANES - 1, up, r), lax.rem(lane + 1, LANES))

    def halo_copies(turn):
        return [
            copy(
                halo_out.at[turn, side], halo_in.at[turn, 1 - side],
                halo_send.at[turn, side], halo_recv.at[turn, 1 - side], there,
            )
            for side, there in ((0, left), (1, right))
        ]

    def substep(s):
        force = forces(s)
        since = lax.rem(s, DEPTH)
        row_no = iota((NODE_ROWS, NB), 0)
        ext_no = jnp.where(
            row_no < OWN, row_no + DEPTH, jnp.where(row_no < OWN + DEPTH, row_no - OWN, row_no)
        )
        margin = jnp.where(since == DEPTH - 1, 0, 1 + since)
        valid = (ext_no >= margin) & (ext_no < OWN + 2 * DEPTH - margin)
        weight = contact[...]
        inverse = 1.0 / mass[...]
        for c in range(3):
            pull = -force[:, c * NB : (c + 1) * NB]
            if c == 0:
                pull = pull - contact_stiffness * weight * disp[0]
            based[c] = vel[c] + dt * (pull * inverse)
        free = disp[0, own, :] + dt * based[0, own, :]
        part = jnp.sum(contact[own, :] * (start_gap - free), axis=0, keepdims=True)
        pay[s] = part + state[5:6, :]
        buf_a[s, spot_a] = pay[s]

        @pl.when(s < ahead)
        def _():
            for there in members_a():
                copy(
                    pay.at[s], buf_a.at[s, spot_a], pay_send.at[2], a_recv.at[s], there
                ).start()

        @pl.when((s == 2) | (s == 5))
        def _():
            turn = s // DEPTH
            for side, first in ((0, 0), (1, OWN - DEPTH)):
                for c in range(3):
                    halo_out[turn, side, c] = disp[c, first : first + DEPTH, :]
                    halo_out[turn, side, 3 + c] = based[c, first : first + DEPTH, :]
            moves = halo_copies(turn)
            for move in moves:
                move.start()

            @pl.loop(0, 3)
            def _(k):
                relay(s - 2 + k)

            for move in moves:
                move.wait_recv()
            for side, place in ((0, left_row), (1, right_row)):
                for c in range(3):
                    disp[c, place : place + DEPTH, :] = halo_in[turn, side, c]
                    based[c, place : place + DEPTH, :] = halo_in[turn, side, 3 + c]

        @pl.when(s == ahead - 1)
        def _():
            sum_ahead()

        @pl.when(s == 1)
        def _():
            collect_first()

        @pl.when(s >= 2)
        def _():
            collect(s - 2)

        @pl.when(s == ahead - 1)
        def _():
            state[7:8, :] = state[1:2, :]

        z_now = state[1:2, :]
        pushed = (dt * contact_stiffness) * z_now * (weight * inverse)
        for c in range(3):
            fresh = based[c] + pushed if c == 0 else based[c]
            vel[c] = jnp.where(valid, fresh, vel[c])
            disp[c] = jnp.where(valid, disp[c] + dt * fresh, disp[c])

    own_part = pl.ds(pl.multiple_of(lane * (OWN * NB), OWN * NB), OWN * NB)
    other_parts = pl.ds(0, (LANES - 1) * OWN * NB)

    def gather_out(source, ref, slot):
        start = pl.multiple_of(lane * (OWN * NB), OWN * NB)
        for j in range(OWN):
            for c in range(3):
                ref[c : c + 1, pl.ds(start + j * NB, NB)] = source[c, j : j + 1, :]

        for k in FAR_FIRST:
            there = (r, shifted(lane, k, LANES))
            copy(
                ref.at[:, own_part], ref.at[:, own_part], send_sem.at[5 + slot],
                recv_sem.at[4 + slot], there,
            ).start()

    @pl.loop(0, SUBSTEPS)
    def _(s):
        substep(s)

        @pl.when(s == SUBSTEPS - 2)
        def _():
            gather_out(disp, disp_all, 0)

    gather_out(vel, vel_out, 1)
    relay_last()
    wait_bytes(disp_all.at[:, other_parts], recv_sem.at[4])
    for s in range(SUBSTEPS - 1):
        react_out[s] = jnp.max(react[s : s + 1, :])
    unfit = jnp.max(jnp.where(jnp.abs(react[: SUBSTEPS - 1, :]) < jnp.inf, 0, 1))
    wait_bytes(vel_out.at[:, other_parts], recv_sem.at[5])
    disp_out[...] = disp_all[...] + dt * vel_out[...]
    collect_last()
    last = jnp.max(react[SUBSTEPS - 1 :, :])
    react_out[SUBSTEPS - 1] = last
    flag_out[0] = jnp.maximum(unfit, jnp.where(jnp.abs(last) < jnp.inf, 0, 1))

    edge_up.wait_send()
    edge_down.wait_send()

    @pl.when((lane == 0) | (lane == LANES - 1))
    def _():
        rim_up.wait_send()

    order_up.wait_send()
    order_down.wait_send()
    for turn in range(2):
        for move in halo_copies(turn):
            move.wait_send()
    wait_bytes(pack_in.at[pl.ds(0, LANES - 1)], send_sem.at[3])
    wait_bytes(order_in.at[pl.ds(0, LANES - 1)], send_sem.at[4])
    wait_bytes(disp_all.at[:, other_parts], send_sem.at[5])
    wait_bytes(vel_out.at[:, other_parts], send_sem.at[6])
    wait_bytes(first_a.at[pl.ds(0, size_a - 1)], pay_send.at[0])
    wait_bytes(first_b.at[pl.ds(0, chips - 1)], pay_send.at[1])
    wait_bytes(buf_a.at[pl.ds(0, ahead), pl.ds(0, size_a - 1)], pay_send.at[2])
    wait_bytes(buf_b.at[pl.ds(0, ahead), pl.ds(0, chips - 1)], pay_send.at[3])
    wait_bytes(last_a.at[pl.ds(0, size_a - 1)], pay_send.at[4])
    wait_bytes(last_b.at[pl.ds(0, chips - 1)], pay_send.at[5])


def run_cycle(regions, init_disp, init_vel, mass, contact, modulus, stiffness, levels, windows, conn):
    chips = regions // 2
    vmem = pl.BlockSpec(memory_space=pltpu.VMEM)
    V = pltpu.VMEM
    vel, disp, react, flag = pl.pallas_call(
        functools.partial(cycle_kernel, regions),
        out_shape=(
            jax.ShapeDtypeStruct(init_vel.shape, f32),
            jax.ShapeDtypeStruct(init_disp.shape, f32),
            jax.ShapeDtypeStruct((SUBSTEPS,), f32),
            jax.ShapeDtypeStruct((1,), i32),
        ),
        in_specs=[pl.BlockSpec(memory_space=pltpu.HBM)] * 5
        + [vmem]
        + [pl.BlockSpec(memory_space=pltpu.HBM)] * 3,
        out_specs=[vmem] * 2 + [pl.BlockSpec(memory_space=pltpu.SMEM)] * 2,
        scratch_shapes=[
            V(init_disp.shape, f32), V(init_vel.shape, f32), V((LANES * OWN, NB), f32),
            V((LANES * OWN, NB), f32), V((16, 64), f32), V((24, 24), f32),
            V((1, 64), i32), V((1, 64), i32), V((64, NB), i32),
            V((LANES, PACK + 8, NB), f32), V((LANES, PACK + 8, NB), f32),
            V((2, EDGE + 8, NB), f32), V((LANES, EDGE + 8, NB), f32),
            V((LANES, PACK, NB), f32), V((LANES, PACK, NB), f32),
            V((2, EDGE, NB), f32), V((LANES, EDGE, NB), f32),
            V((8, DEPTH, NB), f32), V((8, DEPTH, NB), f32),
            V((2, 2, 6, DEPTH, NB), f32), V((2, 2, 6, DEPTH, NB), f32),
            V((3, NB), f32), V((2 * LANES, 3, NB), f32), V((chips, 3, NB), f32),
            V((SUBSTEPS, 1, NB), f32), V((SUBSTEPS, 2 * LANES, 1, NB), f32),
            V((SUBSTEPS, chips, 1, NB), f32),
            V((4, NB), f32), V((2 * LANES, 4, NB), f32), V((chips, 4, NB), f32),
            V((SUBSTEPS, NB), f32), V(init_disp.shape, f32),
            V((3, NODE_ROWS, NB), f32), V((3, NODE_ROWS, NB), f32), V((3, NODE_ROWS, NB), f32),
            V((NODE_ROWS, NB), f32), V((NODE_ROWS, NB), f32),
            V((NB, 5 * NB), bf16), V((4 * ROWS, 3 * NB), bf16),
            V((9 * NB, 3 * NB), bf16), V((2 * NB, NB), bf16),
            V((2 * ROWS, NB), bf16), V((NODE_ROWS, 4 * ROWS), bf16),
            V((ROWS, LANES * (PACK + EDGE)), bf16),
            V((LANES * (PACK + EDGE), LANES * (PACK + EDGE)), bf16),
            V((ROWS, NB), i32), V((ROWS, NB), i32), V((ROWS, NB), i32),
            V((ROWS, NB), i32), V((ROWS, NB), i32),
            V((ROWS, NB), f32), V((ROWS, NB), i32), V((3, ROWS, NB), f32), V((8, NB), f32),
            pltpu.SemaphoreType.DMA((9,)), pltpu.SemaphoreType.DMA((7,)),
            pltpu.SemaphoreType.DMA((6,)), pltpu.SemaphoreType.DMA((2,)),
            pltpu.SemaphoreType.DMA((SUBSTEPS,)), pltpu.SemaphoreType.DMA((SUBSTEPS,)),
            pltpu.SemaphoreType.DMA((9,)),
            pltpu.SemaphoreType.DMA((2, 2)), pltpu.SemaphoreType.DMA((2, 2)),
            pltpu.SemaphoreType.DMA((2,)), pltpu.SemaphoreType.REGULAR,
        ],
        compiler_params=pltpu.CompilerParams(
            collective_id=0, has_side_effects=True, vmem_limit_bytes=48 * 1024 * 1024
        ),
        name="crush_cycle",
    )(
        init_disp, init_vel, mass.reshape(-1, NB), contact.reshape(-1, NB), modulus.T, stiffness,
        levels.reshape(1, -1), windows.reshape(1, -1), conn,
    )
    return (disp, vel, react), flag[0]


def hand_over(disp_in, vel_in, react_in, disp_out, vel_out, react_out):
    disp_out[...] = disp_in[...]
    vel_out[...] = vel_in[...]
    for s in range(SUBSTEPS):
        react_out[s] = react_in[s]


def finish(results):
    vmem = pl.BlockSpec(memory_space=pltpu.VMEM)
    smem = pl.BlockSpec(memory_space=pltpu.SMEM)
    return pl.pallas_call(
        hand_over,
        out_shape=tuple(jax.ShapeDtypeStruct(x.shape, f32) for x in results),
        in_specs=[vmem, vmem, smem],
        out_specs=(vmem, vmem, smem),
        name="hand_over",
    )(*results)


def sum_over(value, axis):
    count = lax.axis_size(axis)
    step = 1
    while step < count:
        value = value + lax.ppermute(value, axis, [(i, i ^ step) for i in range(count)])
        step *= 2
    return value


def with_halo(array, sides, width):
    for axis, dim in sides:
        count, length = (lax.axis_size(axis), array.shape[dim])
        up = [(i, (i + 1) % count) for i in range(count)]
        down = [(j, i) for i, j in up]
        last = lax.slice_in_dim(array, length - width, length, axis=dim)
        initial = lax.slice_in_dim(array, 0, width, axis=dim)
        before = lax.ppermute(last, axis, up)
        after = lax.ppermute(initial, axis, down)
        array = jnp.concatenate([before, array, after], axis=dim)
    return array


def element_forces(slot_disp, block_modulus, stiffness):
    count = slot_disp.shape[0]
    elements = block_modulus.shape[1]
    vectors = (
        slot_disp.reshape(count, 3, elements, 8).transpose(0, 2, 1, 3).reshape(count, elements, 24)
    )
    strain = jnp.einsum("bek,jk->bej", vectors, stiffness, precision=lax.Precision.HIGHEST)
    result = block_modulus[:, :, None] * (strain + hardening * strain * strain * strain)
    return (
        result.reshape(count, elements, 3, 8).transpose(0, 2, 1, 3).reshape(count, 3, elements * 8)
    )


def plain_cycle(init_disp, init_vel, mass, contact, modulus, stiffness, levels, windows, conn):
    region_count = lax.axis_size("region")
    node_region = init_disp.shape[1]
    slot_count = conn.shape[1]
    block_rows = NB
    node_total = node_region * region_count
    impactor_mass = impactor_ratio * node_total
    extended_blocks = node_region // block_rows + 2
    block_order = jnp.argsort(levels, stable=True)
    conn = conn[block_order]
    windows = windows[block_order]
    levels = levels[block_order]
    modulus = modulus[block_order]
    level_slot = (
        (levels >= 2).astype(jnp.int32)
        + (levels >= 4).astype(jnp.int32)
        + (levels >= 8).astype(jnp.int32)
    )
    level_force = jnp.zeros((4, 3, extended_blocks, block_rows), jnp.float32)
    disp_full = init_disp
    disp_state = init_disp
    vel_state = init_vel
    gap_now = jnp.float32(start_gap)
    speed = jnp.float32(start_speed)
    history = []
    slot_iota = lax.broadcasted_iota(jnp.int32, (group_size, 2 * block_rows, slot_count), 1)
    for substep in range(SUBSTEPS):
        top_level = SUBSTEPS if substep == 0 else min(substep & -substep, SUBSTEPS)
        top_index = top_level.bit_length() - 1
        active_count = jnp.sum((levels <= top_level).astype(jnp.int32))
        level_force = level_force.at[: top_index + 1].set(0.0)
        disp_ext = with_halo(disp_full, (("region", 1),), block_rows)

        def one_group(group_index, totals):
            offset = group_index * group_size
            conn_group = lax.dynamic_slice_in_dim(conn, offset, group_size, 0)
            window_group = lax.dynamic_slice_in_dim(windows, offset, group_size, 0)
            level_group = lax.dynamic_slice_in_dim(level_slot, offset, group_size, 0)
            modulus_group = lax.dynamic_slice_in_dim(modulus, offset, group_size, 0)
            valid = offset + jnp.arange(group_size, dtype=jnp.int32) < active_count
            window_disp = jax.vmap(
                lambda first_block: lax.dynamic_slice_in_dim(
                    disp_ext, first_block * block_rows, 2 * block_rows, 1
                )
            )(window_group)
            onehot = (slot_iota == conn_group[:, None, :]).astype(jnp.float32)
            slot_disp = jnp.einsum(
                "gcw,gws->gcs", window_disp, onehot, precision=lax.Precision.HIGHEST
            )
            slot_force = element_forces(slot_disp, modulus_group, stiffness)
            slot_force = jnp.where(valid[:, None, None], slot_force, 0.0)
            window_force = jnp.einsum(
                "gcs,gws->gcw", slot_force, onehot, precision=lax.Precision.HIGHEST
            )
            window_force = window_force.reshape(group_size, 3, 2, block_rows)
            totals = totals.at[level_group, :, window_group].add(window_force[:, :, 0])
            totals = totals.at[level_group, :, window_group + 1].add(window_force[:, :, 1])
            return totals

        group_total = (active_count + group_size - 1) // group_size
        level_force = lax.fori_loop(0, group_total, one_group, level_force)
        force_ext = jnp.sum(level_force, axis=0).reshape(3, extended_blocks * block_rows)
        outer_rims = jnp.concatenate(
            (force_ext[:, :block_rows], force_ext[:, -block_rows:]), axis=1
        )
        rim_terms = with_halo(outer_rims, (("region", 1),), block_rows)
        partial_force = force_ext[:, block_rows:-block_rows]
        partial_force = partial_force.at[:, :block_rows].add(rim_terms[:, :block_rows])
        partial_force = partial_force.at[:, -block_rows:].add(rim_terms[:, -block_rows:])
        force = sum_over(partial_force, "lane")
        disp_state = disp_full
        gap = gap_now - disp_state[0]
        total = sum_over(jnp.sum(contact * gap), "region")
        history.append(total / node_total)
        push = jnp.zeros_like(force).at[0].set(contact_stiffness * contact * gap)
        accel = (push - force) / mass[None, :]
        vel_state = vel_state + time_step * accel
        disp_state = disp_state + time_step * vel_state
        speed = speed - time_step * contact_stiffness * total / impactor_mass
        gap_now = gap_now + time_step * speed
        disp_full = disp_state
    return (disp_full, vel_state, jnp.stack(history))


def on_device(*arguments):
    regions = lax.axis_size("region")
    fast, flag = run_cycle(regions, *arguments)
    return finish(lax.cond(flag == 0, lambda: fast, lambda: plain_cycle(*arguments)))


def solution(mesh):
    in_specs = (
        P(None, "region"),
        P(None, "region"),
        P("region"),
        P("region"),
        P(("region", "lane"), None),
        P(),
        P(("region", "lane")),
        P(("region", "lane")),
        P(("region", "lane"), None),
    )
    out_specs = (P(None, "region"), P(None, "region"), P())
    return jax.shard_map(
        on_device, mesh=mesh, in_specs=in_specs, out_specs=out_specs, check_vma=False
    )
```
